32 devices in a mesh: dp: 8 (over y, x, core), fsdp: 4 (over z).
Axes of the slice: x: 2, y: 2, z: 4, core: 2. Of those that a mesh axis runs over, the one named last changes fastest.
Arguments:
- tokens: bfloat16 [32, 1024, 768], P(('dp', 'fsdp')), may hold values from -6 to 6
- w_qkv: bfloat16 [768, 2304], P(('dp', 'fsdp')), may hold values from -0.21875 to 0.21875
- b_qkv: bfloat16 [2304], P(('dp', 'fsdp')), may hold values from -2 to 2
- conv_kv: bfloat16 [5, 1536], P(None, ('dp', 'fsdp')), may hold values from -0.19921875 to 0.59765625
- w_out: bfloat16 [768, 768], P(None, ('dp', 'fsdp')), may hold values from -1.75 to 1.75
- b_out: bfloat16 [768], P(('dp', 'fsdp')), may hold values from -2 to 2
- gain_one: bfloat16 [768], P(('dp', 'fsdp')), may hold values from 0.5 to 1.5
- shift_one: bfloat16 [768], P(('dp', 'fsdp')), may hold values from -2 to 2
- w_up: bfloat16 [768, 3072], P(('dp', 'fsdp')), may hold values from -0.21875 to 0.21875
- b_up: bfloat16 [3072], P(('dp', 'fsdp')), may hold values from -2 to 2
- w_down: bfloat16 [3072, 768], P(None, ('dp', 'fsdp')), may hold values from -0.109375 to 0.109375
- b_down: bfloat16 [768], P(('dp', 'fsdp')), may hold values from -2 to 2
- gain_two: bfloat16 [768], P(('dp', 'fsdp')), may hold values from 0.5 to 1.5
- shift_two: bfloat16 [768], P(('dp', 'fsdp')), may hold values from -2 to 2
- positions: int32 [32, 160], P(('dp', 'fsdp')), may hold values from 0 to 1024, as said below
- cotangent: bfloat16 [32, 160, 768], P(('dp', 'fsdp')), may hold values from -6 to 6
Outputs:
- layer_out: bfloat16 [32, 1024, 768], P(('dp', 'fsdp'))
- grad_tokens: float32 [32, 1024, 768], P(('dp', 'fsdp'))
- grad_qkv: float32 [768, 2304], P(('dp', 'fsdp'))
- grad_qkvbias: float32 [2304], P(('dp', 'fsdp'))
- grad_conv: float32 [5, 1536], P(None, ('dp', 'fsdp'))
- grad_wout: float32 [768, 768], P(None, ('dp', 'fsdp'))
- grad_bout: float32 [768], P(('dp', 'fsdp'))
- grad_gainone: float32 [768], P(('dp', 'fsdp'))
- grad_shiftone: float32 [768], P(('dp', 'fsdp'))
- grad_wup: float32 [768, 3072], P(('dp', 'fsdp'))
- grad_bup: float32 [3072], P(('dp', 'fsdp'))
- grad_wdown: float32 [3072, 768], P(None, ('dp', 'fsdp'))
- grad_bdown: float32 [768], P(('dp', 'fsdp'))
- grad_gaintwo: float32 [768], P(('dp', 'fsdp'))
- grad_shifttwo: float32 [768], P(('dp', 'fsdp'))
The draws below stay inside these ranges and needn't reach their ends.
Inputs may be any that keep to these rules, and one draw needn't show every extreme that they name: Each row lists distinct token positions of its item in no particular order, followed by the value 1024 in its unused slots; a row holds at least 120 positions, and some row holds 160.
All inputs are finite; a program needn't handle non-finite values.
Results may differ from the reference program's by a relative error of at most 0.013.
Values may be sent and summed in bfloat16 or wider, within the bound.
A program may use at most 256 MiB of HBM per device.

```python
import jax
import jax.numpy as jnp
from jax import lax

D = 768
HEADS = 12
HEAD_DIM = 64
FF = 3072
SEQ = 1024
WIN = 128
POOL_WIN = 512
STRIDE = 4
KERNEL = 5
MASKED = 160
ITEMS = 32


def draw_positions(key, part):
    key = jax.random.fold_in(key, 7)
    count_key, order_key, full_key = jax.random.split(key, 3)
    counts = jax.random.randint(count_key, (ITEMS,), MASKED * 3 // 4, MASKED + 1)
    fullest = jax.random.randint(full_key, (), 0, ITEMS)
    counts = jnp.where(jnp.arange(ITEMS) == fullest, MASKED, counts)
    orders = jax.vmap(lambda item_key: jax.random.permutation(item_key, SEQ)[:MASKED])(jax.random.split(order_key, ITEMS))
    slot_index = jnp.arange(MASKED)
    return jnp.where(slot_index[None, :] < counts[:, None], orders, SEQ).astype(jnp.int32)


def with_spikes(entries, key, source, target, parts, factor):
    owner, partner = [(jnp.arange(entries.shape[dim]) // (entries.shape[dim] // parts)).reshape([-1 if axis == dim else 1 for axis in range(entries.ndim)]) for dim in (source, target)]
    chosen = jax.random.permutation(key, parts)[partner]
    strong = (owner == chosen) | (owner == (partner + parts // 2) % parts)
    return jnp.where(strong, factor * entries, entries)


def block_levels(stream_key, shape, shards, low, top_value):
    level = 1.0
    for position, shards_of in shards:
        heights = jax.random.uniform(jax.random.fold_in(jax.random.fold_in(stream_key, 6), position), (shards_of,), jnp.float32, low / len(shards), top_value / len(shards))
        level = level * jnp.repeat(jnp.exp(heights), shape[position] // shards_of).reshape((-1,) + (1,) * (len(shape) - 1 - position))
    return level


def gaussian(own_key, dims, scale, limit, pieces=(), kind=jnp.bfloat16):
    array = scale * jax.random.normal(own_key, dims, jnp.float32)
    if pieces:
        array = array * block_levels(own_key, dims, pieces, -0.22, 0.18)
    return jnp.clip(array, -limit, limit).astype(kind)


def noise_with(rng, extent, scale, reach, cuts, heavy, kind=jnp.bfloat16):
    values = scale * jax.random.normal(rng, extent, jnp.float32)
    if cuts:
        values = values * block_levels(rng, extent, cuts, -0.22, 0.18)
    return jnp.clip(with_spikes(values, jax.random.fold_in(rng, 3), *heavy), -reach, reach).astype(kind)


def setup_inputs(seed: int = 0) -> dict:
    splits = jax.random.split(jax.random.key(seed), 17)
    tokens = noise_with(splits[0], (ITEMS, SEQ, D), 1.0, 6.0, ((0, 32),), (0, 2, 32, 2.75))
    w_qkv = gaussian(splits[1], (D, 3 * D), D ** -0.5, 0.21875, ((0, 32),))
    b_qkv = gaussian(splits[2], (3 * D,), 0.3, 2.0, ((0, 32),))
    conv_kv = jnp.clip(-0.19921875 + 0.796875 * jax.random.uniform(splits[3], (KERNEL, 2 * D), jnp.float32) ** block_levels(splits[3], (KERNEL, 2 * D), ((1, 32),), -0.2, 0.2), -0.19921875, 0.59765625).astype(jnp.bfloat16)
    w_out = gaussian(splits[4], (D, D), (D // 64) ** -0.5, 1.75, ((1, 32),))
    b_out = gaussian(splits[5], (D,), 0.3, 2.0, ((0, 32),))
    gain_one = jnp.clip(1.0 + 0.1 * jax.random.normal(splits[6], (D,), jnp.float32), 0.5, 1.5).astype(jnp.bfloat16)
    shift_one = gaussian(splits[7], (D,), 0.3, 2.0, ((0, 32),))
    w_up = gaussian(splits[8], (D, FF), D ** -0.5, 0.21875, ((0, 32),))
    b_up = gaussian(splits[9], (FF,), 0.3, 2.0, ((0, 32),))
    w_down = gaussian(splits[10], (FF, D), FF ** -0.5, 0.109375, ((1, 32),))
    b_down = gaussian(splits[11], (D,), 0.3, 2.0, ((0, 32),))
    gain_two = jnp.clip(1.0 + 0.1 * jax.random.normal(splits[12], (D,), jnp.float32), 0.5, 1.5).astype(jnp.bfloat16)
    shift_two = gaussian(splits[13], (D,), 0.3, 2.0, ((0, 32),))
    positions = draw_positions(jax.random.fold_in(splits[16], 71), 0)
    cotangent = noise_with(splits[15], (ITEMS, MASKED, D), 1.0, 6.0, ((0, 32),), (0, 2, 32, 2.75))
    return {"tokens": tokens, "w_qkv": w_qkv, "b_qkv": b_qkv, "conv_kv": conv_kv, "w_out": w_out, "b_out": b_out, "gain_one": gain_one, "shift_one": shift_one, "w_up": w_up, "b_up": b_up, "w_down": w_down, "b_down": b_down, "gain_two": gain_two, "shift_two": shift_two, "positions": positions, "cotangent": cotangent}


@jax.custom_vjp
def low(v):
    return lax.optimization_barrier(v.astype(jnp.bfloat16)).astype(jnp.float32)

@jax.custom_vjp
def low_back(v):
    return v

def low_keep(v):
    return (low(v), None)

def low_pass(kept, grad):
    return (grad,)

def back_keep(v):
    return (v, None)

def back_low(kept, grad):
    return (low(grad),)
low.defvjp(low_keep, low_pass)
low_back.defvjp(back_keep, back_low)

def product(left, right):
    return jnp.dot(left, right, precision=lax.Precision.HIGHEST, preferred_element_type=jnp.float32)

def layer_norm(values, norm_gain, norm_shift):
    average = lax.optimization_barrier(jnp.mean(values, axis=-1, keepdims=True))
    centred = values - average
    variance = lax.optimization_barrier(jnp.mean(centred * centred, axis=-1, keepdims=True))
    return centred * lax.rsqrt(variance + 1e-05) * norm_gain + norm_shift

def window_mask(first_row, block_rows):
    near_half = WIN // 2
    far_half = POOL_WIN // 2
    query_pos = first_row + jnp.arange(block_rows, dtype=jnp.int32)
    key_pos = first_row - near_half + jnp.arange(block_rows + 2 * near_half, dtype=jnp.int32)
    nearby = (jnp.abs(query_pos[:, None] - key_pos[None, :]) <= near_half) & (key_pos[None, :] >= 0) & (key_pos[None, :] < SEQ)
    pool_slot = first_row // STRIDE - far_half // STRIDE + jnp.arange((block_rows + 2 * far_half) // STRIDE, dtype=jnp.int32)
    distant = (jnp.abs(query_pos[:, None] - STRIDE * pool_slot[None, :]) <= far_half) & (pool_slot[None, :] >= 0) & (pool_slot[None, :] < SEQ // STRIDE)
    return jnp.concatenate([nearby, distant], axis=1)

def pool_window(values, taps):
    half_kernel = KERNEL // 2
    padded = jnp.pad(values, ((half_kernel, half_kernel), (0, 0)))
    pool_count = SEQ // STRIDE
    summed = jnp.zeros((pool_count, values.shape[1]), jnp.float32)
    for tap_index in range(KERNEL):
        summed = summed + taps[tap_index] * padded[tap_index:tap_index + STRIDE * pool_count:STRIDE]
    return summed

def attend_block(first_row, queries, kv_pad, pooled_pad):
    block_rows = queries.shape[0]
    near_span = block_rows + 2 * (WIN // 2)
    far_span = (block_rows + 2 * (POOL_WIN // 2)) // STRIDE
    nearby = lax.dynamic_slice_in_dim(kv_pad, first_row, near_span, 0)
    distant = lax.dynamic_slice_in_dim(pooled_pad, first_row // STRIDE, far_span, 0)
    keys_all = jnp.concatenate([nearby[:, :D], distant[:, :D]], 0).reshape(-1, HEADS, HEAD_DIM)
    values_all = jnp.concatenate([nearby[:, D:], distant[:, D:]], 0).reshape(-1, HEADS, HEAD_DIM)
    heads_q = queries.reshape(block_rows, HEADS, HEAD_DIM)
    scores = low_back(jnp.einsum('qhd,khd->hqk', heads_q, keys_all, precision=lax.Precision.HIGHEST) * HEAD_DIM ** (-0.5))
    allowed = window_mask(first_row, block_rows)
    masked = jnp.where(allowed[None], scores, -1e+30)
    row_peak = lax.optimization_barrier(jnp.max(masked, axis=-1, keepdims=True))
    exponent = jnp.exp(masked - row_peak)
    attn_probs = low(exponent / lax.optimization_barrier(jnp.sum(exponent, axis=-1, keepdims=True)))
    context = jnp.einsum('hqk,khd->qhd', attn_probs, values_all, precision=lax.Precision.HIGHEST)
    return context.reshape(block_rows, D)

def sequence_forward(tokens, weights):
    w_qkv, b_qkv, conv_kv, w_out, b_out, gain_one, shift_one, w_up, b_up, w_down, b_down, gain_two, shift_two = weights
    projected = low(low_back(product(tokens, w_qkv) + b_qkv))
    queries = projected[:, :D]
    pooled = low(pool_window(projected[:, D:], conv_kv))
    near_half = WIN // 2
    far_half = POOL_WIN // 2 // STRIDE
    kv_pad = jnp.pad(projected[:, D:], ((near_half, near_half), (0, 0)))
    pooled_pad = jnp.pad(pooled, ((far_half, far_half), (0, 0)))
    block_rows = min(512, SEQ)
    starts = jnp.arange(SEQ // block_rows, dtype=jnp.int32) * block_rows

    def one_block(first_row):
        block_q = lax.dynamic_slice_in_dim(queries, first_row, block_rows, 0)
        return attend_block(first_row, block_q, kv_pad, pooled_pad)
    blocks = lax.map(jax.checkpoint(one_block), starts)
    context = low(low_back(blocks.reshape(SEQ, D)))
    attn_out = low_back(product(context, w_out) + b_out)
    first = low(layer_norm(tokens + attn_out, gain_one, shift_one))
    hidden_pre = low_back(product(first, w_up) + b_up)
    active = low(jax.nn.gelu(hidden_pre))
    branch = low_back(product(active, w_down) + b_down)
    return layer_norm(first + branch, gain_two, shift_two)

def reference(tokens, w_qkv, b_qkv, conv_kv, w_out, b_out, gain_one, shift_one, w_up, b_up, w_down, b_down, gain_two, shift_two, positions, cotangent):
    weights = tuple((member.astype(jnp.float32) for member in (w_qkv, b_qkv, conv_kv, w_out, b_out, gain_one, shift_one, w_up, b_up, w_down, b_down, gain_two, shift_two)))
    inputs = tokens.astype(jnp.float32)

    def forward(inputs, weights):
        return lax.map(lambda sequence: jax.checkpoint(sequence_forward)(sequence, weights), inputs)
    outputs, pullback = jax.vjp(forward, inputs, weights)
    present = positions < SEQ
    clipped = jnp.minimum(positions, SEQ - 1).astype(jnp.int32)
    picked = cotangent.astype(jnp.float32) * present[..., None].astype(jnp.float32)
    dense_cot = jax.vmap(lambda rows_in, index_in: jnp.zeros((SEQ, D), jnp.float32).at[index_in].add(rows_in))(picked, clipped)
    grad_in, grad_weights = pullback(dense_cot)
    return (outputs.astype(jnp.bfloat16), grad_in, grad_weights[0], grad_weights[1], grad_weights[2], grad_weights[3], grad_weights[4], grad_weights[5], grad_weights[6], grad_weights[7], grad_weights[8], grad_weights[9], grad_weights[10], grad_weights[11], grad_weights[12])
```

```python
import functools
import jax
import jax.numpy as jnp
from jax import lax
from jax.experimental import pallas as pl
from jax.experimental.pallas import tpu as pltpu
from jax.sharding import PartitionSpec as P

F32 = jnp.float32
BF = jnp.bfloat16
EPS = 1e-5
NT = (((1,), (1,)), ((), ()))
TN = (((0,), (0,)), ((), ()))


def mm(a, b):
    return jnp.dot(a, b, preferred_element_type=F32)


def mm_nt(a, b):
    return lax.dot_general(a, b, NT, preferred_element_type=F32)


def mm_tn(a, b):
    return lax.dot_general(a, b, TN, preferred_element_type=F32)


def norm_stats(values):
    average = jnp.mean(values, axis=-1, keepdims=True)
    centred = values - average
    variance = jnp.mean(centred * centred, axis=-1, keepdims=True)
    rate = lax.rsqrt(variance + EPS)
    return centred * rate, rate


def norm_back(xhat, rate, gain, dy):
    e = dy * gain
    mean_e = jnp.mean(e, axis=-1, keepdims=True)
    mean_ex = jnp.mean(e * xhat, axis=-1, keepdims=True)
    return rate * (e - mean_e - xhat * mean_ex)


def colsum(v):
    return jnp.sum(v, axis=0, keepdims=True)


def gelu_both(u):
    c = 0.7978845608028654
    u2 = u * u
    t = jnp.tanh(u * (c + (c * 0.044715) * u2))
    half = 0.5 + 0.5 * t
    value = u * half
    slope = half + (0.5 * u) * (1.0 - t * t) * (c + (3.0 * c * 0.044715) * u2)
    return value, slope


def head_split(x, scale):
    lane = lax.broadcasted_iota(jnp.int32, x.shape, 1)
    low = jnp.where(lane < 64, scale, 0.0).astype(BF)
    high = jnp.where(lane < 64, 0.0, scale).astype(BF)
    return jnp.concatenate([x * low, x * high], axis=0)


def head_join(r):
    return jnp.concatenate([r[:64, :128], r[64:, 128:]], axis=0)


def window(b):
    ns = pl.multiple_of(jnp.clip(b * 128 - 64, 0, 1024 - 256), 64)
    ps = pl.multiple_of(jnp.clip(b * 32 - 64, 0, 256 - 160), 32)
    col = b * 128 + (lax.broadcasted_iota(jnp.int32, (256, 256), 1) & 127)
    row = ns + lax.broadcasted_iota(jnp.int32, (256, 256), 0)
    near = jnp.abs(row - col) <= 64
    colp = b * 128 + (lax.broadcasted_iota(jnp.int32, (160, 256), 1) & 127)
    rowp = 4 * (ps + lax.broadcasted_iota(jnp.int32, (160, 256), 0))
    far = jnp.abs(rowp - colp) <= 256
    return ns, ps, near, far


def fwd_group(g, tok, w, bqkv, conv, qkv, pkv, kvf, ctx, lse):
    for r in range(2):
        rows = pl.ds(512 * r, 512)
        low = (mm(tok[rows, :], w[g]) + bqkv[g]).astype(BF)
        qkv[g, rows, :] = low
        for cpart in range(4):
            kvf[cpart, pl.ds(8 + 512 * r, 512), :] = low[:, 256 + 128 * cpart:384 + 128 * cpart].astype(F32)
    for cpart in range(4):
        cols = pl.ds(128 * cpart, 128)
        total = jnp.zeros((256, 128), F32)
        for t in range(5):
            total = total + conv[g, pl.ds(t, 1), cols] * kvf[cpart, pl.ds(6 + t, 256, stride=4), :]
        pkv[g, :, cols] = total.astype(BF)

    def block(b, carry):
        ns, ps, near, far = window(b)
        rows = pl.ds(pl.multiple_of(b * 128, 128), 128)
        for pr in range(2):
            qm = head_split(qkv[g, rows, 128 * pr:128 * pr + 128], 0.125)
            kn = qkv[g, pl.ds(ns, 256), 256 + 128 * pr:384 + 128 * pr]
            kp = pkv[g, pl.ds(ps, 160), 128 * pr:128 * pr + 128]
            sn = jnp.where(near, mm_nt(kn, qm), -1e30)
            sp = jnp.where(far, mm_nt(kp, qm), -1e30)
            peak = jnp.maximum(jnp.max(sn, axis=0, keepdims=True), jnp.max(sp, axis=0, keepdims=True))
            en = jnp.exp(sn - peak)
            ep = jnp.exp(sp - peak)
            total = jnp.sum(en, axis=0, keepdims=True) + jnp.sum(ep, axis=0, keepdims=True)
            vn = qkv[g, pl.ds(ns, 256), 512 + 128 * pr:640 + 128 * pr]
            vp = pkv[g, pl.ds(ps, 160), 256 + 128 * pr:384 + 128 * pr]
            out = mm_tn(vn, en.astype(BF)) + mm_tn(vp, ep.astype(BF))
            out = out * pl.reciprocal(total)
            ctx[rows, 256 * g + 128 * pr:256 * g + 128 * pr + 128] = head_join(out).T.astype(BF)
            lse[(g * 2 + pr) * 8 + b] = peak + jnp.log(total)
        return carry

    lax.fori_loop(0, 8, block, 0)


def fwd_kernel(tok, w, bqkv, conv, vec, bup, pos, cot,
               out, dpre, gff, gsm, gbup, qkv, pkv, ctx, lse,
               kvf, first, act, gp, dh, dbr, tr, stage, sems):
    pre = dpre
    kvf[:, 0:8, :] = jnp.zeros((4, 8, 128), F32)
    kvf[:, 1032:1040, :] = jnp.zeros((4, 8, 128), F32)
    for g in range(3):
        fwd_group(g, tok, w, bqkv, conv, qkv, pkv, kvf, ctx, lse)
    b_out, gain1, shift1, b_down, gain2, shift2 = [vec[pl.ds(i, 1), :] for i in range(6)]
    sums = [jnp.zeros((1, 768), F32) for _ in range(5)]
    gbup[...] = jnp.zeros_like(gbup)
    T = 256
    for tile in range(1024 // T):
        rows = pl.ds(tile * T, T)
        pre_one = tok[rows, :].astype(F32) + mm_nt(ctx[rows, :], w[3]) + b_out
        pre[rows, :] = pre_one
        xhat, rate = norm_stats(pre_one)
        first[rows, :] = (xhat * gain1 + shift1).astype(BF)
    for tile in range(1024 // T):
        rows = pl.ds(tile * T, T)
        fl = first[rows, :]
        acc = fl.astype(F32) + b_down
        for j in range(4):
            value, slope = gelu_both(mm(fl, w[4 + j]) + bup[j])
            low = value.astype(BF)
            act[j, rows, :] = low
            gp[j] = slope
            acc = acc + mm_nt(low, w[8 + j])
        xhat, rate = norm_stats(acc)
        out[rows, :] = (xhat * gain2 + shift2).astype(BF)
        row = tile * T + lax.broadcasted_iota(jnp.int32, (T, 160), 0)
        dy = mm((row == pos[...]).astype(BF), cot[...])
        sums[3] = sums[3] + colsum(dy * xhat)
        sums[4] = sums[4] + colsum(dy)
        dacc = norm_back(xhat, rate, gain2, dy)
        db = dacc.astype(BF)
        dbr[rows, :] = db
        sums[2] = sums[2] + colsum(db.astype(F32))
        for j in range(4):
            low = (mm(db, w[8 + j]) * gp[j]).astype(BF)
            dh[j, rows, :] = low
            gbup[j] += colsum(low.astype(F32))
            dacc = dacc + mm_nt(low, w[4 + j])
        xhat, rate = norm_stats(pre[rows, :])
        sums[0] = sums[0] + colsum(dacc * xhat)
        sums[1] = sums[1] + colsum(dacc)
        dpre[rows, :] = norm_back(xhat, rate, gain1, dacc)
    for i in range(5):
        gsm[pl.ds(i, 1), :] = sums[i]
    sent = [None, None]
    for j in range(8):
        if j % 4 == 0:
            tr[...] = (first if j < 4 else dbr)[...].T
        if sent[j % 2] is not None:
            sent[j % 2].wait()
        stage[j % 2] = mm(tr[...], (dh if j < 4 else act)[j % 4]).astype(BF)
        sent[j % 2] = pltpu.make_async_copy(stage.at[j % 2], gff.at[j], sems.at[j % 2])
        sent[j % 2].start()
    sent[0].wait()
    sent[1].wait()


VM = pl.BlockSpec(memory_space=pltpu.VMEM)


def fwd_call(tok, w, bqkv, conv, vec, bup, pos, cot):
    s = jax.ShapeDtypeStruct
    return pl.pallas_call(
        fwd_kernel,
        in_specs=[VM] * 8,
        out_specs=[VM] * 2 + [pl.BlockSpec(memory_space=pl.ANY)] + [VM] * 6,
        out_shape=[
            s((1024, 768), BF), s((1024, 768), F32), s((8, 768, 768), BF), s((8, 768), F32), s((4, 1, 768), F32),
            s((3, 1024, 768), BF), s((3, 256, 512), BF), s((1024, 768), BF), s((48, 1, 256), F32),
        ],
        scratch_shapes=[
            pltpu.VMEM((4, 1040, 128), F32), pltpu.VMEM((1024, 768), BF),
            pltpu.VMEM((4, 1024, 768), BF), pltpu.VMEM((4, 256, 768), F32), pltpu.VMEM((4, 1024, 768), BF),
            pltpu.VMEM((1024, 768), BF), pltpu.VMEM((768, 1024), BF), pltpu.VMEM((2, 768, 768), BF),
            pltpu.SemaphoreType.DMA((2,)),
        ],
        compiler_params=pltpu.CompilerParams(vmem_limit_bytes=64 * 1024 * 1024 - 1024*512),
        name="forward",
    )(tok, w, bqkv, conv, vec, bup, pos, cot)


def bwd_group(g, tokt, w, conv, qkv, pkv, dctx, lse, kvf, dq, dk, dv, dpk, dpv, dproj, gqkv, gconv, gbias):
    dk[...] = jnp.zeros_like(dk)
    dv[...] = jnp.zeros_like(dv)
    dpk[...] = jnp.zeros_like(dpk)
    dpv[...] = jnp.zeros_like(dpv)

    def block(b, carry):
        ns, ps, near, far = window(b)
        rows = pl.ds(pl.multiple_of(b * 128, 128), 128)
        nr, prow = pl.ds(ns, 256), pl.ds(ps, 160)
        for pr in range(2):
            ln = pl.ds(128 * pr, 128)
            qm = head_split(qkv[g, rows, 128 * pr:128 * pr + 128], 0.125)
            dm = head_split(dctx[rows, 256 * g + 128 * pr:256 * g + 128 * pr + 128], 1.0)
            kn = qkv[g, nr, 256 + 128 * pr:384 + 128 * pr]
            kp = pkv[g, prow, 128 * pr:128 * pr + 128]
            vn = qkv[g, nr, 512 + 128 * pr:640 + 128 * pr]
            vp = pkv[g, prow, 256 + 128 * pr:384 + 128 * pr]
            ls = lse[(g * 2 + pr) * 8 + b]
            pn = jnp.exp(jnp.where(near, mm_nt(kn, qm), -1e30) - ls)
            pp = jnp.exp(jnp.where(far, mm_nt(kp, qm), -1e30) - ls)
            dn = mm_nt(vn, dm)
            dp = mm_nt(vp, dm)
            rd = jnp.sum(pn * dn, axis=0, keepdims=True) + jnp.sum(pp * dp, axis=0, keepdims=True)
            sn = (pn * (dn - rd)).astype(BF)
            sp = (pp * (dp - rd)).astype(BF)
            dk[nr, ln] += mm(sn, qm)
            dpk[prow, ln] += mm(sp, qm)
            dv[nr, ln] += mm(pn.astype(BF), dm)
            dpv[prow, ln] += mm(pp.astype(BF), dm)
            r = mm_tn(kn, sn) + mm_tn(kp, sp)
            dproj[g, rows, ln] = (head_join(r).T * 0.125).astype(BF)
        return carry

    lax.fori_loop(0, 8, block, 0)
    for cpart in range(4):
        kvf[cpart, 8:1032, :] = qkv[g, :, 256 + 128 * cpart:384 + 128 * cpart].astype(F32)
    for cpart in range(4):
        cols = pl.ds(128 * cpart, 128)
        src = dpk if cpart < 2 else dpv
        dst = dk if cpart < 2 else dv
        c2 = pl.ds(128 * (cpart % 2), 128)
        dpool = src[:, c2]
        for t in range(5):
            gconv[g, pl.ds(t, 1), cols] = colsum(dpool * kvf[cpart, pl.ds(6 + t, 256, stride=4), :])
        kvf[cpart, 0:8, :] = jnp.zeros((8, 128), F32)
        kvf[cpart, 1032:1040, :] = jnp.zeros((8, 128), F32)
        kvf[cpart, 8:1032, :] = dst[:, c2]
        for t in range(5):
            at = pl.ds(6 + t, 256, stride=4)
            kvf[cpart, at, :] += conv[g, pl.ds(t, 1), cols] * dpool
        dproj[g, :, 256 + 128 * cpart:384 + 128 * cpart] = kvf[cpart, 8:1032, :].astype(BF)
        kvf[cpart, 0:8, :] = jnp.zeros((8, 128), F32)
        kvf[cpart, 1032:1040, :] = jnp.zeros((8, 128), F32)
    gqkv[g] = mm(tokt[...], dproj[g]).astype(BF)
    gbias[g] = colsum(dproj[g].astype(F32))


def bwd_kernel(tok, w, conv, dpre, qkv, pkv, ctx, lse,
               gtok, gat, gconv, gbias, gbout,
               kvf, dk, dv, dpk, dpv, dctx, dproj, tr):
    kvf[:, 0:8, :] = jnp.zeros((4, 8, 128), F32)
    kvf[:, 1032:1040, :] = jnp.zeros((4, 8, 128), F32)
    da = dpre[...].astype(BF)
    gbout[...] = colsum(da.astype(F32))
    tr[...] = da.T
    for r in range(2):
        rows = pl.ds(512 * r, 512)
        dctx[rows, :] = mm(dpre[rows, :].astype(BF), w[3]).astype(BF)
    gat[3] = mm(tr[...], ctx[...]).astype(BF)
    tr[...] = tok[...].T
    for g in range(3):
        bwd_group(g, tr, w, conv, qkv, pkv, dctx, lse, kvf, None, dk, dv, dpk, dpv, dproj, gat, gconv, gbias)
    for r in range(2):
        rows = pl.ds(512 * r, 512)
        acc = dpre[rows, :]
        for g in range(3):
            acc = acc + mm_nt(dproj[g, rows, :], w[g])
        gtok[rows, :] = acc


def bwd_call(tok, w, conv, dpre, qkv, pkv, ctx, lse):
    s = jax.ShapeDtypeStruct
    return pl.pallas_call(
        bwd_kernel,
        in_specs=[VM] * 8,
        out_specs=[VM] * 5,
        out_shape=[
            s((1024, 768), F32), s((4, 768, 768), BF), s((3, 8, 512), F32), s((3, 1, 768), F32), s((1, 768), F32),
        ],
        scratch_shapes=[
            pltpu.VMEM((4, 1040, 128), F32), pltpu.VMEM((1024, 256), F32), pltpu.VMEM((1024, 256), F32),
            pltpu.VMEM((256, 256), F32), pltpu.VMEM((256, 256), F32), pltpu.VMEM((1024, 768), BF),
            pltpu.VMEM((3, 1024, 768), BF), pltpu.VMEM((768, 1024), BF),
        ],
        compiler_params=pltpu.CompilerParams(vmem_limit_bytes=64 * 1024 * 1024 - 1024*512),
        name="backward",
    )(tok, w, conv, dpre, qkv, pkv, ctx, lse)


AXES = ("dp", "fsdp")


def small_pack(qb, cv, six, ub):
    return jnp.concatenate([qb, cv.reshape(-1)] + six + [ub])


def small_unpack(rows):
    count = rows.shape[0]
    sizes = [2304 // count] + [1536 // count] * 5 + [768 // count] * 6 + [3072 // count]
    at, parts = 0, []
    for size in sizes:
        parts.append(rows[:, at:at + size].reshape(-1))
        at += size
    return parts


def by_group(v, kinds):
    return v.reshape(kinds, 3, 256).transpose(1, 0, 2).reshape(3, 1, kinds * 256)


def shards(tokens, w_qkv, b_qkv, conv_kv, w_out, b_out, gain_one, shift_one, w_up, b_up, w_down, b_down, gain_two,
           shift_two, positions, cotangent):
    rows = w_qkv.shape[0]
    count = 768 // rows
    own = jnp.concatenate([
        w_qkv.reshape(rows, 3, 3, 256).transpose(2, 0, 1, 3).reshape(3, rows, 768),
        w_out.T[None],
        w_up.reshape(rows, 4, 768).transpose(1, 0, 2),
        w_down.reshape(4, 768, rows).transpose(0, 2, 1),
    ], 0)
    w = lax.all_gather(own, AXES, axis=1, tiled=True)
    small = small_pack(b_qkv, conv_kv, [b_out, gain_one, shift_one, b_down, gain_two, shift_two], b_up)
    parts = small_unpack(lax.all_gather(small[None], AXES, axis=0, tiled=True).astype(F32))
    bqkv = by_group(parts[0], 3)
    conv = jnp.concatenate([by_group(p, 2) for p in parts[1:6]] + [jnp.zeros((3, 3, 512), F32)], 1)
    vec = jnp.stack(parts[6:12] + [jnp.zeros((768,), F32)] * 2)
    bup = parts[12].reshape(4, 1, 768)
    out, dpre, gff, gsm, gbup, qkv, pkv, ctx, lse = fwd_call(tokens[0], w, bqkv, conv, vec, bup, positions, cotangent[0])
    gff = lax.psum_scatter(gff, AXES, scatter_dimension=1, tiled=True).astype(F32)
    gtok, gat, gconv, gbias, gbout = bwd_call(tokens[0], w, conv, dpre, qkv, pkv, ctx, lse)
    gat = lax.psum_scatter(gat, AXES, scatter_dimension=1, tiled=True).astype(F32)
    flat = [gbias.reshape(3, 3, 256).transpose(1, 0, 2).reshape(count, -1)]
    flat += [gconv[:, t].reshape(3, 2, 256).transpose(1, 0, 2).reshape(count, -1) for t in range(5)]
    flat += [gbout[0].reshape(count, -1)] + [gsm[i].reshape(count, -1) for i in range(5)] + [gbup.reshape(count, -1)]
    flat = lax.psum_scatter(jnp.concatenate(flat, 1), AXES, scatter_dimension=0, tiled=True)
    s = [p for p in small_unpack_own(flat, count)]
    return (
        out[None], gtok[None],
        gat[:3].reshape(3, rows, 3, 256).transpose(1, 2, 0, 3).reshape(rows, 2304),
        s[0], jnp.stack(s[1:6]), gat[3].T, s[6], s[7], s[8],
        gff[:4].transpose(1, 0, 2).reshape(rows, 3072), s[12],
        gff[4:].transpose(0, 2, 1).reshape(3072, rows), s[9], s[10], s[11],
    )


def small_unpack_own(row, count):
    sizes = [2304 // count] + [1536 // count] * 5 + [768 // count] * 6 + [3072 // count]
    at = 0
    for size in sizes:
        yield row[0, at:at + size]
        at += size


def solution(mesh):
    rows, cols, flat, item = P(AXES, None), P(None, AXES), P(AXES), P(AXES, None, None)
    return jax.shard_map(
        shards,
        mesh=mesh,
        in_specs=(item, rows, flat, cols, cols, flat, flat, flat, rows, flat, cols, flat, flat, flat, rows, item),
        out_specs=(item, item, rows, flat, cols, cols, flat, flat, flat, rows, flat, cols, flat, flat, flat),
        check_vma=False,
    )
```

```python
import functools
import jax
import jax.numpy as jnp
from jax import lax
from jax.experimental import pallas as pl
from jax.experimental.pallas import tpu as pltpu
from jax.sharding import PartitionSpec as P

F32 = jnp.float32
BF = jnp.bfloat16
EPS = 1e-5
NT = (((1,), (1,)), ((), ()))
TN = (((0,), (0,)), ((), ()))
AXES = ("dp", "fsdp")
VM = pl.BlockSpec(memory_space=pltpu.VMEM)
ANY = pl.BlockSpec(memory_space=pl.ANY)
LIMIT = 64 * 1024 * 1024 - 512 * 1024
DMA = pltpu.SemaphoreType.DMA
struct = jax.ShapeDtypeStruct


def mm(a, b):
    return jnp.dot(a, b, preferred_element_type=F32)


def mm_nt(a, b):
    return lax.dot_general(a, b, NT, preferred_element_type=F32)


def mm_tn(a, b):
    return lax.dot_general(a, b, TN, preferred_element_type=F32)


def norm_stats(values):
    average = jnp.mean(values, axis=-1, keepdims=True)
    centred = values - average
    variance = jnp.mean(centred * centred, axis=-1, keepdims=True)
    rate = lax.rsqrt(variance + EPS)
    return centred * rate, rate


def norm_back(xhat, rate, gain, dy):
    e = dy * gain
    mean_e = jnp.mean(e, axis=-1, keepdims=True)
    mean_ex = jnp.mean(e * xhat, axis=-1, keepdims=True)
    return rate * (e - mean_e - xhat * mean_ex)


def colsum(v):
    return jnp.sum(v, axis=0, keepdims=True)


def gelu_both(u):
    c = 0.7978845608028654
    u2 = u * u
    t = jnp.tanh(u * (c + (c * 0.044715) * u2))
    half = 0.5 + 0.5 * t
    value = u * half
    slope = half + (0.5 * u) * (1.0 - t * t) * (c + (3.0 * c * 0.044715) * u2)
    return value, slope


def head_split(x, scale):
    lane = lax.broadcasted_iota(jnp.int32, x.shape, 1)
    low = jnp.where(lane < 64, scale, 0.0).astype(BF)
    high = jnp.where(lane < 64, 0.0, scale).astype(BF)
    return jnp.concatenate([x * low, x * high], axis=0)


def head_join(r):
    return jnp.concatenate([r[:64, :128], r[64:, 128:]], axis=0)


def window(b):
    ns = pl.multiple_of(jnp.clip(b * 128 - 64, 0, 1024 - 256), 64)
    ps = pl.multiple_of(jnp.clip(b * 32 - 64, 0, 256 - 160), 32)
    col = b * 128 + (lax.broadcasted_iota(jnp.int32, (256, 256), 1) & 127)
    row = ns + lax.broadcasted_iota(jnp.int32, (256, 256), 0)
    near = jnp.abs(row - col) <= 64
    colp = b * 128 + (lax.broadcasted_iota(jnp.int32, (160, 256), 1) & 127)
    rowp = 4 * (ps + lax.broadcasted_iota(jnp.int32, (160, 256), 0))
    far = jnp.abs(rowp - colp) <= 256
    return ns, ps, near, far


class Place:
    def __init__(self):
        d = lax.axis_index("dp")
        self.d, self.z = d, lax.axis_index("fsdp")
        self.k, self.x, self.y = lax.rem(d, 2), lax.rem(lax.div(d, 2), 2), lax.div(d, 4)
        self.sib = d + 1 - 2 * self.k
        self.xn = d + 2 - 4 * self.x
        self.yn = d + 4 - 8 * self.y
        self.diag = self.xn + 4 - 8 * self.y

    def up(self, dz):
        return lax.rem(self.z + dz, 4)

    def copy(self, src, dst, send, recv, dp=None, z=None):
        return pltpu.make_async_remote_copy(
            src_ref=src, dst_ref=dst, send_sem=send, recv_sem=recv,
            device_id={"dp": self.d if dp is None else dp, "fsdp": self.z if z is None else z},
            device_id_type=pl.DeviceIdType.MESH)

    def greet(self):
        barrier = pltpu.get_barrier_semaphore()
        for dp in (self.sib, self.xn, self.yn, self.diag):
            pl.semaphore_signal(barrier, inc=1, device_id={"dp": dp, "fsdp": self.z},
                                device_id_type=pl.DeviceIdType.MESH)
        for dz in (1, 2, 3):
            pl.semaphore_signal(barrier, inc=1, device_id={"dp": self.d, "fsdp": self.up(dz)},
                                device_id_type=pl.DeviceIdType.MESH)
        pl.semaphore_wait(barrier, 7)


def slab_of(rows):
    last = jnp.concatenate([rows[..., 16:, :384], rows[..., 16:, 384:]], axis=-2)
    return jnp.concatenate([rows[..., :16, :], last], axis=-1).astype(BF)


def rows_of(slab):
    v = slab.astype(F32)
    last = jnp.concatenate([v[..., :8, 768:], v[..., 8:, 768:]], axis=-1)
    return jnp.concatenate([v[..., :768], last], axis=-2)


class Gather:
    def __init__(self, p, slab, dense, sems):
        self.p, self.slab, self.dense = p, slab, dense
        self.zs, self.zr, self.xs, self.xr, self.ks, self.kr = sems

    def along_z(self, c, dz, arriving=False):
        p = self.p
        slot = p.up(4 - dz) if arriving else p.z
        return p.copy(self.slab.at[c, p.z], self.slab.at[c, slot], self.zs.at[c, dz - 1], self.zr.at[c, dz - 1],
                      z=p.up(dz))

    def first(self, c, arriving=False):
        p, w = self.p, self.dense
        ya = 1 - p.y if arriving else p.y
        xa = 1 - p.x if arriving else p.x
        a, b = pl.ds(0, 384), pl.ds(384, 384)
        return (
            p.copy(w.at[c, p.y, p.x, p.k, :, a], w.at[c, p.y, xa, p.k, :, a], self.xs.at[c, 0], self.xr.at[c, 0], dp=p.xn),
            p.copy(w.at[c, p.y, p.x, p.k, :, b], w.at[c, ya, p.x, p.k, :, b], self.xs.at[c, 1], self.xr.at[c, 1], dp=p.yn),
        )

    def second(self, c, arriving=False):
        p, w = self.p, self.dense
        ya = 1 - p.y if arriving else p.y
        xa = 1 - p.x if arriving else p.x
        a, b = pl.ds(0, 384), pl.ds(384, 384)
        return (
            p.copy(w.at[c, p.y, :, p.k, :, a], w.at[c, ya, :, p.k, :, a], self.xs.at[c, 2], self.xr.at[c, 2], dp=p.yn),
            p.copy(w.at[c, :, p.x, p.k, :, b], w.at[c, :, xa, p.k, :, b], self.xs.at[c, 3], self.xr.at[c, 3], dp=p.xn),
        )

    def across(self, c, arriving=False):
        p, w = self.p, self.dense
        k = 1 - p.k if arriving else p.k
        return p.copy(w.at[c, :, :, p.k], w.at[c, :, :, k], self.ks.at[c], self.kr.at[c], dp=p.sib)

    def s1(self, c):
        for dz in (1, 2, 3):
            self.along_z(c, dz).start()

    def s2(self, c):
        p = self.p
        for dz in (1, 2, 3):
            self.along_z(c, dz, True).wait_recv()
        self.dense[c, p.y, p.x, p.k] = rows_of(self.slab[c]).reshape(96, 768).astype(BF)
        for copy in self.first(c):
            copy.start()

    def s3(self, c):
        for copy in self.first(c, True):
            copy.wait_recv()
        for copy in self.second(c):
            copy.start()

    def s4(self, c):
        for copy in self.second(c, True):
            copy.wait_recv()
        self.across(c).start()

    def s5(self, c):
        self.across(c, True).wait_recv()

    def sent(self, count):
        def one(c, carry):
            for dz in (1, 2, 3):
                self.along_z(c, dz).wait_send()
            for copy in self.first(c) + self.second(c) + (self.across(c),):
                copy.wait_send()
            return carry
        lax.fori_loop(0, count, one, 0)


class SmallGather:
    def __init__(self, p, slab, dense, send, recv):
        self.p, self.slab, self.dense, self.send, self.recv = p, slab, dense, send, recv

    def along_z(self, dz, arriving=False):
        p = self.p
        slot = p.up(4 - dz) if arriving else p.z
        return p.copy(self.slab.at[p.z], self.slab.at[slot], self.send.at[dz - 1], self.recv.at[dz - 1], z=p.up(dz))

    def plane(self, arriving=False):
        p, w = self.p, self.dense
        out = []
        for n, (dp, y, x) in enumerate(((p.xn, p.y, 1 - p.x), (p.yn, 1 - p.y, p.x), (p.diag, 1 - p.y, 1 - p.x))):
            dst = w.at[y, x, p.k] if arriving else w.at[p.y, p.x, p.k]
            out.append(p.copy(w.at[p.y, p.x, p.k], dst, self.send.at[3 + n], self.recv.at[3 + n], dp=dp))
        return out

    def across(self, arriving=False):
        p, w = self.p, self.dense
        k = 1 - p.k if arriving else p.k
        return p.copy(w.at[:, :, p.k], w.at[:, :, k], self.send.at[6], self.recv.at[6], dp=p.sib)

    def s1(self):
        for dz in (1, 2, 3):
            self.along_z(dz).start()

    def s2(self):
        p = self.p
        for dz in (1, 2, 3):
            self.along_z(dz, True).wait_recv()
        self.dense[p.y, p.x, p.k] = self.slab[...]
        for copy in self.plane():
            copy.start()

    def s3(self):
        for copy in self.plane(True):
            copy.wait_recv()
        self.across().start()

    def s4(self):
        self.across(True).wait_recv()

    def sent(self):
        for dz in (1, 2, 3):
            self.along_z(dz).wait_send()
        for copy in self.plane() + [self.across()]:
            copy.wait_send()


class Scatter:
    def __init__(self, p, r0, r1a, r1b, r2, v, r3, fin, sems):
        self.p, self.r0, self.r1a, self.r1b, self.r2, self.v, self.r3, self.fin = p, r0, r1a, r1b, r2, v, r3, fin
        self.ks, self.kr, self.xs, self.xr, self.zs, self.zr = sems

    def across(self, c, src):
        p = self.p
        return p.copy(src.at[:, :, 1 - p.k], self.r0.at[c], self.ks.at[c], self.kr.at[c], dp=p.sib)

    def first(self, c):
        p, r = self.p, self.r0
        return (
            p.copy(r.at[c, :, 1 - p.x, :, pl.ds(0, 384)], self.r1a.at[c], self.xs.at[c, 0], self.xr.at[c, 0], dp=p.xn),
            p.copy(r.at[c, 1 - p.y, :, :, pl.ds(384, 384)], self.r1b.at[c], self.xs.at[c, 1], self.xr.at[c, 1], dp=p.yn),
        )

    def second(self, c):
        p = self.p
        return (
            p.copy(self.r1a.at[c, 1 - p.y], self.r2.at[c, 0], self.xs.at[c, 2], self.xr.at[c, 2], dp=p.yn),
            p.copy(self.r1b.at[c, 1 - p.x], self.r2.at[c, 1], self.xs.at[c, 3], self.xr.at[c, 3], dp=p.xn),
        )

    def along_z(self, c, dz):
        p = self.p
        return p.copy(self.v.at[c, p.up(dz)], self.r3.at[c, dz - 1], self.zs.at[c, dz - 1], self.zr.at[c, dz - 1],
                      z=p.up(dz))

    def s1(self, c, src, own):
        self.across(c, src).wait_recv()
        for a in range(2):
            for b in range(2):
                self.r0[c, a, b] = (self.r0[c, a, b].astype(F32) + own(a, b).astype(F32)).astype(BF)
        for copy in self.first(c):
            copy.start()

    def s2(self, c):
        p = self.p
        for copy in self.first(c):
            copy.wait_recv()
        for a in range(2):
            self.r1a[c, a] = (self.r1a[c, a].astype(F32) + self.r0[c, a, p.x, :, :384].astype(F32)).astype(BF)
            self.r1b[c, a] = (self.r1b[c, a].astype(F32) + self.r0[c, p.y, a, :, 384:].astype(F32)).astype(BF)
        for copy in self.second(c):
            copy.start()

    def s3(self, c):
        p = self.p
        for copy in self.second(c):
            copy.wait_recv()
        left = self.r1a[c, p.y].astype(F32) + self.r2[c, 0].astype(F32)
        right = self.r1b[c, p.x].astype(F32) + self.r2[c, 1].astype(F32)
        self.v[c] = slab_of(jnp.concatenate([left, right], axis=1).reshape(4, 24, 768))
        for dz in (1, 2, 3):
            self.along_z(c, dz).start()

    def s4(self, c):
        for dz in (1, 2, 3):
            self.along_z(c, dz).wait_recv()
        total = rows_of(self.v[c, self.p.z])
        for dz in range(3):
            total = total + rows_of(self.r3[c, dz])
        self.fin[c] = total

    def sent(self, c, src):
        for copy in (self.across(c, src),) + self.first(c) + self.second(c):
            copy.wait_send()
        for dz in (1, 2, 3):
            self.along_z(c, dz).wait_send()


class SmallScatter:
    def __init__(self, p, src, r0, r1, r2, send, recv):
        self.p, self.src, self.r0, self.r1, self.r2, self.send, self.recv = p, src, r0, r1, r2, send, recv

    def across(self):
        p = self.p
        return p.copy(self.src.at[:, :, 1 - p.k], self.r0, self.send.at[0], self.recv.at[0], dp=p.sib)

    def plane(self):
        p = self.p
        return [p.copy(self.r0.at[y, x], self.r1.at[n], self.send.at[1 + n], self.recv.at[1 + n], dp=dp)
                for n, (dp, y, x) in enumerate(((p.xn, p.y, 1 - p.x), (p.yn, 1 - p.y, p.x), (p.diag, 1 - p.y, 1 - p.x)))]

    def along_z(self, dz):
        p = self.p
        return p.copy(self.r0.at[p.y, p.x, pl.ds(pl.multiple_of(24 * p.up(dz), 8), 24)], self.r2.at[dz - 1],
                      self.send.at[3 + dz], self.recv.at[3 + dz], z=p.up(dz))

    def s0(self):
        self.across().start()

    def s1(self):
        p = self.p
        self.across().wait_recv()
        for a in range(2):
            for b in range(2):
                self.r0[a, b] = self.r0[a, b] + self.src[a, b, p.k]
        for copy in self.plane():
            copy.start()

    def s2(self):
        p = self.p
        for copy in self.plane():
            copy.wait_recv()
        self.r0[p.y, p.x] = self.r0[p.y, p.x] + self.r1[0] + self.r1[1] + self.r1[2]
        for dz in (1, 2, 3):
            self.along_z(dz).start()

    def s3(self):
        p = self.p
        for dz in (1, 2, 3):
            self.along_z(dz).wait_recv()
        own = self.r0[p.y, p.x, pl.ds(pl.multiple_of(24 * p.z, 8), 24), :]
        return own + self.r2[0] + self.r2[1] + self.r2[2]

    def sent(self):
        for copy in [self.across()] + self.plane() + [self.along_z(dz) for dz in (1, 2, 3)]:
            copy.wait_send()


def piece_masks(width, total, count):
    lane = lax.broadcasted_iota(jnp.int32, (1, total), 1)
    inside = lax.rem(lane, width)
    place = lax.broadcasted_iota(jnp.int32, (128, total), 0) == inside
    owner = lax.broadcasted_iota(jnp.int32, (count, total), 0) * width == lane - inside
    return place, owner


def unpack_small(pieces, first, number, width, total):
    place, owner = piece_masks(width, total, 32)
    place = place.astype(BF)
    out = []
    for n in range(number):
        spread = mm(pieces[:, first + n, :].astype(BF), place)
        out.append(jnp.sum(jnp.where(owner, spread, 0.0), axis=0, keepdims=True))
    return out


def pack_small(pieces, first, vectors, width, total):
    place, owner = piece_masks(width, total, 32)
    place = place.astype(F32)
    for n, vector in enumerate(vectors):
        spread = jnp.where(owner, vector, 0.0)
        pieces[:, first + n, :] = lax.dot_general(spread, place, NT, precision=lax.Precision.HIGHEST,
                                                  preferred_element_type=F32)


def weight(w, c):
    return w[c].reshape(768, 768)


def lane_block(start):
    return pl.ds(pl.multiple_of(start, 128), 128)


def project_group(g, tok, w, bqkv, conv, qkv, pkv, kvf):
    for r in range(2):
        rows = pl.ds(512 * r, 512)
        low = (mm(tok[rows, :], weight(w, g)) + bqkv[g]).astype(BF)
        qkv[g, rows, :] = low
        for part in range(4):
            kvf[part, pl.ds(8 + 512 * r, 512), :] = low[:, 256 + 128 * part:384 + 128 * part].astype(F32)
    for part in range(4):
        cols = pl.ds(128 * part, 128)
        total = jnp.zeros((256, 128), F32)
        for t in range(5):
            total = total + conv[g, pl.ds(t, 1), cols] * kvf[part, pl.ds(6 + t, 256, stride=4), :]
        pkv[g, :, cols] = total.astype(BF)


def attend_block(g, b, qkv, pkv, ctx, lse):
    ns, ps, near, far = window(b)
    rows = pl.ds(pl.multiple_of(b * 128, 128), 128)
    for pr in range(2):
        qm = head_split(qkv[g, rows, 128 * pr:128 * pr + 128], 0.125)
        kn = qkv[g, pl.ds(ns, 256), 256 + 128 * pr:384 + 128 * pr]
        kp = pkv[g, pl.ds(ps, 160), 128 * pr:128 * pr + 128]
        sn = jnp.where(near, mm_nt(kn, qm), -1e30)
        sp = jnp.where(far, mm_nt(kp, qm), -1e30)
        peak = jnp.maximum(jnp.max(sn, axis=0, keepdims=True), jnp.max(sp, axis=0, keepdims=True))
        en = jnp.exp(sn - peak)
        ep = jnp.exp(sp - peak)
        total = jnp.sum(en, axis=0, keepdims=True) + jnp.sum(ep, axis=0, keepdims=True)
        vn = qkv[g, pl.ds(ns, 256), 512 + 128 * pr:640 + 128 * pr]
        vp = pkv[g, pl.ds(ps, 160), 256 + 128 * pr:384 + 128 * pr]
        out = mm_tn(vn, en.astype(BF)) + mm_tn(vp, ep.astype(BF))
        out = out * pl.reciprocal(total)
        ctx[rows, lane_block(256 * g + 128 * pr)] = head_join(out).T.astype(BF)
        lse[(g * 2 + pr) * 8 + b] = peak + jnp.log(total)


def clear_edges(kvf):
    kvf[:, 0:8, :] = jnp.zeros((4, 8, 128), F32)
    kvf[:, 1032:1040, :] = jnp.zeros((4, 8, 128), F32)


def forward_kernel(comm, *refs):
    if comm:
        (tok, wqkv, bq_own, cv_own, wout, *six, wup, bu_own, wdn, pos, cot,
         out, dpre, gff, gsm, gbup, qkv_out, pkv, ctx, lse, w_out, conv,
         w, buf, act, gp, acc, first, dbr, tr, kvf, stage, sems, csem,
         slab, slab_s, dense_s, pieces, bqkv, vec, bup,
         zs, zr, xs, xr, ks, kr, ss, sr) = refs
    else:
        (tok, w_in, bqkv, conv, vec, bup, pos, cot,
         out, dpre, gff, gsm, gbup, qkv_out, pkv, ctx, lse,
         w, buf, act, gp, acc, first, dbr, tr, kvf, stage, sems, csem) = refs
    pre = dpre
    qkv = buf
    clear_edges(kvf)
    gbup[...] = jnp.zeros_like(gbup)
    todo = []
    if comm:
        p = Place()
        big = Gather(p, slab, w, (zs, zr, xs, xr, ks, kr))
        tiny = SmallGather(p, slab_s, dense_s, ss, sr)
        slab_s[p.z] = jnp.zeros((24, 128), F32)
        slab_s[p.z, 0:1, 0:72] = bq_own[...].astype(F32)
        slab_s[p.z, 1:6, 0:48] = cv_own[...].astype(F32)
        for i in range(6):
            slab_s[p.z, 6 + i:7 + i, 0:24] = six[i][...].astype(F32)
        slab_s[p.z, 12:13, 0:96] = bu_own[...].astype(F32)
        p.greet()
        tiny.s1()
        for c in range(12):
            if c < 3:
                rows24 = jnp.concatenate([wqkv[:, 768 * i + 256 * c:768 * i + 256 * c + 256] for i in range(3)], axis=1)
            elif c == 3:
                rows24 = wout[...].astype(F32).T
            elif c % 2 == 0:
                rows24 = wup[:, 384 * (c - 4):384 * (c - 4) + 768]
            else:
                rows24 = wdn[384 * (c - 5):384 * (c - 5) + 768, :].astype(F32).T
            slab[c, p.z] = slab_of(rows24.astype(F32))
            big.s1(c)
        tiny.s2()
        big.s2(0)
        big.s2(1)
        tiny.s3()
        big.s3(0)
        big.s2(2)
        big.s3(1)
        big.s4(0)
        tiny.s4()
        pieces[...] = dense_s[...].reshape(32, 24, 128)
        whole = unpack_small(pieces, 0, 1, 72, 2304)[0]
        for g in range(3):
            for i in range(3):
                bqkv[g, :, 256 * i:256 * i + 256] = whole[:, 768 * i + 256 * g:768 * i + 256 * g + 256]
        taps = unpack_small(pieces, 1, 5, 48, 1536)
        for t in range(5):
            for g in range(3):
                for i in range(2):
                    conv[g, t:t + 1, 256 * i:256 * i + 256] = taps[t][:, 768 * i + 256 * g:768 * i + 256 * g + 256]
        rest = unpack_small(pieces, 6, 6, 24, 768)
        for i in range(6):
            vec[i:i + 1, :] = rest[i]
        whole = unpack_small(pieces, 12, 1, 96, 3072)[0]
        for j in range(4):
            bup[j] = whole[:, 768 * j:768 * j + 768]
        big.s5(0)
        todo = [(big.s3, 8), (big.s2, 9), (big.s4, 7), (big.s3, 9), (big.s2, 10), (big.s4, 8), (big.s3, 10), (big.s2, 11),
                (big.s4, 9), (big.s3, 11), (big.s4, 10), (big.s4, 11)]
    else:
        load = pltpu.make_async_copy(w_in, w, csem.at[0])
        load.start()
        load.wait()

    def progress(count):
        for _ in range(min(count, len(todo))):
            step, c = todo.pop(0)
            step(c)

    def group(g, carry):
        if comm:
            @pl.when(g > 0)
            def _():
                big.s5(g)
        project_group(g, tok, w, bqkv, conv, qkv, pkv, kvf)

        def block(b, inner):
            attend_block(g, b, qkv, pkv, ctx, lse)
            if comm:
                i = 8 * g + b

                @pl.when(lax.rem(i, 4) == 0)
                def _():
                    n = lax.div(i, 4)
                    big.s3(2 + n)
                    big.s2(3 + n)

                @pl.when(lax.rem(i, 4) == 2)
                def _():
                    big.s4(1 + lax.div(i, 4))
            return inner

        return lax.fori_loop(0, 8, block, carry)

    lax.fori_loop(0, 3, group, 0)
    keep = pltpu.make_async_copy(qkv.at[pl.ds(0, 3)], qkv_out, csem.at[0])
    keep.start()
    if comm:
        big.s5(3)
        keep_w = pltpu.make_async_copy(w.at[pl.ds(0, 4)], w_out, csem.at[1])
        keep_w.start()
    b_out, gain1, shift1, b_down, gain2, shift2 = [vec[pl.ds(i, 1), :] for i in range(6)]
    sums = [jnp.zeros((1, 768), F32) for _ in range(5)]
    tiles = [pl.ds(512 * r, 512) for r in range(2)]
    for rows in tiles:
        pre_one = tok[rows, :].astype(F32) + mm_nt(ctx[rows, :], weight(w, 3)) + b_out
        pre[rows, :] = pre_one
        xhat, rate = norm_stats(pre_one)
        low = (xhat * gain1 + shift1).astype(BF)
        first[rows, :] = low
        acc[rows, :] = low.astype(F32) + b_down
        progress(1)
    for j in range(4):
        if comm:
            big.s5(4 + 2 * j)
            big.s5(5 + 2 * j)
        for rows in tiles:
            value, slope = gelu_both(mm(first[rows, :], weight(w, 4 + 2 * j)) + bup[j])
            low = value.astype(BF)
            act[j, rows, :] = low
            gp[j, rows, :] = slope.astype(BF)
            acc[rows, :] += mm_nt(low, weight(w, 5 + 2 * j))
            progress(3 if j < 3 else 12)
    for r, rows in enumerate(tiles):
        xhat, rate = norm_stats(acc[rows, :])
        out[rows, :] = (xhat * gain2 + shift2).astype(BF)
        row = 512 * r + lax.broadcasted_iota(jnp.int32, (512, 160), 0)
        dy = mm((row == pos[...]).astype(BF), cot[...])
        sums[3] = sums[3] + colsum(dy * xhat)
        sums[4] = sums[4] + colsum(dy)
        dacc = norm_back(xhat, rate, gain2, dy)
        low = dacc.astype(BF)
        dbr[rows, :] = low
        acc[rows, :] = dacc
        sums[2] = sums[2] + colsum(low.astype(F32))
    keep.wait()
    dh = buf
    sent = []

    def emit(n, left, right):
        if n >= 2:
            sent[n - 2].wait()
        stage[n % 2] = mm(left[...], right).astype(BF).reshape(2, 2, 2, 96, 768)
        sent.append(pltpu.make_async_copy(stage.at[n % 2], gff.at[n], sems.at[n % 2]))
        sent[n].start()

    tr[...] = dbr[...].T
    for j in range(4):
        emit(j, tr, act[j])
    tr[...] = first[...].T
    for j in range(4):
        for rows in tiles:
            low = (mm(dbr[rows, :], weight(w, 5 + 2 * j)) * gp[j, rows, :].astype(F32)).astype(BF)
            dh[j, rows, :] = low
            gbup[j] += colsum(low.astype(F32))
            acc[rows, :] += mm_nt(low, weight(w, 4 + 2 * j))
        emit(4 + j, tr, dh[j])
    for rows in tiles:
        xhat, rate = norm_stats(pre[rows, :])
        dacc = acc[rows, :]
        sums[0] = sums[0] + colsum(dacc * xhat)
        sums[1] = sums[1] + colsum(dacc)
        dpre[rows, :] = norm_back(xhat, rate, gain1, dacc)
    for i in range(5):
        gsm[pl.ds(i, 1), :] = sums[i]
    sent[6].wait()
    sent[7].wait()
    if comm:
        keep_w.wait()
        big.sent(12)
        tiny.sent()


def forward_call(comm, *args):
    outs = [
        (struct((1024, 768), BF), VM), (struct((1024, 768), F32), VM), (struct((8, 2, 2, 2, 96, 768), BF), ANY),
        (struct((8, 768), F32), VM), (struct((4, 1, 768), F32), VM), (struct((3, 1024, 768), BF), ANY),
        (struct((3, 256, 512), BF), VM), (struct((1024, 768), BF), VM), (struct((48, 1, 256), F32), VM),
    ]
    scratch = [
        pltpu.VMEM((12, 2, 2, 2, 96, 768), BF), pltpu.VMEM((4, 1024, 768), BF), pltpu.VMEM((4, 1024, 768), BF),
        pltpu.VMEM((4, 1024, 768), BF), pltpu.VMEM((1024, 768), F32), pltpu.VMEM((1024, 768), BF),
        pltpu.VMEM((1024, 768), BF), pltpu.VMEM((768, 1024), BF), pltpu.VMEM((4, 1040, 128), F32),
        pltpu.VMEM((2, 2, 2, 2, 96, 768), BF), DMA((2,)), DMA((2,)),
    ]
    if comm:
        outs += [(struct((4, 2, 2, 2, 96, 768), BF), ANY), (struct((3, 8, 512), F32), VM)]
        scratch += [
            pltpu.VMEM((12, 4, 16, 1152), BF), pltpu.VMEM((4, 24, 128), F32), pltpu.VMEM((2, 2, 2, 4, 24, 128), F32),
            pltpu.VMEM((32, 24, 128), F32), pltpu.VMEM((3, 1, 768), F32), pltpu.VMEM((8, 768), F32),
            pltpu.VMEM((4, 1, 768), F32),
            DMA((12, 3)), DMA((12, 3)), DMA((12, 4)), DMA((12, 4)), DMA((12,)), DMA((12,)), DMA((7,)), DMA((7,)),
        ]
        params = pltpu.CompilerParams(vmem_limit_bytes=LIMIT, collective_id=1, has_side_effects=True)
    else:
        params = pltpu.CompilerParams(vmem_limit_bytes=LIMIT)
    ins = [VM] * len(args)
    if not comm:
        ins[1] = ANY
    return pl.pallas_call(
        functools.partial(forward_kernel, comm), in_specs=ins, out_specs=[o[1] for o in outs],
        out_shape=[o[0] for o in outs], scratch_shapes=scratch, compiler_params=params, name="forward")(*args)


def back_block(g, b, qkv, pkv, dctx, lse, dk, dv, dpk, dpv, dproj):
    ns, ps, near, far = window(b)
    rows = pl.ds(pl.multiple_of(b * 128, 128), 128)
    nr, prow = pl.ds(ns, 256), pl.ds(ps, 160)
    for pr in range(2):
        ln = pl.ds(128 * pr, 128)
        qm = head_split(qkv[g, rows, 128 * pr:128 * pr + 128], 0.125)
        dm = head_split(dctx[rows, lane_block(256 * g + 128 * pr)], 1.0)
        kn = qkv[g, nr, 256 + 128 * pr:384 + 128 * pr]
        kp = pkv[g, prow, 128 * pr:128 * pr + 128]
        vn = qkv[g, nr, 512 + 128 * pr:640 + 128 * pr]
        vp = pkv[g, prow, 256 + 128 * pr:384 + 128 * pr]
        ls = lse[(g * 2 + pr) * 8 + b]
        pn = jnp.exp(jnp.where(near, mm_nt(kn, qm), -1e30) - ls)
        pp = jnp.exp(jnp.where(far, mm_nt(kp, qm), -1e30) - ls)
        dn = mm_nt(vn, dm)
        dp = mm_nt(vp, dm)
        rd = jnp.sum(pn * dn, axis=0, keepdims=True) + jnp.sum(pp * dp, axis=0, keepdims=True)
        sn = (pn * (dn - rd)).astype(BF)
        sp = (pp * (dp - rd)).astype(BF)
        dk[nr, ln] += mm(sn, qm)
        dpk[prow, ln] += mm(sp, qm)
        dv[nr, ln] += mm(pn.astype(BF), dm)
        dpv[prow, ln] += mm(pp.astype(BF), dm)
        r = mm_tn(kn, sn) + mm_tn(kp, sp)
        dproj[g, rows, ln] = (head_join(r).T * 0.125).astype(BF)


def pool_back(g, conv, qkv, kvf, dk, dv, dpk, dpv, dproj, gconv):
    for part in range(4):
        kvf[part, 8:1032, :] = qkv[g, :, 256 + 128 * part:384 + 128 * part].astype(F32)
    for part in range(4):
        cols = pl.ds(128 * part, 128)
        src, dst = (dpk, dk) if part < 2 else (dpv, dv)
        half = pl.ds(128 * (part % 2), 128)
        dpool = src[:, half]
        for t in range(5):
            gconv[g, pl.ds(t, 1), cols] = colsum(dpool * kvf[part, pl.ds(6 + t, 256, stride=4), :])
        kvf[part, 8:1032, :] = dst[:, half]
        for t in range(5):
            at = pl.ds(6 + t, 256, stride=4)
            kvf[part, at, :] += conv[g, pl.ds(t, 1), cols] * dpool
        dproj[g, :, 256 + 128 * part:384 + 128 * part] = kvf[part, 8:1032, :].astype(BF)
        kvf[part, 0:8, :] = jnp.zeros((8, 128), F32)
        kvf[part, 1032:1040, :] = jnp.zeros((8, 128), F32)


def backward_kernel(comm, *refs):
    tok, w, conv, dpre, qkv, pkv, ctx, lse = refs[:8]
    if comm:
        (gff, gsm, gbup, gtok, gqkv, gqb, gcv, gwo, gbo, gg1, gs1, gwu, gbu, gwd, gbd, gg2, gs2,
         kvf, dk, dv, dpk, dpv, dctx, dproj, tr,
         gat, gconv, gbias, gbout, r0, r1a, r1b, r2, v, r3, fin, own, pieces, small, t0, t1, t2,
         ks, kr, xs, xr, zs, zr, ls, ss, sr) = refs[8:]
    else:
        (gtok, gat, gconv, gbias, gbout, kvf, dk, dv, dpk, dpv, dctx, dproj, tr) = refs[8:]
    clear_edges(kvf)
    if comm:
        p = Place()
        big = Scatter(p, r0, r1a, r1b, r2, v, r3, fin, (ks, kr, xs, xr, zs, zr))
        tiny = SmallScatter(p, small, t0, t1, t2, ss, sr)
        p.greet()

        def fetch_ff(c):
            return pltpu.make_async_copy(gff.at[c, :, :, p.k], own.at[lax.rem(c, 2)], ls.at[lax.rem(c, 2)])

        def fetch(c):
            @pl.when(c < 8)
            def _():
                fetch_ff(c).start()

            @pl.when(c == 8)
            def _():
                pltpu.make_async_copy(gat.at[3, :, :, p.k], own.at[lax.rem(c, 2)], ls.at[lax.rem(c, 2)]).start()

            @pl.when(c > 8)
            def _():
                pltpu.make_async_copy(gat.at[lax.max(c - 9, 0), :, :, p.k], own.at[lax.rem(c, 2)], ls.at[lax.rem(c, 2)]).start()

        def start_ff(c, carry):
            big.across(c, gff.at[c]).start()
            return carry

        lax.fori_loop(0, 8, start_ff, 0)
        fetch_ff(0).start()
        fetch_ff(1).start()
    da = dpre[...].astype(BF)
    gbout[...] = colsum(da.astype(F32))
    tr[...] = da.T
    for r in range(2):
        rows = pl.ds(512 * r, 512)
        dctx[rows, :] = mm(dpre[rows, :].astype(BF), weight(w, 3)).astype(BF)
    gat[3] = mm(tr[...], ctx[...]).astype(BF).reshape(2, 2, 2, 96, 768)
    if comm:
        big.across(8, gat.at[3]).start()
    tr[...] = tok[...].T

    def group(g, carry):
        dk[...] = jnp.zeros_like(dk)
        dv[...] = jnp.zeros_like(dv)
        dpk[...] = jnp.zeros_like(dpk)
        dpv[...] = jnp.zeros_like(dpv)

        def block(b, inner):
            if comm:
                i = 8 * g + b
                n = lax.div(i, 2)

                @pl.when((lax.rem(i, 2) == 0) & (n < 11))
                def _():
                    pltpu.make_async_copy(gff.at[0, :, :, p.k], own.at[lax.rem(n, 2)], ls.at[lax.rem(n, 2)]).wait()
                    big.s1(n, gff.at[0], lambda a, b2: own[lax.rem(n, 2), a, b2])
                    pl.when(n < 9)(lambda: fetch(n + 2))

                @pl.when((lax.rem(i, 2) == 1) & (i >= 3))
                def _():
                    big.s2(n - 1)

                @pl.when((lax.rem(i, 2) == 1) & (i >= 5))
                def _():
                    big.s3(n - 2)

                @pl.when((lax.rem(i, 2) == 0) & (i >= 8))
                def _():
                    big.s4(n - 4)
            back_block(g, b, qkv, pkv, dctx, lse, dk, dv, dpk, dpv, dproj)
            return inner

        lax.fori_loop(0, 8, block, 0)
        pool_back(g, conv, qkv, kvf, dk, dv, dpk, dpv, dproj, gconv)
        gat[g] = mm(tr[...], dproj[g]).astype(BF).reshape(2, 2, 2, 96, 768)
        gbias[g] = colsum(dproj[g].astype(F32))
        if comm:
            big.across(9 + g, gat.at[g]).start()
        return carry

    lax.fori_loop(0, 3, group, 0)

    def token_part(n):
        rows = pl.ds(256 * n, 256)
        acc = dpre[rows, :]
        for g in range(3):
            acc = acc + mm_nt(dproj[g, rows, :], weight(w, g))
        gtok[rows, :] = acc

    if not comm:
        for n in range(4):
            token_part(n)
        return

    pieces[...] = jnp.zeros_like(pieces)
    kinds = [jnp.concatenate([gbias[g][:, 256 * i:256 * i + 256] for i in range(3) for g in range(3)], axis=1)]
    pack_small(pieces, 0, kinds, 72, 2304)
    pack_small(pieces, 1, [
        jnp.concatenate([gconv[g, t:t + 1, 256 * i:256 * i + 256] for i in range(2) for g in range(3)], axis=1)
        for t in range(5)], 48, 1536)
    pack_small(pieces, 6, [gbout[...]] + [gsm[i:i + 1, :] for i in range(5)], 24, 768)
    pack_small(pieces, 12, [jnp.concatenate([gbup[j] for j in range(4)], axis=1)], 96, 3072)
    small[...] = pieces[...].reshape(2, 2, 2, 96, 128)
    tiny.s0()
    big.s1(11, gff.at[0], lambda a, b: gat[2, a, b, p.k])
    big.s3(10)
    token_part(0)
    big.s2(11)
    tiny.s1()
    big.s4(8)
    token_part(1)
    big.s3(11)
    tiny.s2()
    big.s4(9)
    token_part(2)
    big.s4(10)
    token_part(3)
    for j in range(4):
        gwd[768 * j:768 * j + 768, :] = fin[j].T
        gwu[:, 768 * j:768 * j + 768] = fin[4 + j]
    gwo[...] = fin[8].T
    total = tiny.s3()
    gqb[...] = total[0:1, 0:72]
    gcv[...] = total[1:6, 0:48]
    for i, ref in enumerate((gbo, gg1, gs1, gbd, gg2, gs2)):
        ref[...] = total[6 + i:7 + i, 0:24]
    gbu[...] = total[12:13, 0:96]
    big.s4(11)
    for g in range(3):
        for i in range(3):
            gqkv[:, 768 * i + 256 * g:768 * i + 256 * g + 256] = fin[9 + g, :, 256 * i:256 * i + 256]

    def drain(c, carry):
        big.sent(c, gff.at[0])
        return carry

    lax.fori_loop(0, 12, drain, 0)
    tiny.sent()


def backward_call(comm, *args):
    scratch = [
        pltpu.VMEM((4, 1040, 128), F32), pltpu.VMEM((1024, 256), F32), pltpu.VMEM((1024, 256), F32),
        pltpu.VMEM((256, 256), F32), pltpu.VMEM((256, 256), F32), pltpu.VMEM((1024, 768), BF),
        pltpu.VMEM((3, 1024, 768), BF), pltpu.VMEM((768, 1024), BF),
    ]
    ins = [VM] * len(args)
    local = [((4, 2, 2, 2, 96, 768), BF), ((3, 8, 512), F32), ((3, 1, 768), F32), ((1, 768), F32)]
    outs = [struct((1024, 768), F32)]
    if comm:
        ins[8] = ANY
        outs += [struct(s, F32) for s in ((24, 2304), (1, 72), (5, 48), (768, 24), (1, 24), (1, 24), (1, 24), (24, 3072), (1, 96),
                                          (3072, 24), (1, 24), (1, 24), (1, 24))]
        scratch += [pltpu.VMEM(*s) for s in local]
        scratch += [
            pltpu.VMEM((12, 2, 2, 96, 768), BF), pltpu.VMEM((12, 2, 96, 384), BF), pltpu.VMEM((12, 2, 96, 384), BF),
            pltpu.VMEM((12, 2, 96, 384), BF), pltpu.VMEM((12, 4, 16, 1152), BF), pltpu.VMEM((12, 3, 16, 1152), BF),
            pltpu.VMEM((12, 24, 768), F32), pltpu.VMEM((2, 2, 2, 96, 768), BF), pltpu.VMEM((32, 24, 128), F32),
            pltpu.VMEM((2, 2, 2, 96, 128), F32), pltpu.VMEM((2, 2, 96, 128), F32), pltpu.VMEM((3, 96, 128), F32),
            pltpu.VMEM((3, 24, 128), F32),
            DMA((12,)), DMA((12,)), DMA((12, 4)), DMA((12, 4)), DMA((12, 3)), DMA((12, 3)), DMA((2,)), DMA((7,)), DMA((7,)),
        ]
        params = pltpu.CompilerParams(vmem_limit_bytes=LIMIT, collective_id=2, has_side_effects=True)
    else:
        outs += [struct(*s) for s in local]
        params = pltpu.CompilerParams(vmem_limit_bytes=LIMIT)
    return pl.pallas_call(
        functools.partial(backward_kernel, comm), in_specs=ins, out_specs=[VM] * len(outs), out_shape=outs,
        scratch_shapes=scratch, compiler_params=params, name="backward")(*args)


def shards_direct(tokens, w_qkv, b_qkv, conv_kv, w_out, b_out, gain_one, shift_one, w_up, b_up, w_down, b_down, gain_two,
                  shift_two, positions, cotangent):
    tok = tokens[0]
    out, dpre, gff, gsm, gbup, qkv, pkv, ctx, lse, w, conv = forward_call(
        True, tok, w_qkv, b_qkv[None], conv_kv, w_out, b_out[None], gain_one[None], shift_one[None], b_down[None],
        gain_two[None], shift_two[None], w_up, b_up[None], w_down, positions, cotangent[0])
    (gtok, gqkv, gqb, gcv, gwo, gbo, gg1, gs1, gwu, gbu, gwd, gbd, gg2, gs2) = backward_call(
        True, tok, w, conv, dpre, qkv, pkv, ctx, lse, gff, gsm, gbup)
    return (out[None], gtok[None], gqkv, gqb[0], gcv, gwo, gbo[0], gg1[0], gs1[0], gwu, gbu[0], gwd, gbd[0], gg2[0], gs2[0])


def small_sizes(count):
    return [2304 // count] + [1536 // count] * 5 + [768 // count] * 6 + [3072 // count]


def by_group(v, kinds):
    return v.reshape(kinds, 3, 256).transpose(1, 0, 2).reshape(3, 1, kinds * 256)


def shards_general(tokens, w_qkv, b_qkv, conv_kv, w_out, b_out, gain_one, shift_one, w_up, b_up, w_down, b_down, gain_two,
                   shift_two, positions, cotangent):
    rows = w_qkv.shape[0]
    count = 768 // rows
    blocks = (2, 2, 2, 96, 768)
    up = w_up.reshape(rows, 4, 768).transpose(1, 0, 2)
    down = w_down.reshape(4, 768, rows).transpose(0, 2, 1)
    own = jnp.concatenate([
        w_qkv.reshape(rows, 3, 3, 256).transpose(2, 0, 1, 3).reshape(3, rows, 768),
        w_out.T[None],
        jnp.stack([up, down], 1).reshape(8, rows, 768),
    ], 0)
    w = lax.all_gather(own, AXES, axis=1, tiled=True).reshape((12,) + blocks)
    small = jnp.concatenate([b_qkv, conv_kv.reshape(-1), b_out, gain_one, shift_one, b_down, gain_two, shift_two, b_up])
    small = lax.all_gather(small[None], AXES, axis=0, tiled=True).astype(F32)
    at, parts = 0, []
    for size in small_sizes(count):
        parts.append(small[:, at:at + size].reshape(-1))
        at += size
    bqkv = by_group(parts[0], 3)
    conv = jnp.concatenate([by_group(p, 2) for p in parts[1:6]] + [jnp.zeros((3, 3, 512), F32)], 1)
    vec = jnp.stack(parts[6:12] + [jnp.zeros((768,), F32)] * 2)
    bup = parts[12].reshape(4, 1, 768)
    out, dpre, gff, gsm, gbup, qkv, pkv, ctx, lse = forward_call(
        False, tokens[0], w, bqkv, conv, vec, bup, positions, cotangent[0])
    gff = lax.psum_scatter(gff.reshape(8, 768, 768), AXES, scatter_dimension=1, tiled=True).astype(F32)
    gtok, gat, gconv, gbias, gbout = backward_call(False, tokens[0], w[:4], conv, dpre, qkv, pkv, ctx, lse)
    gat = lax.psum_scatter(gat.reshape(4, 768, 768), AXES, scatter_dimension=1, tiled=True).astype(F32)
    flat = [gbias.reshape(3, 3, 256).transpose(1, 0, 2).reshape(count, -1)]
    flat += [gconv[:, t].reshape(3, 2, 256).transpose(1, 0, 2).reshape(count, -1) for t in range(5)]
    flat += [gbout[0].reshape(count, -1)] + [gsm[i].reshape(count, -1) for i in range(5)] + [gbup.reshape(count, -1)]
    flat = lax.psum_scatter(jnp.concatenate(flat, 1), AXES, scatter_dimension=0, tiled=True)
    at, s = 0, []
    for size in small_sizes(count):
        s.append(flat[0, at:at + size])
        at += size
    return (
        out[None], gtok[None],
        gat[:3].reshape(3, rows, 3, 256).transpose(1, 2, 0, 3).reshape(rows, 2304),
        s[0], jnp.stack(s[1:6]), gat[3].T, s[6], s[7], s[8],
        gff[4:].transpose(1, 0, 2).reshape(rows, 3072), s[12],
        gff[:4].transpose(0, 2, 1).reshape(3072, rows), s[9], s[10], s[11],
    )


def solution(mesh):
    rows, cols, flat, item = P(AXES, None), P(None, AXES), P(AXES), P(AXES, None, None)
    direct = mesh.shape["dp"] == 8 and mesh.shape["fsdp"] == 4
    return jax.shard_map(
        shards_direct if direct else shards_general,
        mesh=mesh,
        in_specs=(item, rows, flat, cols, cols, flat, flat, flat, rows, flat, cols, flat, flat, flat, rows, item),
        out_specs=(item, item, rows, flat, cols, cols, flat, flat, flat, rows, flat, cols, flat, flat, flat),
        check_vma=False,
    )
```

```python
import functools
import jax
import jax.numpy as jnp
from jax import lax
from jax.experimental import pallas as pl
from jax.experimental.pallas import tpu as pltpu
from jax.sharding import PartitionSpec as P

F32 = jnp.float32
BF = jnp.bfloat16
EPS = 1e-5
NT = (((1,), (1,)), ((), ()))
TN = (((0,), (0,)), ((), ()))
AXES = ("dp", "fsdp")
VM = pl.BlockSpec(memory_space=pltpu.VMEM)
ANY = pl.BlockSpec(memory_space=pl.ANY)
LIMIT = 64 * 1024 * 1024 - 512 * 1024
DMA = pltpu.SemaphoreType.DMA
struct = jax.ShapeDtypeStruct


def mm(a, b):
    return jnp.dot(a, b, preferred_element_type=F32)


def mm_nt(a, b):
    return lax.dot_general(a, b, NT, preferred_element_type=F32)


def mm_tn(a, b):
    return lax.dot_general(a, b, TN, preferred_element_type=F32)


def norm_stats(values):
    average = jnp.mean(values, axis=-1, keepdims=True)
    centred = values - average
    variance = jnp.mean(centred * centred, axis=-1, keepdims=True)
    rate = lax.rsqrt(variance + EPS)
    return centred * rate, rate


def norm_back(xhat, rate, gain, dy):
    e = dy * gain
    mean_e = jnp.mean(e, axis=-1, keepdims=True)
    mean_ex = jnp.mean(e * xhat, axis=-1, keepdims=True)
    return rate * (e - mean_e - xhat * mean_ex)


def colsum(v):
    return jnp.sum(v, axis=0, keepdims=True)


def gelu_both(u):
    c = 0.7978845608028654
    u2 = u * u
    t = jnp.tanh(u * (c + (c * 0.044715) * u2))
    half = 0.5 + 0.5 * t
    value = u * half
    slope = half + (0.5 * u) * (1.0 - t * t) * (c + (3.0 * c * 0.044715) * u2)
    return value, slope


def head_split(x, scale):
    lane = lax.broadcasted_iota(jnp.int32, x.shape, 1)
    low = jnp.where(lane < 64, scale, 0.0).astype(BF)
    high = jnp.where(lane < 64, 0.0, scale).astype(BF)
    return jnp.concatenate([x * low, x * high], axis=0)


def head_join(r):
    return jnp.concatenate([r[:64, :128], r[64:, 128:]], axis=0)


def window(b):
    ns = pl.multiple_of(jnp.clip(b * 128 - 64, 0, 1024 - 256), 64)
    ps = pl.multiple_of(jnp.clip(b * 32 - 64, 0, 256 - 160), 32)
    col = b * 128 + (lax.broadcasted_iota(jnp.int32, (256, 256), 1) & 127)
    row = ns + lax.broadcasted_iota(jnp.int32, (256, 256), 0)
    near = jnp.abs(row - col) <= 64
    colp = b * 128 + (lax.broadcasted_iota(jnp.int32, (160, 256), 1) & 127)
    rowp = 4 * (ps + lax.broadcasted_iota(jnp.int32, (160, 256), 0))
    far = jnp.abs(rowp - colp) <= 256
    return ns, ps, near, far


class Place:
    def __init__(self):
        d = lax.axis_index("dp")
        self.d, self.z = d, lax.axis_index("fsdp")
        self.k, self.x, self.y = lax.rem(d, 2), lax.rem(lax.div(d, 2), 2), lax.div(d, 4)
        self.sib = d + 1 - 2 * self.k
        self.xn = d + 2 - 4 * self.x
        self.yn = d + 4 - 8 * self.y
        self.diag = self.xn + 4 - 8 * self.y

    def up(self, dz):
        return lax.rem(self.z + dz, 4)

    def copy(self, src, dst, send, recv, dp=None, z=None):
        return pltpu.make_async_remote_copy(
            src_ref=src, dst_ref=dst, send_sem=send, recv_sem=recv,
            device_id={"dp": self.d if dp is None else dp, "fsdp": self.z if z is None else z},
            device_id_type=pl.DeviceIdType.MESH)

    def greet(self):
        barrier = pltpu.get_barrier_semaphore()
        for dp in (self.sib, self.xn, self.yn, self.diag):
            pl.semaphore_signal(barrier, inc=1, device_id={"dp": dp, "fsdp": self.z},
                                device_id_type=pl.DeviceIdType.MESH)
        for dz in (1, 2, 3):
            pl.semaphore_signal(barrier, inc=1, device_id={"dp": self.d, "fsdp": self.up(dz)},
                                device_id_type=pl.DeviceIdType.MESH)
        pl.semaphore_wait(barrier, 7)


def slab_of(rows):
    last = jnp.concatenate([rows[..., 16:, :384], rows[..., 16:, 384:]], axis=-2)
    return jnp.concatenate([rows[..., :16, :], last], axis=-1).astype(BF)


def rows_of(slab):
    v = slab.astype(F32)
    last = jnp.concatenate([v[..., :8, 768:], v[..., 8:, 768:]], axis=-1)
    return jnp.concatenate([v[..., :768], last], axis=-2)


class Gather:
    def __init__(self, p, slab, dense, sems):
        self.p, self.slab, self.dense = p, slab, dense
        self.zs, self.zr, self.xs, self.xr, self.ks, self.kr = sems

    def along_z(self, c, dz, arriving=False):
        p = self.p
        slot = p.up(4 - dz) if arriving else p.z
        return p.copy(self.slab.at[c, p.z], self.slab.at[c, slot], self.zs.at[c, dz - 1], self.zr.at[c, dz - 1],
                      z=p.up(dz))

    def first(self, c, arriving=False):
        p, w = self.p, self.dense
        ya = 1 - p.y if arriving else p.y
        xa = 1 - p.x if arriving else p.x
        a, b = pl.ds(0, 384), pl.ds(384, 384)
        return (
            p.copy(w.at[c, p.y, p.x, p.k, :, a], w.at[c, p.y, xa, p.k, :, a], self.xs.at[c, 0], self.xr.at[c, 0], dp=p.xn),
            p.copy(w.at[c, p.y, p.x, p.k, :, b], w.at[c, ya, p.x, p.k, :, b], self.xs.at[c, 1], self.xr.at[c, 1], dp=p.yn),
        )

    def second(self, c, arriving=False):
        p, w = self.p, self.dense
        ya = 1 - p.y if arriving else p.y
        xa = 1 - p.x if arriving else p.x
        a, b = pl.ds(0, 384), pl.ds(384, 384)
        return (
            p.copy(w.at[c, p.y, :, p.k, :, a], w.at[c, ya, :, p.k, :, a], self.xs.at[c, 2], self.xr.at[c, 2], dp=p.yn),
            p.copy(w.at[c, :, p.x, p.k, :, b], w.at[c, :, xa, p.k, :, b], self.xs.at[c, 3], self.xr.at[c, 3], dp=p.xn),
        )

    def across(self, c, arriving=False):
        p, w = self.p, self.dense
        k = 1 - p.k if arriving else p.k
        return p.copy(w.at[c, :, :, p.k], w.at[c, :, :, k], self.ks.at[c], self.kr.at[c], dp=p.sib)

    def s1(self, c):
        for dz in (1, 2, 3):
            self.along_z(c, dz).start()

    def s2(self, c):
        p = self.p
        for dz in (1, 2, 3):
            self.along_z(c, dz, True).wait_recv()
        self.dense[c, p.y, p.x, p.k] = rows_of(self.slab[c]).reshape(96, 768).astype(BF)
        for copy in self.first(c):
            copy.start()

    def s3(self, c):
        for copy in self.first(c, True):
            copy.wait_recv()
        for copy in self.second(c):
            copy.start()

    def s4(self, c):
        for copy in self.second(c, True):
            copy.wait_recv()
        self.across(c).start()

    def s5(self, c):
        self.across(c, True).wait_recv()

    def sent(self, count):
        def one(c, carry):
            for dz in (1, 2, 3):
                self.along_z(c, dz).wait_send()
            for copy in self.first(c) + self.second(c) + (self.across(c),):
                copy.wait_send()
            return carry
        lax.fori_loop(0, count, one, 0)


class SmallGather:
    def __init__(self, p, slab, dense, send, recv):
        self.p, self.slab, self.dense, self.send, self.recv = p, slab, dense, send, recv

    def along_z(self, dz, arriving=False):
        p = self.p
        slot = p.up(4 - dz) if arriving else p.z
        return p.copy(self.slab.at[p.z], self.slab.at[slot], self.send.at[dz - 1], self.recv.at[dz - 1], z=p.up(dz))

    def plane(self, arriving=False):
        p, w = self.p, self.dense
        out = []
        for n, (dp, y, x) in enumerate(((p.xn, p.y, 1 - p.x), (p.yn, 1 - p.y, p.x), (p.diag, 1 - p.y, 1 - p.x))):
            dst = w.at[y, x, p.k] if arriving else w.at[p.y, p.x, p.k]
            out.append(p.copy(w.at[p.y, p.x, p.k], dst, self.send.at[3 + n], self.recv.at[3 + n], dp=dp))
        return out

    def across(self, arriving=False):
        p, w = self.p, self.dense
        k = 1 - p.k if arriving else p.k
        return p.copy(w.at[:, :, p.k], w.at[:, :, k], self.send.at[6], self.recv.at[6], dp=p.sib)

    def s1(self):
        for dz in (1, 2, 3):
            self.along_z(dz).start()

    def s2(self):
        p = self.p
        for dz in (1, 2, 3):
            self.along_z(dz, True).wait_recv()
        self.dense[p.y, p.x, p.k] = self.slab[...]
        for copy in self.plane():
            copy.start()

    def s3(self):
        for copy in self.plane(True):
            copy.wait_recv()
        self.across().start()

    def s4(self):
        self.across(True).wait_recv()

    def sent(self):
        for dz in (1, 2, 3):
            self.along_z(dz).wait_send()
        for copy in self.plane() + [self.across()]:
            copy.wait_send()


class Scatter:
    def __init__(self, p, r0, r1a, r1b, r2, v, r3, fin, sems):
        self.p, self.r0, self.r1a, self.r1b, self.r2, self.v, self.r3, self.fin = p, r0, r1a, r1b, r2, v, r3, fin
        self.ks, self.kr, self.xs, self.xr, self.zs, self.zr = sems

    def across(self, c, src):
        p = self.p
        return p.copy(src.at[:, :, 1 - p.k], self.r0.at[c], self.ks.at[c], self.kr.at[c], dp=p.sib)

    def first(self, c):
        p, r = self.p, self.r0
        return (
            p.copy(r.at[c, :, 1 - p.x, :, pl.ds(0, 384)], self.r1a.at[c], self.xs.at[c, 0], self.xr.at[c, 0], dp=p.xn),
            p.copy(r.at[c, 1 - p.y, :, :, pl.ds(384, 384)], self.r1b.at[c], self.xs.at[c, 1], self.xr.at[c, 1], dp=p.yn),
        )

    def second(self, c):
        p = self.p
        return (
            p.copy(self.r1a.at[c, 1 - p.y], self.r2.at[c, 0], self.xs.at[c, 2], self.xr.at[c, 2], dp=p.yn),
            p.copy(self.r1b.at[c, 1 - p.x], self.r2.at[c, 1], self.xs.at[c, 3], self.xr.at[c, 3], dp=p.xn),
        )

    def along_z(self, c, dz):
        p = self.p
        return p.copy(self.v.at[c, p.up(dz)], self.r3.at[c, dz - 1], self.zs.at[c, dz - 1], self.zr.at[c, dz - 1],
                      z=p.up(dz))

    def s1(self, c, src, own):
        self.across(c, src).wait_recv()
        for a in range(2):
            for b in range(2):
                self.r0[c, a, b] = (self.r0[c, a, b].astype(F32) + own(a, b).astype(F32)).astype(BF)
        for copy in self.first(c):
            copy.start()

    def s2(self, c):
        p = self.p
        for copy in self.first(c):
            copy.wait_recv()
        for a in range(2):
            self.r1a[c, a] = (self.r1a[c, a].astype(F32) + self.r0[c, a, p.x, :, :384].astype(F32)).astype(BF)
            self.r1b[c, a] = (self.r1b[c, a].astype(F32) + self.r0[c, p.y, a, :, 384:].astype(F32)).astype(BF)
        for copy in self.second(c):
            copy.start()

    def s3(self, c):
        p = self.p
        for copy in self.second(c):
            copy.wait_recv()
        left = self.r1a[c, p.y].astype(F32) + self.r2[c, 0].astype(F32)
        right = self.r1b[c, p.x].astype(F32) + self.r2[c, 1].astype(F32)
        self.v[c] = slab_of(jnp.concatenate([left, right], axis=1).reshape(4, 24, 768))
        for dz in (1, 2, 3):
            self.along_z(c, dz).start()

    def s4(self, c):
        for dz in (1, 2, 3):
            self.along_z(c, dz).wait_recv()
        total = rows_of(self.v[c, self.p.z])
        for dz in range(3):
            total = total + rows_of(self.r3[c, dz])
        self.fin[c] = total

    def sent(self, c, src):
        for copy in (self.across(c, src),) + self.first(c) + self.second(c):
            copy.wait_send()
        for dz in (1, 2, 3):
            self.along_z(c, dz).wait_send()


class SmallScatter:
    def __init__(self, p, src, r0, r1, r2, send, recv):
        self.p, self.src, self.r0, self.r1, self.r2, self.send, self.recv = p, src, r0, r1, r2, send, recv

    def across(self):
        p = self.p
        return p.copy(self.src.at[:, :, 1 - p.k], self.r0, self.send.at[0], self.recv.at[0], dp=p.sib)

    def plane(self):
        p = self.p
        return [p.copy(self.r0.at[y, x], self.r1.at[n], self.send.at[1 + n], self.recv.at[1 + n], dp=dp)
                for n, (dp, y, x) in enumerate(((p.xn, p.y, 1 - p.x), (p.yn, 1 - p.y, p.x), (p.diag, 1 - p.y, 1 - p.x)))]

    def along_z(self, dz):
        p = self.p
        return p.copy(self.r0.at[p.y, p.x, pl.ds(pl.multiple_of(24 * p.up(dz), 8), 24)], self.r2.at[dz - 1],
                      self.send.at[3 + dz], self.recv.at[3 + dz], z=p.up(dz))

    def s0(self):
        self.across().start()

    def s1(self):
        p = self.p
        self.across().wait_recv()
        for a in range(2):
            for b in range(2):
                self.r0[a, b] = self.r0[a, b] + self.src[a, b, p.k]
        for copy in self.plane():
            copy.start()

    def s2(self):
        p = self.p
        for copy in self.plane():
            copy.wait_recv()
        self.r0[p.y, p.x] = self.r0[p.y, p.x] + self.r1[0] + self.r1[1] + self.r1[2]
        for dz in (1, 2, 3):
            self.along_z(dz).start()

    def s3(self):
        p = self.p
        for dz in (1, 2, 3):
            self.along_z(dz).wait_recv()
        own = self.r0[p.y, p.x, pl.ds(pl.multiple_of(24 * p.z, 8), 24), :]
        return own + self.r2[0] + self.r2[1] + self.r2[2]

    def sent(self):
        for copy in [self.across()] + self.plane() + [self.along_z(dz) for dz in (1, 2, 3)]:
            copy.wait_send()


def piece_masks(width, total, count):
    lane = lax.broadcasted_iota(jnp.int32, (1, total), 1)
    inside = lax.rem(lane, width)
    place = lax.broadcasted_iota(jnp.int32, (128, total), 0) == inside
    owner = lax.broadcasted_iota(jnp.int32, (count, total), 0) * width == lane - inside
    return place, owner


def unpack_small(pieces, first, number, width, total):
    place, owner = piece_masks(width, total, 32)
    place = place.astype(BF)
    out = []
    for n in range(number):
        spread = mm(pieces[:, first + n, :].astype(BF), place)
        out.append(jnp.sum(jnp.where(owner, spread, 0.0), axis=0, keepdims=True))
    return out


def pack_small(pieces, first, vectors, width, total):
    place, owner = piece_masks(width, total, 32)
    place = place.astype(BF)
    for n, vector in enumerate(vectors):
        high = vector.astype(BF)
        low = (vector - high.astype(F32)).astype(BF)
        both = jnp.concatenate([jnp.where(owner, high.astype(F32), 0.0), jnp.where(owner, low.astype(F32), 0.0)], axis=0)
        both = mm_nt(both.astype(BF), place)
        pieces[:, first + n, :] = both[:32] + both[32:]


def weight(w, c):
    return w[c].reshape(768, 768)


def lane_block(start):
    return pl.ds(pl.multiple_of(start, 128), 128)


def project_group(g, tok, w, bqkv, conv, qkv, pkv, kvf):
    for r in range(2):
        rows = pl.ds(512 * r, 512)
        low = (mm(tok[rows, :], weight(w, g)) + bqkv[g]).astype(BF)
        qkv[g, rows, :] = low
        for part in range(4):
            kvf[part, pl.ds(8 + 512 * r, 512), :] = low[:, 256 + 128 * part:384 + 128 * part].astype(F32)
    for part in range(4):
        cols = pl.ds(128 * part, 128)
        total = jnp.zeros((256, 128), F32)
        for t in range(5):
            total = total + conv[g, pl.ds(t, 1), cols] * kvf[part, pl.ds(6 + t, 256, stride=4), :]
        pkv[g, :, cols] = total.astype(BF)


def attend_block(g, b, qkv, pkv, ctx, lse):
    ns, ps, near, far = window(b)
    rows = pl.ds(pl.multiple_of(b * 128, 128), 128)
    for pr in range(2):
        qm = head_split(qkv[g, rows, 128 * pr:128 * pr + 128], 0.125)
        kn = qkv[g, pl.ds(ns, 256), 256 + 128 * pr:384 + 128 * pr]
        kp = pkv[g, pl.ds(ps, 160), 128 * pr:128 * pr + 128]
        sn = jnp.where(near, mm_nt(kn, qm), -1e30)
        sp = jnp.where(far, mm_nt(kp, qm), -1e30)
        peak = jnp.maximum(jnp.max(sn, axis=0, keepdims=True), jnp.max(sp, axis=0, keepdims=True))
        en = jnp.exp(sn - peak)
        ep = jnp.exp(sp - peak)
        total = jnp.sum(en, axis=0, keepdims=True) + jnp.sum(ep, axis=0, keepdims=True)
        vn = qkv[g, pl.ds(ns, 256), 512 + 128 * pr:640 + 128 * pr]
        vp = pkv[g, pl.ds(ps, 160), 256 + 128 * pr:384 + 128 * pr]
        out = mm_tn(vn, en.astype(BF)) + mm_tn(vp, ep.astype(BF))
        out = out * pl.reciprocal(total)
        ctx[rows, lane_block(256 * g + 128 * pr)] = head_join(out).T.astype(BF)
        lse[(g * 2 + pr) * 8 + b] = peak + jnp.log(total)


def clear_edges(kvf):
    kvf[:, 0:8, :] = jnp.zeros((4, 8, 128), F32)
    kvf[:, 1032:1040, :] = jnp.zeros((4, 8, 128), F32)


def forward_kernel(comm, *refs):
    if comm:
        (tok, wqkv, bq_own, cv_own, wout, *six, wup, bu_own, wdn, pos, cot,
         out_o, pre_o, first_o, acc_o, dbr_o, gp_o, gwd_o, qkv_o, pkv_o, ctx_o, lse_o, gsm, w_o, conv, vec,
         w, buf, act, gp, acc, pre, first, dbr, tr, ctx, pkv, lse, out, kvf, stage, sems, osem,
         slab, slab_s, dense_s, pieces, bqkv, bup,
         zs, zr, xs, xr, ks, kr, ss, sr) = refs
    else:
        (tok, w_in, bqkv, conv, vec, bup, pos, cot,
         out_o, pre_o, first_o, acc_o, dbr_o, gp_o, gwd_o, qkv_o, pkv_o, ctx_o, lse_o, gsm,
         w, buf, act, gp, acc, pre, first, dbr, tr, ctx, pkv, lse, out, kvf, stage, sems, osem) = refs
    qkv = buf
    clear_edges(kvf)
    kept = []

    def keep(src, dst):
        kept.append(pltpu.make_async_copy(src, dst, osem.at[len(kept)]))
        kept[-1].start()

    todo = []
    if comm:
        p = Place()
        big = Gather(p, slab, w, (zs, zr, xs, xr, ks, kr))
        tiny = SmallGather(p, slab_s, dense_s, ss, sr)
        slab_s[p.z] = jnp.zeros((24, 128), F32)
        slab_s[p.z, 0:1, 0:72] = bq_own[...].astype(F32)
        slab_s[p.z, 1:6, 0:48] = cv_own[...].astype(F32)
        for i in range(6):
            slab_s[p.z, 6 + i:7 + i, 0:24] = six[i][...].astype(F32)
        slab_s[p.z, 12:13, 0:96] = bu_own[...].astype(F32)
        for c in range(12):
            if c < 3:
                rows24 = jnp.concatenate([wqkv[:, 768 * i + 256 * c:768 * i + 256 * c + 256] for i in range(3)], axis=1)
            elif c == 3:
                rows24 = wout[...]
            else:
                rows24 = (wup if c % 2 == 0 else wdn)[:, 768 * ((c - 4) // 2):768 * ((c - 4) // 2) + 768]
            slab[c, p.z] = slab_of(rows24.astype(F32))
            if c == 0:
                p.greet()
                tiny.s1()
            big.s1(c)
        tiny.s2()
        big.s2(0)
        big.s2(1)
        tiny.s3()
        big.s3(0)
        big.s2(2)
        big.s3(1)
        big.s2(3)
        big.s4(0)
        tiny.s4()
        pieces[...] = dense_s[...].reshape(32, 24, 128)
        whole = unpack_small(pieces, 0, 1, 72, 2304)[0]
        for g in range(3):
            for i in range(3):
                bqkv[g, :, 256 * i:256 * i + 256] = whole[:, 768 * i + 256 * g:768 * i + 256 * g + 256]
        taps = unpack_small(pieces, 1, 5, 48, 1536)
        for t in range(5):
            for g in range(3):
                for i in range(2):
                    conv[g, t:t + 1, 256 * i:256 * i + 256] = taps[t][:, 768 * i + 256 * g:768 * i + 256 * g + 256]
        rest = unpack_small(pieces, 6, 6, 24, 768)
        for i in range(6):
            vec[i:i + 1, :] = rest[i]
        whole = unpack_small(pieces, 12, 1, 96, 3072)[0]
        for j in range(4):
            bup[j] = whole[:, 768 * j:768 * j + 768]
        big.s5(0)
        todo = [[(big.s2, 10), (big.s3, 8)], [(big.s4, 7), (big.s2, 11)], [(big.s3, 9)], [(big.s4, 8), (big.s3, 10)],
                [(big.s4, 9), (big.s3, 11)], [(big.s4, 10)], [(big.s4, 11)]]
    else:
        load = pltpu.make_async_copy(w_in, w, sems.at[0])
        load.start()
        load.wait()

    def progress():
        for step, c in todo.pop(0) if todo else ():
            step(c)

    def group(g, carry):
        if comm:
            @pl.when(g > 0)
            def _():
                big.s5(g)
        project_group(g, tok, w, bqkv, conv, qkv, pkv, kvf)

        def block(b, inner):
            attend_block(g, b, qkv, pkv, ctx, lse)
            if comm:
                i = 8 * g + b

                @pl.when(lax.rem(i, 4) == 0)
                def _():
                    n = lax.div(i, 4)
                    big.s2(4 + n)
                    big.s3(2 + n)

                @pl.when(lax.rem(i, 4) == 2)
                def _():
                    big.s4(1 + lax.div(i, 4))
            return inner

        return lax.fori_loop(0, 8, block, carry)

    lax.fori_loop(0, 3, group, 0)
    keep(qkv.at[pl.ds(0, 3)], qkv_o)
    keep(pkv, pkv_o)
    keep(ctx, ctx_o)
    keep(lse, lse_o)
    if comm:
        big.s5(3)
        keep(w.at[pl.ds(0, 4)], w_o.at[pl.ds(0, 4)])
    b_out, gain1, shift1, b_down, gain2, shift2 = [vec[pl.ds(i, 1), :] for i in range(6)]
    tiles = [pl.ds(512 * r, 512) for r in range(2)]
    for rows in tiles:
        pre_one = tok[rows, :].astype(F32) + mm_nt(ctx[rows, :], weight(w, 3)) + b_out
        pre[rows, :] = pre_one
        xhat, rate = norm_stats(pre_one)
        low = (xhat * gain1 + shift1).astype(BF)
        first[rows, :] = low
        acc[rows, :] = low.astype(F32) + b_down
        progress()
    keep(pre, pre_o)
    keep(first, first_o)
    for j in range(4):
        if comm:
            big.s5(4 + 2 * j)
            big.s5(5 + 2 * j)
            keep(w.at[pl.ds(4 + 2 * j, 2)], w_o.at[pl.ds(4 + 2 * j, 2)])
        for rows in tiles:
            value, slope = gelu_both(mm(first[rows, :], weight(w, 4 + 2 * j)) + bup[j])
            low = value.astype(BF)
            act[j, rows, :] = low
            gp[j, rows, :] = slope.astype(BF)
            acc[rows, :] += mm_nt(low, weight(w, 5 + 2 * j))
            progress()
        keep(gp.at[j], gp_o.at[j])
    sums = [jnp.zeros((1, 768), F32) for _ in range(3)]
    for r, rows in enumerate(tiles):
        xhat, rate = norm_stats(acc[rows, :])
        out[rows, :] = (xhat * gain2 + shift2).astype(BF)
        row = 512 * r + lax.broadcasted_iota(jnp.int32, (512, 160), 0)
        dy = mm((row == pos[...]).astype(BF), cot[...])
        sums[1] = sums[1] + colsum(dy * xhat)
        sums[2] = sums[2] + colsum(dy)
        dacc = norm_back(xhat, rate, gain2, dy)
        low = dacc.astype(BF)
        dbr[rows, :] = low
        acc[rows, :] = dacc
        sums[0] = sums[0] + colsum(low.astype(F32))
    gsm[...] = jnp.zeros_like(gsm)
    for i in range(3):
        gsm[2 + i:3 + i, :] = sums[i]
    keep(out, out_o)
    keep(dbr, dbr_o)
    keep(acc, acc_o)
    tr[...] = dbr[...].T
    sent = []
    for j in range(4):
        if j >= 2:
            sent[j - 2].wait()
        stage[j % 2] = mm(tr[...], act[j]).astype(BF).reshape(2, 2, 2, 96, 768)
        sent.append(pltpu.make_async_copy(stage.at[j % 2], gwd_o.at[j], sems.at[j % 2]))
        sent[j].start()
    sent[2].wait()
    sent[3].wait()
    for copy in kept:
        copy.wait()
    if comm:
        big.sent(12)
        tiny.sent()


def forward_call(comm, *args):
    outs = [
        (struct((1024, 768), BF), ANY), (struct((1024, 768), F32), ANY), (struct((1024, 768), BF), ANY),
        (struct((1024, 768), F32), ANY), (struct((1024, 768), BF), ANY), (struct((4, 1024, 768), BF), ANY),
        (struct((4, 2, 2, 2, 96, 768), BF), ANY), (struct((3, 1024, 768), BF), ANY), (struct((3, 256, 512), BF), ANY),
        (struct((1024, 768), BF), ANY), (struct((48, 1, 256), F32), ANY), (struct((8, 768), F32), VM),
    ]
    scratch = [
        pltpu.VMEM((12, 2, 2, 2, 96, 768), BF), pltpu.VMEM((3, 1024, 768), BF), pltpu.VMEM((4, 1024, 768), BF),
        pltpu.VMEM((4, 1024, 768), BF), pltpu.VMEM((1024, 768), F32), pltpu.VMEM((1024, 768), F32),
        pltpu.VMEM((1024, 768), BF), pltpu.VMEM((1024, 768), BF), pltpu.VMEM((768, 1024), BF), pltpu.VMEM((1024, 768), BF),
        pltpu.VMEM((3, 256, 512), BF), pltpu.VMEM((48, 1, 256), F32), pltpu.VMEM((1024, 768), BF),
        pltpu.VMEM((4, 1040, 128), F32), pltpu.VMEM((2, 2, 2, 2, 96, 768), BF), DMA((2,)), DMA((20,)),
    ]
    if comm:
        outs += [(struct((12, 2, 2, 2, 96, 768), BF), ANY), (struct((3, 8, 512), F32), VM), (struct((8, 768), F32), VM)]
        scratch += [
            pltpu.VMEM((12, 4, 16, 1152), BF), pltpu.VMEM((4, 24, 128), F32), pltpu.VMEM((2, 2, 2, 4, 24, 128), F32),
            pltpu.VMEM((32, 24, 128), F32), pltpu.VMEM((3, 1, 768), F32), pltpu.VMEM((4, 1, 768), F32),
            DMA((12, 3)), DMA((12, 3)), DMA((12, 4)), DMA((12, 4)), DMA((12,)), DMA((12,)), DMA((7,)), DMA((7,)),
        ]
        params = pltpu.CompilerParams(vmem_limit_bytes=LIMIT, collective_id=1, has_side_effects=True)
    else:
        params = pltpu.CompilerParams(vmem_limit_bytes=LIMIT)
    ins = [VM] * len(args)
    if not comm:
        ins[1] = ANY
    return pl.pallas_call(
        functools.partial(forward_kernel, comm), in_specs=ins, out_specs=[o[1] for o in outs],
        out_shape=[o[0] for o in outs], scratch_shapes=scratch, compiler_params=params, name="forward")(*args)


def qkv_rows(g, start, size):
    return pl.ds(pl.multiple_of(3072 + 1024 * g + start, 32), size)


def back_block(g, b, wb, pkv, buf, lse, dk, dv, dpk, dpv):
    ns, ps, near, far = window(b)
    first_row = pl.multiple_of(b * 128, 128)
    rows = pl.ds(first_row, 128)
    nr, prow = pl.ds(ns, 256), pl.ds(ps, 160)
    qrows, krows = qkv_rows(g, first_row, 128), qkv_rows(g, ns, 256)
    for pr in range(2):
        ln = pl.ds(128 * pr, 128)
        qm = head_split(wb[qrows, 128 * pr:128 * pr + 128], 0.125)
        dm = head_split(buf[3, rows, lane_block(256 * g + 128 * pr)], 1.0)
        kn = wb[krows, 256 + 128 * pr:384 + 128 * pr]
        kp = pkv[g, prow, 128 * pr:128 * pr + 128]
        vn = wb[krows, 512 + 128 * pr:640 + 128 * pr]
        vp = pkv[g, prow, 256 + 128 * pr:384 + 128 * pr]
        ls = lse[(g * 2 + pr) * 8 + b]
        pn = jnp.exp(jnp.where(near, mm_nt(kn, qm), -1e30) - ls)
        pp = jnp.exp(jnp.where(far, mm_nt(kp, qm), -1e30) - ls)
        dn = mm_nt(vn, dm)
        dp = mm_nt(vp, dm)
        rd = jnp.sum(pn * dn, axis=0, keepdims=True) + jnp.sum(pp * dp, axis=0, keepdims=True)
        sn = (pn * (dn - rd)).astype(BF)
        sp = (pp * (dp - rd)).astype(BF)
        dk[nr, ln] += mm(sn, qm)
        dpk[prow, ln] += mm(sp, qm)
        dv[nr, ln] += mm(pn.astype(BF), dm)
        dpv[prow, ln] += mm(pp.astype(BF), dm)
        r = mm_tn(kn, sn) + mm_tn(kp, sp)
        buf[g, rows, ln] = (head_join(r).T * 0.125).astype(BF)


def pool_back(g, conv, wb, kvf, dk, dv, dpk, dpv, buf, gconv):
    for part in range(4):
        kvf[part, 8:1032, :] = wb[qkv_rows(g, 0, 1024), 256 + 128 * part:384 + 128 * part].astype(F32)
    for part in range(4):
        cols = pl.ds(128 * part, 128)
        src, dst = (dpk, dk) if part < 2 else (dpv, dv)
        half = pl.ds(128 * (part % 2), 128)
        dpool = src[:, half]
        for t in range(5):
            gconv[g, pl.ds(t, 1), cols] = colsum(dpool * kvf[part, pl.ds(6 + t, 256, stride=4), :])
        kvf[part, 8:1032, :] = dst[:, half]
        for t in range(5):
            at = pl.ds(6 + t, 256, stride=4)
            kvf[part, at, :] += conv[g, pl.ds(t, 1), cols] * dpool
        buf[g, :, 256 + 128 * part:384 + 128 * part] = kvf[part, 8:1032, :].astype(BF)
        kvf[part, 0:8, :] = jnp.zeros((8, 128), F32)
        kvf[part, 1032:1040, :] = jnp.zeros((8, 128), F32)


BLOCKS = (2, 2, 2, 96, 768)


STEPS = (
    ((1, 0),), (), ((1, 1),), ((2, 0),), ((1, 2),), ((2, 1),), ((3, 0), (1, 3)), ((2, 2),), ((3, 1), (1, 4)),
    ((2, 3),), ((4, 0), (3, 2), (1, 5)), ((2, 4),), ((3, 3), (4, 1), (1, 6), (2, 5)), ((4, 2), (3, 4)), ((4, 3),),
)
LOOP_STEPS = {
    0: ((1, 7),), 1: ((2, 6),), 2: ((3, 5),), 3: ((1, 8),), 4: ((2, 7), (4, 4)), 5: ((3, 6),), 7: ((2, 8),),
    8: ((3, 7), (4, 5)), 9: ((1, 9),), 11: ((3, 8), (4, 6)), 13: ((2, 9), (4, 7)), 16: ((4, 8), (3, 9)), 17: ((1, 10),),
    20: ((2, 10),), 21: ((4, 9),), 23: ((3, 10),),
}


def backward_kernel(comm, *refs):
    (tok_i, w_i, conv, vec, pre_i, first_i, acc_i, dbr_i, gp_i, qkv_i, pkv_i, ctx_i, lse_i, gsm_in) = refs[:14]
    if comm:
        (gwd_i, gtok_o, fin, tot,
         wb, buf, xb, db, tr, acc, gtok, pkv, lse, kvf, dk, dv, dpk, dpv, isem, osem,
         gat, gconv, gbias, gbout, gsm, gbup, r0, r1a, r1b, r2, v, r3, own, pieces, small, t0, t1, t2,
         ks, kr, xs, xr, zs, zr, ls, ss, sr) = refs[14:]
    else:
        (gtok_o, gat, gconv, gbias, gbout, gsm, gbup,
         wb, buf, xb, db, tr, acc, gtok, pkv, lse, kvf, dk, dv, dpk, dpv, isem, osem) = refs[14:]
    loads = {}

    def load(name, src, dst):
        loads[name] = pltpu.make_async_copy(src, dst, isem.at[len(loads)])
        loads[name].start()

    def slot(n):
        return wb[pl.ds(768 * n, 768), :]

    def load_weight(c, n):
        for i in range(8):
            load(("w", c, i), w_i.at[c, i // 4, i // 2 % 2, i % 2], wb.at[pl.ds(768 * n + 96 * i, 96), :])

    def have_weight(c):
        for i in range(8):
            loads["w", c, i].wait()

    load("dbr", dbr_i, db)
    load_weight(5, 1)
    load(("gp", 0), gp_i.at[0], buf.at[0])
    load_weight(4, 0)
    load("acc", acc_i, acc)
    load("first", first_i, xb)
    if comm:
        p = Place()
        big = Scatter(p, r0, r1a, r1b, r2, v, r3, fin, (ks, kr, xs, xr, zs, zr))
        tiny = SmallScatter(p, small, t0, t1, t2, ss, sr)
        p.greet()

        def fetch(c):
            return pltpu.make_async_copy(gwd_i.at[c, :, :, p.k], own.at[c % 2], ls.at[c % 2])

        for c in range(4):
            big.across(c, gwd_i.at[c]).start()
        fetch(0).start()
        fetch(1).start()

        def take(steps):
            for stage, c in steps:
                if stage > 1:
                    (big.s2, big.s3, big.s4)[stage - 2](c)
                elif c >= 4:
                    at = c - 4 if c < 9 else c - 9
                    big.s1(c, gat.at[0], lambda a, b: gat[at, a, b, p.k])
                else:
                    fetch(c).wait()
                    big.s1(c, gat.at[0], lambda a, b: own[c % 2, a, b])
                    if c < 2:
                        fetch(c + 2).start()

    def run(n):
        if comm:
            take(STEPS[n])

    for j in range(1, 4):
        load_weight(5 + 2 * j, 1 + 2 * j)
        load(("gp", j), gp_i.at[j], buf.at[j])
        load_weight(4 + 2 * j, 2 * j)
    load("pre", pre_i, gtok)
    load("pkv", pkv_i, pkv)
    load("lse", lse_i, lse)
    clear_edges(kvf)
    gbup[...] = jnp.zeros_like(gbup)
    gsm[...] = gsm_in[...]
    tiles = [pl.ds(512 * r, 512) for r in range(2)]
    loads["first"].wait()
    tr[...] = xb[...].T
    load("tok", tok_i, xb)
    loads["dbr"].wait()
    for j in range(4):
        have_weight(5 + 2 * j)
        loads["gp", j].wait()
        for r, rows in enumerate(tiles):
            low = (mm(db[rows, :], slot(1 + 2 * j)) * buf[j, rows, :].astype(F32)).astype(BF)
            buf[j, rows, :] = low
            gbup[j] += colsum(low.astype(F32))
            if r == 0:
                have_weight(4 + 2 * j)
                if j == 0:
                    loads["acc"].wait()
            acc[rows, :] += mm_nt(low, slot(2 * j))
            run(3 * j + r)
        gat[j] = mm(tr[...], buf[j]).astype(BF).reshape(BLOCKS)
        if comm:
            big.across(4 + j, gat.at[j]).start()
            run(3 * j + 2)
        if j == 1:
            for c in range(4):
                load_weight(c, c)
    for g in range(3):
        load(("qkv", g), qkv_i.at[g], wb.at[pl.ds(3072 + 1024 * g, 1024), :])
    load("ctx", ctx_i, db)
    loads["pre"].wait()
    gain1 = vec[1:2, :]
    sums = [jnp.zeros((1, 768), F32) for _ in range(3)]
    have_weight(3)
    for rows in tiles:
        xhat, rate = norm_stats(gtok[rows, :])
        dacc = acc[rows, :]
        sums[0] = sums[0] + colsum(dacc * xhat)
        sums[1] = sums[1] + colsum(dacc)
        dpre = norm_back(xhat, rate, gain1, dacc)
        gtok[rows, :] = dpre
        da = dpre.astype(BF)
        sums[2] = sums[2] + colsum(da.astype(F32))
        buf[3, rows, :] = mm(da, slot(3)).astype(BF)
        tr[:, rows] = da.T
    gsm[0:1, :] = sums[0]
    gsm[1:2, :] = sums[1]
    gbout[...] = sums[2]
    if comm:
        run(12)
        pieces[...] = jnp.zeros_like(pieces)
        pack_small(pieces, 6, [gbout[...]] + [gsm[i:i + 1, :] for i in range(5)], 24, 768)
        pack_small(pieces, 12, [jnp.concatenate([gbup[j] for j in range(4)], axis=1)], 96, 3072)
    loads["ctx"].wait()
    gat[4] = mm(tr[...], db[...]).astype(BF).reshape(BLOCKS)
    if comm:
        big.across(8, gat.at[4]).start()
        run(13)
    loads["tok"].wait()
    tr[...] = xb[...].T
    loads["pkv"].wait()
    loads["lse"].wait()
    for g in range(3):
        loads["qkv", g].wait()
        have_weight(g)
    run(14)

    def group(g, carry):
        dk[...] = jnp.zeros_like(dk)
        dv[...] = jnp.zeros_like(dv)
        dpk[...] = jnp.zeros_like(dpk)
        dpv[...] = jnp.zeros_like(dpv)

        def block(b, inner):
            if comm:
                for i, steps in LOOP_STEPS.items():
                    pl.when(8 * g + b == i)(functools.partial(take, steps))
            back_block(g, b, wb, pkv, buf, lse, dk, dv, dpk, dpv)
            return inner

        lax.fori_loop(0, 8, block, 0)
        pool_back(g, conv, wb, kvf, dk, dv, dpk, dpv, buf, gconv)
        if comm:
            big.across(4 + g, gat.at[0]).wait_send()
        gat[g if comm else 5 + g] = mm(tr[...], buf[g]).astype(BF).reshape(BLOCKS)
        if comm:
            big.across(9 + g, gat.at[g]).start()
        gbias[g] = colsum(buf[g].astype(F32))
        return carry

    lax.fori_loop(0, 3, group, 0)
    parts = []

    def token_part(n):
        rows = pl.ds(256 * n, 256)
        total = gtok[rows, :]
        for g in range(3):
            total = total + mm_nt(buf[g, rows, :], slot(g))
        gtok[rows, :] = total
        parts.append(pltpu.make_async_copy(gtok.at[rows, :], gtok_o.at[rows, :], osem.at[n]))
        parts[n].start()

    if not comm:
        for n in range(4):
            token_part(n)
        for copy in parts:
            copy.wait()
        return

    take(((1, 11),))
    kinds = [jnp.concatenate([gbias[g][:, 256 * i:256 * i + 256] for i in range(3) for g in range(3)], axis=1)]
    pack_small(pieces, 0, kinds, 72, 2304)
    pack_small(pieces, 1, [
        jnp.concatenate([gconv[g, t:t + 1, 256 * i:256 * i + 256] for i in range(2) for g in range(3)], axis=1)
        for t in range(5)], 48, 1536)
    small[...] = pieces[...].reshape(2, 2, 2, 96, 128)
    tiny.s0()
    token_part(0)
    tiny.s1()
    take(((2, 11),))
    token_part(1)
    tiny.s2()
    take(((3, 11),))
    token_part(2)
    take(((4, 10),))
    token_part(3)
    tot[...] = tiny.s3()
    take(((4, 11),))
    for c in range(12):
        for copy in big.first(c) + big.second(c) + tuple(big.along_z(c, dz) for dz in (1, 2, 3)):
            copy.wait_send()
        if c not in (4, 5, 6):
            big.across(c, gat.at[0]).wait_send()
    tiny.sent()
    for copy in parts:
        copy.wait()


def backward_call(comm, *args):
    scratch = [
        pltpu.VMEM((6144, 768), BF), pltpu.VMEM((4, 1024, 768), BF), pltpu.VMEM((1024, 768), BF), pltpu.VMEM((1024, 768), BF),
        pltpu.VMEM((768, 1024), BF), pltpu.VMEM((1024, 768), F32), pltpu.VMEM((1024, 768), F32),
        pltpu.VMEM((3, 256, 512), BF), pltpu.VMEM((48, 1, 256), F32),
        pltpu.VMEM((4, 1040, 128), F32), pltpu.VMEM((1024, 256), F32), pltpu.VMEM((1024, 256), F32),
        pltpu.VMEM((256, 256), F32), pltpu.VMEM((256, 256), F32), DMA((120,)), DMA((4,)),
    ]
    ins = [ANY] * len(args)
    for i in (2, 3, 13):
        ins[i] = VM
    local = [((5 if comm else 8,) + BLOCKS, BF), ((3, 8, 512), F32), ((3, 1, 768), F32), ((1, 768), F32), ((8, 768), F32), ((4, 1, 768), F32)]
    outs = [(struct((1024, 768), F32), ANY)]
    if comm:
        outs += [(struct((12, 24, 768), F32), VM), (struct((24, 128), F32), VM)]
        scratch += [pltpu.VMEM(*s) for s in local]
        scratch += [
            pltpu.VMEM((12, 2, 2, 96, 768), BF), pltpu.VMEM((12, 2, 96, 384), BF), pltpu.VMEM((12, 2, 96, 384), BF),
            pltpu.VMEM((12, 2, 96, 384), BF), pltpu.VMEM((12, 4, 16, 1152), BF), pltpu.VMEM((12, 3, 16, 1152), BF),
            pltpu.VMEM((2, 2, 2, 96, 768), BF), pltpu.VMEM((32, 24, 128), F32),
            pltpu.VMEM((2, 2, 2, 96, 128), F32), pltpu.VMEM((2, 2, 96, 128), F32), pltpu.VMEM((3, 96, 128), F32),
            pltpu.VMEM((3, 24, 128), F32),
            DMA((12,)), DMA((12,)), DMA((12, 4)), DMA((12, 4)), DMA((12, 3)), DMA((12, 3)), DMA((2,)), DMA((7,)), DMA((7,)),
        ]
        params = pltpu.CompilerParams(vmem_limit_bytes=LIMIT, collective_id=2, has_side_effects=True)
    else:
        outs += [(struct(*s), VM) for s in local]
        params = pltpu.CompilerParams(vmem_limit_bytes=LIMIT)
    return pl.pallas_call(
        functools.partial(backward_kernel, comm), in_specs=ins, out_specs=[o[1] for o in outs], out_shape=[o[0] for o in outs],
        scratch_shapes=scratch, compiler_params=params, name="backward")(*args)


def finish_kernel(out_i, gtok_i, fin, tot, out, gtok, gqkv, gqb, gcv, gwo, gbo, gg1, gs1, gwu, gbu, gwd, gbd, gg2, gs2):
    out[...] = out_i[...]
    gtok[...] = gtok_i[...]

    @pl.when(pl.program_id(0) == 0)
    def _():
        for j in range(4):
            gwd[:, 768 * j:768 * j + 768] = fin[j]
            gwu[:, 768 * j:768 * j + 768] = fin[4 + j]
        gwo[...] = fin[8]
        for g in range(3):
            for i in range(3):
                gqkv[:, 768 * i + 256 * g:768 * i + 256 * g + 256] = fin[9 + g, :, 256 * i:256 * i + 256]
        gqb[...] = tot[0:1, 0:72]
        gcv[...] = tot[1:6, 0:48]
        for i, ref in enumerate((gbo, gg1, gs1, gbd, gg2, gs2)):
            ref[...] = tot[6 + i:7 + i, 0:24]
        gbu[...] = tot[12:13, 0:96]


def finish_call(*args):
    shapes = ((24, 2304), (1, 72), (5, 48), (24, 768), (1, 24), (1, 24), (1, 24), (24, 3072), (1, 96),
              (24, 3072), (1, 24), (1, 24), (1, 24))
    part = pl.BlockSpec((256, 768), lambda n: (n, 0))

    def full(shape):
        return pl.BlockSpec(shape, lambda n: (0,) * len(shape))

    return pl.pallas_call(
        finish_kernel, grid=(4,), in_specs=[part, part, full((12, 24, 768)), full((24, 128))],
        out_specs=[part, part] + [full(s) for s in shapes],
        out_shape=[struct((1024, 768), BF), struct((1024, 768), F32)] + [struct(s, F32) for s in shapes],
        name="finish")(*args)


def shards_direct(tokens, w_qkv, b_qkv, conv_kv, w_out, b_out, gain_one, shift_one, w_up, b_up, w_down, b_down, gain_two,
                  shift_two, positions, cotangent):
    tok = tokens[0]
    out, pre, first, acc, dbr, gp, gwd, qkv, pkv, ctx, lse, gsm, w, conv, vec = forward_call(
        True, tok, w_qkv, b_qkv[None], conv_kv, w_out.T, b_out[None], gain_one[None], shift_one[None], b_down[None],
        gain_two[None], shift_two[None], w_up, b_up[None], w_down.T, positions, cotangent[0])
    gtok, fin, tot = backward_call(True, tok, w, conv, vec, pre, first, acc, dbr, gp, qkv, pkv, ctx, lse, gsm, gwd)
    (out, gtok, gqkv, gqb, gcv, gwo, gbo, gg1, gs1, gwu, gbu, gwd, gbd, gg2, gs2) = finish_call(out, gtok, fin, tot)
    return (out[None], gtok[None], gqkv, gqb[0], gcv, gwo.T, gbo[0], gg1[0], gs1[0], gwu, gbu[0], gwd.T, gbd[0], gg2[0], gs2[0])


def small_sizes(count):
    return [2304 // count] + [1536 // count] * 5 + [768 // count] * 6 + [3072 // count]


def by_group(v, kinds):
    return v.reshape(kinds, 3, 256).transpose(1, 0, 2).reshape(3, 1, kinds * 256)


def shards_general(tokens, w_qkv, b_qkv, conv_kv, w_out, b_out, gain_one, shift_one, w_up, b_up, w_down, b_down, gain_two,
                   shift_two, positions, cotangent):
    rows = w_qkv.shape[0]
    count = 768 // rows
    blocks = (2, 2, 2, 96, 768)
    up = w_up.reshape(rows, 4, 768).transpose(1, 0, 2)
    down = w_down.reshape(4, 768, rows).transpose(0, 2, 1)
    own = jnp.concatenate([
        w_qkv.reshape(rows, 3, 3, 256).transpose(2, 0, 1, 3).reshape(3, rows, 768),
        w_out.T[None],
        jnp.stack([up, down], 1).reshape(8, rows, 768),
    ], 0)
    w = lax.all_gather(own, AXES, axis=1, tiled=True).reshape((12,) + blocks)
    small = jnp.concatenate([b_qkv, conv_kv.reshape(-1), b_out, gain_one, shift_one, b_down, gain_two, shift_two, b_up])
    small = lax.all_gather(small[None], AXES, axis=0, tiled=True).astype(F32)
    at, parts = 0, []
    for size in small_sizes(count):
        parts.append(small[:, at:at + size].reshape(-1))
        at += size
    bqkv = by_group(parts[0], 3)
    conv = jnp.concatenate([by_group(p, 2) for p in parts[1:6]] + [jnp.zeros((3, 3, 512), F32)], 1)
    vec = jnp.stack(parts[6:12] + [jnp.zeros((768,), F32)] * 2)
    bup = parts[12].reshape(4, 1, 768)
    out, pre, first, acc, dbr, gp, gwd, qkv, pkv, ctx, lse, gsm = forward_call(
        False, tokens[0], w, bqkv, conv, vec, bup, positions, cotangent[0])
    gwd = lax.psum_scatter(gwd.reshape(4, 768, 768), AXES, scatter_dimension=1, tiled=True).astype(F32)
    gtok, gat, gconv, gbias, gbout, gsm, gbup = backward_call(
        False, tokens[0], w, conv, vec, pre, first, acc, dbr, gp, qkv, pkv, ctx, lse, gsm)
    gat = lax.psum_scatter(gat.reshape(8, 768, 768), AXES, scatter_dimension=1, tiled=True).astype(F32)
    flat = [gbias.reshape(3, 3, 256).transpose(1, 0, 2).reshape(count, -1)]
    flat += [gconv[:, t].reshape(3, 2, 256).transpose(1, 0, 2).reshape(count, -1) for t in range(5)]
    flat += [gbout[0].reshape(count, -1)] + [gsm[i].reshape(count, -1) for i in range(5)] + [gbup.reshape(count, -1)]
    flat = lax.psum_scatter(jnp.concatenate(flat, 1), AXES, scatter_dimension=0, tiled=True)
    at, s = 0, []
    for size in small_sizes(count):
        s.append(flat[0, at:at + size])
        at += size
    return (
        out[None], gtok[None],
        gat[5:].reshape(3, rows, 3, 256).transpose(1, 2, 0, 3).reshape(rows, 2304),
        s[0], jnp.stack(s[1:6]), gat[4].T, s[6], s[7], s[8],
        gat[:4].transpose(1, 0, 2).reshape(rows, 3072), s[12],
        gwd.transpose(0, 2, 1).reshape(3072, rows), s[9], s[10], s[11],
    )


def solution(mesh):
    rows, cols, flat, item = P(AXES, None), P(None, AXES), P(AXES), P(AXES, None, None)
    direct = mesh.shape["dp"] == 8 and mesh.shape["fsdp"] == 4
    return jax.shard_map(
        shards_direct if direct else shards_general,
        mesh=mesh,
        in_specs=(item, rows, flat, cols, cols, flat, flat, flat, rows, flat, cols, flat, flat, flat, rows, item),
        out_specs=(item, item, rows, flat, cols, cols, flat, flat, flat, rows, flat, cols, flat, flat, flat),
        check_vma=False,
    )
```

```python
import functools
import jax
import jax.numpy as jnp
from jax import lax
from jax.experimental import pallas as pl
from jax.experimental.pallas import tpu as pltpu
from jax.sharding import PartitionSpec as P

F32 = jnp.float32
BF = jnp.bfloat16
EPS = 1e-5
NT = (((1,), (1,)), ((), ()))
TN = (((0,), (0,)), ((), ()))
AXES = ("dp", "fsdp")
VM = pl.BlockSpec(memory_space=pltpu.VMEM)
ANY = pl.BlockSpec(memory_space=pl.ANY)
LIMIT = 64 * 1024 * 1024 - 512 * 1024
DMA = pltpu.SemaphoreType.DMA
struct = jax.ShapeDtypeStruct


def mm(a, b):
    return jnp.dot(a, b, preferred_element_type=F32)


def mm_nt(a, b):
    return lax.dot_general(a, b, NT, preferred_element_type=F32)


def mm_tn(a, b):
    return lax.dot_general(a, b, TN, preferred_element_type=F32)


def norm_stats(values):
    average = jnp.mean(values, axis=-1, keepdims=True)
    centred = values - average
    variance = jnp.mean(centred * centred, axis=-1, keepdims=True)
    rate = lax.rsqrt(variance + EPS)
    return centred * rate, rate


def norm_back(xhat, rate, gain, dy):
    e = dy * gain
    mean_e = jnp.mean(e, axis=-1, keepdims=True)
    mean_ex = jnp.mean(e * xhat, axis=-1, keepdims=True)
    return rate * (e - mean_e - xhat * mean_ex)


def colsum(v):
    return jnp.sum(v, axis=0, keepdims=True)


def gelu_both(u):
    c = 0.7978845608028654
    u2 = u * u
    t = jnp.tanh(u * (c + (c * 0.044715) * u2))
    half = 0.5 + 0.5 * t
    value = u * half
    slope = half + (0.5 * u) * (1.0 - t * t) * (c + (3.0 * c * 0.044715) * u2)
    return value, slope


def head_split(x, scale):
    lane = lax.broadcasted_iota(jnp.int32, x.shape, 1)
    low = jnp.where(lane < 64, scale, 0.0).astype(BF)
    high = jnp.where(lane < 64, 0.0, scale).astype(BF)
    return jnp.concatenate([x * low, x * high], axis=0)


def head_join(r):
    return jnp.concatenate([r[:64, :128], r[64:, 128:]], axis=0)


def window(b):
    ns = pl.multiple_of(jnp.clip(b * 128 - 64, 0, 1024 - 256), 64)
    ps = pl.multiple_of(jnp.clip(b * 32 - 64, 0, 256 - 160), 32)
    col = b * 128 + (lax.broadcasted_iota(jnp.int32, (256, 256), 1) & 127)
    row = ns + lax.broadcasted_iota(jnp.int32, (256, 256), 0)
    near = jnp.abs(row - col) <= 64
    colp = b * 128 + (lax.broadcasted_iota(jnp.int32, (160, 256), 1) & 127)
    rowp = 4 * (ps + lax.broadcasted_iota(jnp.int32, (160, 256), 0))
    far = jnp.abs(rowp - colp) <= 256
    return ns, ps, near, far


class Place:
    def __init__(self):
        d = lax.axis_index("dp")
        self.d, self.z = d, lax.axis_index("fsdp")
        self.k, self.x, self.y = lax.rem(d, 2), lax.rem(lax.div(d, 2), 2), lax.div(d, 4)
        self.sib = d + 1 - 2 * self.k
        self.xn = d + 2 - 4 * self.x
        self.yn = d + 4 - 8 * self.y
        self.diag = self.xn + 4 - 8 * self.y

    def up(self, dz):
        return lax.rem(self.z + dz, 4)

    def copy(self, src, dst, send, recv, dp=None, z=None):
        return pltpu.make_async_remote_copy(
            src_ref=src, dst_ref=dst, send_sem=send, recv_sem=recv,
            device_id={"dp": self.d if dp is None else dp, "fsdp": self.z if z is None else z},
            device_id_type=pl.DeviceIdType.MESH)

    def greet(self):
        barrier = pltpu.get_barrier_semaphore()
        for dp in (self.sib, self.xn, self.yn, self.diag):
            pl.semaphore_signal(barrier, inc=1, device_id={"dp": dp, "fsdp": self.z},
                                device_id_type=pl.DeviceIdType.MESH)
        for dz in (1, 2, 3):
            pl.semaphore_signal(barrier, inc=1, device_id={"dp": self.d, "fsdp": self.up(dz)},
                                device_id_type=pl.DeviceIdType.MESH)
        pl.semaphore_wait(barrier, 7)


def slab_of(rows):
    last = jnp.concatenate([rows[..., 16:, :384], rows[..., 16:, 384:]], axis=-2)
    return jnp.concatenate([rows[..., :16, :], last], axis=-1).astype(BF)


def rows_of(slab):
    v = slab.astype(F32)
    last = jnp.concatenate([v[..., :8, 768:], v[..., 8:, 768:]], axis=-1)
    return jnp.concatenate([v[..., :768], last], axis=-2)


class Gather:
    def __init__(self, p, slab, dense, sems):
        self.p, self.slab, self.dense = p, slab, dense
        self.zs, self.zr, self.xs, self.xr, self.ks, self.kr = sems

    def along_z(self, c, dz, arriving=False):
        p = self.p
        slot = p.up(4 - dz) if arriving else p.z
        return p.copy(self.slab.at[c, p.z], self.slab.at[c, slot], self.zs.at[c, dz - 1], self.zr.at[c, dz - 1],
                      z=p.up(dz))

    def first(self, c, arriving=False):
        p, w = self.p, self.dense
        ya = 1 - p.y if arriving else p.y
        xa = 1 - p.x if arriving else p.x
        a, b = pl.ds(0, 384), pl.ds(384, 384)
        return (
            p.copy(w.at[c, p.y, p.x, p.k, :, a], w.at[c, p.y, xa, p.k, :, a], self.xs.at[c, 0], self.xr.at[c, 0], dp=p.xn),
            p.copy(w.at[c, p.y, p.x, p.k, :, b], w.at[c, ya, p.x, p.k, :, b], self.xs.at[c, 1], self.xr.at[c, 1], dp=p.yn),
        )

    def second(self, c, arriving=False):
        p, w = self.p, self.dense
        ya = 1 - p.y if arriving else p.y
        xa = 1 - p.x if arriving else p.x
        a, b = pl.ds(0, 384), pl.ds(384, 384)
        return (
            p.copy(w.at[c, p.y, :, p.k, :, a], w.at[c, ya, :, p.k, :, a], self.xs.at[c, 2], self.xr.at[c, 2], dp=p.yn),
            p.copy(w.at[c, :, p.x, p.k, :, b], w.at[c, :, xa, p.k, :, b], self.xs.at[c, 3], self.xr.at[c, 3], dp=p.xn),
        )

    def across(self, c, arriving=False):
        p, w = self.p, self.dense
        k = 1 - p.k if arriving else p.k
        return p.copy(w.at[c, :, :, p.k], w.at[c, :, :, k], self.ks.at[c], self.kr.at[c], dp=p.sib)

    def s1(self, c):
        for dz in (1, 2, 3):
            self.along_z(c, dz).start()

    def s2(self, c):
        p = self.p
        for dz in (1, 2, 3):
            self.along_z(c, dz, True).wait_recv()
        self.dense[c, p.y, p.x, p.k] = rows_of(self.slab[c]).reshape(96, 768).astype(BF)
        for copy in self.first(c):
            copy.start()

    def s3(self, c):
        for copy in self.first(c, True):
            copy.wait_recv()
        for copy in self.second(c):
            copy.start()

    def s4(self, c):
        for copy in self.second(c, True):
            copy.wait_recv()
        self.across(c).start()

    def s5(self, c):
        self.across(c, True).wait_recv()

    def sent(self, count):
        def one(c, carry):
            for dz in (1, 2, 3):
                self.along_z(c, dz).wait_send()
            for copy in self.first(c) + self.second(c) + (self.across(c),):
                copy.wait_send()
            return carry
        lax.fori_loop(0, count, one, 0)


class SmallGather:
    def __init__(self, p, slab, dense, send, recv):
        self.p, self.slab, self.dense, self.send, self.recv = p, slab, dense, send, recv

    def along_z(self, dz, arriving=False):
        p = self.p
        slot = p.up(4 - dz) if arriving else p.z
        return p.copy(self.slab.at[p.z], self.slab.at[slot], self.send.at[dz - 1], self.recv.at[dz - 1], z=p.up(dz))

    def plane(self, arriving=False):
        p, w = self.p, self.dense
        out = []
        for n, (dp, y, x) in enumerate(((p.xn, p.y, 1 - p.x), (p.yn, 1 - p.y, p.x), (p.diag, 1 - p.y, 1 - p.x))):
            dst = w.at[y, x, p.k] if arriving else w.at[p.y, p.x, p.k]
            out.append(p.copy(w.at[p.y, p.x, p.k], dst, self.send.at[3 + n], self.recv.at[3 + n], dp=dp))
        return out

    def across(self, arriving=False):
        p, w = self.p, self.dense
        k = 1 - p.k if arriving else p.k
        return p.copy(w.at[:, :, p.k], w.at[:, :, k], self.send.at[6], self.recv.at[6], dp=p.sib)

    def s1(self):
        for dz in (1, 2, 3):
            self.along_z(dz).start()

    def s2(self):
        p = self.p
        for dz in (1, 2, 3):
            self.along_z(dz, True).wait_recv()
        self.dense[p.y, p.x, p.k] = self.slab[...]
        for copy in self.plane():
            copy.start()

    def s3(self):
        for copy in self.plane(True):
            copy.wait_recv()
        self.across().start()

    def s4(self):
        self.across(True).wait_recv()

    def sent(self):
        for dz in (1, 2, 3):
            self.along_z(dz).wait_send()
        for copy in self.plane() + [self.across()]:
            copy.wait_send()


class Scatter:
    def __init__(self, p, r0, r1a, r1b, r2, v, r3, fin, sems):
        self.p, self.r0, self.r1a, self.r1b, self.r2, self.v, self.r3, self.fin = p, r0, r1a, r1b, r2, v, r3, fin
        self.ks, self.kr, self.xs, self.xr, self.zs, self.zr = sems

    def across(self, c, src):
        p = self.p
        return p.copy(src.at[:, :, 1 - p.k], self.r0.at[c], self.ks.at[c], self.kr.at[c], dp=p.sib)

    def first(self, c):
        p, r = self.p, self.r0
        return (
            p.copy(r.at[c, :, 1 - p.x, :, pl.ds(0, 384)], self.r1a.at[c], self.xs.at[c, 0], self.xr.at[c, 0], dp=p.xn),
            p.copy(r.at[c, 1 - p.y, :, :, pl.ds(384, 384)], self.r1b.at[c], self.xs.at[c, 1], self.xr.at[c, 1], dp=p.yn),
        )

    def second(self, c):
        p = self.p
        return (
            p.copy(self.r1a.at[c, 1 - p.y], self.r2.at[c, 0], self.xs.at[c, 2], self.xr.at[c, 2], dp=p.yn),
            p.copy(self.r1b.at[c, 1 - p.x], self.r2.at[c, 1], self.xs.at[c, 3], self.xr.at[c, 3], dp=p.xn),
        )

    def along_z(self, c, dz):
        p = self.p
        return p.copy(self.v.at[c, p.up(dz)], self.r3.at[c, dz - 1], self.zs.at[c, dz - 1], self.zr.at[c, dz - 1],
                      z=p.up(dz))

    def s1(self, c, src, own):
        self.across(c, src).wait_recv()
        for a in range(2):
            for b in range(2):
                self.r0[c, a, b] = (self.r0[c, a, b].astype(F32) + own(a, b).astype(F32)).astype(BF)
        for copy in self.first(c):
            copy.start()

    def s2(self, c):
        p = self.p
        for copy in self.first(c):
            copy.wait_recv()
        for a in range(2):
            self.r1a[c, a] = (self.r1a[c, a].astype(F32) + self.r0[c, a, p.x, :, :384].astype(F32)).astype(BF)
            self.r1b[c, a] = (self.r1b[c, a].astype(F32) + self.r0[c, p.y, a, :, 384:].astype(F32)).astype(BF)
        for copy in self.second(c):
            copy.start()

    def s3(self, c):
        p = self.p
        for copy in self.second(c):
            copy.wait_recv()
        left = self.r1a[c, p.y].astype(F32) + self.r2[c, 0].astype(F32)
        right = self.r1b[c, p.x].astype(F32) + self.r2[c, 1].astype(F32)
        self.v[c] = slab_of(jnp.concatenate([left, right], axis=1).reshape(4, 24, 768))
        for dz in (1, 2, 3):
            self.along_z(c, dz).start()

    def s4(self, c):
        for dz in (1, 2, 3):
            self.along_z(c, dz).wait_recv()
        total = rows_of(self.v[c, self.p.z])
        for dz in range(3):
            total = total + rows_of(self.r3[c, dz])
        self.fin[c] = total

    def sent(self, c, src):
        for copy in (self.across(c, src),) + self.first(c) + self.second(c):
            copy.wait_send()
        for dz in (1, 2, 3):
            self.along_z(c, dz).wait_send()


class SmallScatter:
    def __init__(self, p, src, r0, r1, r2, send, recv):
        self.p, self.src, self.r0, self.r1, self.r2, self.send, self.recv = p, src, r0, r1, r2, send, recv

    def across(self):
        p = self.p
        return p.copy(self.src.at[:, :, 1 - p.k], self.r0, self.send.at[0], self.recv.at[0], dp=p.sib)

    def plane(self):
        p = self.p
        return [p.copy(self.r0.at[y, x], self.r1.at[n], self.send.at[1 + n], self.recv.at[1 + n], dp=dp)
                for n, (dp, y, x) in enumerate(((p.xn, p.y, 1 - p.x), (p.yn, 1 - p.y, p.x), (p.diag, 1 - p.y, 1 - p.x)))]

    def along_z(self, dz):
        p = self.p
        return p.copy(self.r0.at[p.y, p.x, pl.ds(pl.multiple_of(24 * p.up(dz), 8), 24)], self.r2.at[dz - 1],
                      self.send.at[3 + dz], self.recv.at[3 + dz], z=p.up(dz))

    def s0(self):
        self.across().start()

    def s1(self):
        p = self.p
        self.across().wait_recv()
        for a in range(2):
            for b in range(2):
                self.r0[a, b] = self.r0[a, b] + self.src[a, b, p.k]
        for copy in self.plane():
            copy.start()

    def s2(self):
        p = self.p
        for copy in self.plane():
            copy.wait_recv()
        self.r0[p.y, p.x] = self.r0[p.y, p.x] + self.r1[0] + self.r1[1] + self.r1[2]
        for dz in (1, 2, 3):
            self.along_z(dz).start()

    def s3(self):
        p = self.p
        for dz in (1, 2, 3):
            self.along_z(dz).wait_recv()
        own = self.r0[p.y, p.x, pl.ds(pl.multiple_of(24 * p.z, 8), 24), :]
        return own + self.r2[0] + self.r2[1] + self.r2[2]

    def sent(self):
        for copy in [self.across()] + self.plane() + [self.along_z(dz) for dz in (1, 2, 3)]:
            copy.wait_send()


def piece_masks(width, total, count):
    lane = lax.broadcasted_iota(jnp.int32, (1, total), 1)
    inside = lax.rem(lane, width)
    place = lax.broadcasted_iota(jnp.int32, (128, total), 0) == inside
    owner = lax.broadcasted_iota(jnp.int32, (count, total), 0) * width == lane - inside
    return place, owner


def unpack_small(pieces, first, number, width, total):
    place, owner = piece_masks(width, total, 32)
    place = place.astype(BF)
    out = []
    for n in range(number):
        spread = mm(pieces[:, first + n, :].astype(BF), place)
        out.append(jnp.sum(jnp.where(owner, spread, 0.0), axis=0, keepdims=True))
    return out


def pack_small(pieces, first, vectors, width, total):
    place, owner = piece_masks(width, total, 32)
    place = place.astype(BF)
    for n, vector in enumerate(vectors):
        high = vector.astype(BF)
        low = (vector - high.astype(F32)).astype(BF)
        both = jnp.concatenate([jnp.where(owner, high.astype(F32), 0.0), jnp.where(owner, low.astype(F32), 0.0)], axis=0)
        both = mm_nt(both.astype(BF), place)
        pieces[:, first + n, :] = both[:32] + both[32:]


def weight(w, c):
    return w[c].reshape(768, 768)


def lane_block(start):
    return pl.ds(pl.multiple_of(start, 128), 128)


def project_group(g, tok, w, bqkv, conv, qkv, pkv, kvf):
    for r in range(2):
        rows = pl.ds(512 * r, 512)
        low = (mm(tok[rows, :], weight(w, g)) + bqkv[g]).astype(BF)
        qkv[g, rows, :] = low
        for part in range(4):
            kvf[part, pl.ds(8 + 512 * r, 512), :] = low[:, 256 + 128 * part:384 + 128 * part].astype(F32)
    for part in range(4):
        cols = pl.ds(128 * part, 128)
        total = jnp.zeros((256, 128), F32)
        for t in range(5):
            total = total + conv[g, pl.ds(t, 1), cols] * kvf[part, pl.ds(6 + t, 256, stride=4), :]
        pkv[g, :, cols] = total.astype(BF)


def attend_blocks(g, blocks, qkv, pkv, ctx, lse):
    parts = []
    for b in blocks:
        ns, ps, near, far = window(b)
        rows = pl.ds(pl.multiple_of(b * 128, 128), 128)
        for pr in range(2):
            parts.append(dict(
                near=near, far=far, rows=rows, lanes=lane_block(256 * g + 128 * pr), at=(g * 2 + pr) * 8 + b,
                qm=head_split(qkv[g, rows, 128 * pr:128 * pr + 128], 0.125),
                kn=qkv[g, pl.ds(ns, 256), 256 + 128 * pr:384 + 128 * pr],
                kp=pkv[g, pl.ds(ps, 160), 128 * pr:128 * pr + 128],
                vn=qkv[g, pl.ds(ns, 256), 512 + 128 * pr:640 + 128 * pr],
                vp=pkv[g, pl.ds(ps, 160), 256 + 128 * pr:384 + 128 * pr]))
    for t in parts:
        t["sn"] = jnp.where(t["near"], mm_nt(t["kn"], t["qm"]), -1e30)
        t["sp"] = jnp.where(t["far"], mm_nt(t["kp"], t["qm"]), -1e30)
    for t in parts:
        t["peak"] = jnp.maximum(jnp.max(t["sn"], axis=0, keepdims=True), jnp.max(t["sp"], axis=0, keepdims=True))
    for t in parts:
        t["en"] = jnp.exp(t["sn"] - t["peak"])
        t["ep"] = jnp.exp(t["sp"] - t["peak"])
    for t in parts:
        t["total"] = jnp.sum(t["en"], axis=0, keepdims=True) + jnp.sum(t["ep"], axis=0, keepdims=True)
    for t in parts:
        out = mm_tn(t["vn"], t["en"].astype(BF)) + mm_tn(t["vp"], t["ep"].astype(BF))
        t["out"] = head_join(out * pl.reciprocal(t["total"])).T.astype(BF)
    for t in parts:
        ctx[t["rows"], t["lanes"]] = t["out"]
        lse[t["at"]] = t["peak"] + jnp.log(t["total"])


def clear_edges(kvf):
    kvf[:, 0:8, :] = jnp.zeros((4, 8, 128), F32)
    kvf[:, 1032:1040, :] = jnp.zeros((4, 8, 128), F32)


def forward_kernel(comm, *refs):
    if comm:
        (tok, wqkv, bq_own, cv_own, wout, *six, wup, bu_own, wdn, pos, cot,
         out_o, pre_o, first_o, acc_o, dbr_o, gp_o, gwd_o, qkv_o, pkv_o, ctx_o, lse_o, gsm, w_o, conv, vec,
         w, buf, act, gp, acc, pre, first, dbr, tr, ctx, pkv, lse, out, kvf, stage, sems, osem,
         slab, slab_s, dense_s, pieces, bqkv, bup,
         zs, zr, xs, xr, ks, kr, ss, sr) = refs
    else:
        (tok, w_in, bqkv, conv, vec, bup, pos, cot,
         out_o, pre_o, first_o, acc_o, dbr_o, gp_o, gwd_o, qkv_o, pkv_o, ctx_o, lse_o, gsm,
         w, buf, act, gp, acc, pre, first, dbr, tr, ctx, pkv, lse, out, kvf, stage, sems, osem) = refs
    qkv = buf
    clear_edges(kvf)
    kept = []

    def keep(src, dst):
        kept.append(pltpu.make_async_copy(src, dst, osem.at[len(kept)]))
        kept[-1].start()

    todo = []
    if comm:
        p = Place()
        big = Gather(p, slab, w, (zs, zr, xs, xr, ks, kr))
        tiny = SmallGather(p, slab_s, dense_s, ss, sr)
        slab_s[p.z] = jnp.zeros((24, 128), F32)
        slab_s[p.z, 0:1, 0:72] = bq_own[...].astype(F32)
        slab_s[p.z, 1:6, 0:48] = cv_own[...].astype(F32)
        for i in range(6):
            slab_s[p.z, 6 + i:7 + i, 0:24] = six[i][...].astype(F32)
        slab_s[p.z, 12:13, 0:96] = bu_own[...].astype(F32)
        for c in range(12):
            if c < 3:
                rows24 = jnp.concatenate([wqkv[:, 768 * i + 256 * c:768 * i + 256 * c + 256] for i in range(3)], axis=1)
            elif c == 3:
                rows24 = wout[...]
            else:
                rows24 = (wup if c % 2 == 0 else wdn)[:, 768 * ((c - 4) // 2):768 * ((c - 4) // 2) + 768]
            slab[c, p.z] = slab_of(rows24.astype(F32))
            if c == 0:
                p.greet()
                tiny.s1()
            big.s1(c)
        tiny.s2()
        big.s2(0)
        big.s2(1)
        tiny.s3()
        big.s3(0)
        big.s2(2)
        big.s3(1)
        big.s2(3)
        big.s4(0)
        tiny.s4()
        pieces[...] = dense_s[...].reshape(32, 24, 128)
        whole = unpack_small(pieces, 0, 1, 72, 2304)[0]
        for g in range(3):
            for i in range(3):
                bqkv[g, :, 256 * i:256 * i + 256] = whole[:, 768 * i + 256 * g:768 * i + 256 * g + 256]
        taps = unpack_small(pieces, 1, 5, 48, 1536)
        for t in range(5):
            for g in range(3):
                for i in range(2):
                    conv[g, t:t + 1, 256 * i:256 * i + 256] = taps[t][:, 768 * i + 256 * g:768 * i + 256 * g + 256]
        rest = unpack_small(pieces, 6, 6, 24, 768)
        for i in range(6):
            vec[i:i + 1, :] = rest[i]
        whole = unpack_small(pieces, 12, 1, 96, 3072)[0]
        for j in range(4):
            bup[j] = whole[:, 768 * j:768 * j + 768]
        big.s5(0)
        todo = [[(big.s2, 10), (big.s3, 8)], [(big.s4, 7), (big.s2, 11)], [(big.s3, 9)], [(big.s4, 8), (big.s3, 10)],
                [(big.s4, 9), (big.s3, 11)], [(big.s4, 10)], [(big.s4, 11)]]
    else:
        load = pltpu.make_async_copy(w_in, w, sems.at[0])
        load.start()
        load.wait()

    def progress():
        for step, c in todo.pop(0) if todo else ():
            step(c)

    def group(g, carry):
        if comm:
            @pl.when(g > 0)
            def _():
                big.s5(g)
        project_group(g, tok, w, bqkv, conv, qkv, pkv, kvf)

        def block(b, inner):
            if comm:
                i = 4 * g + b
                n = lax.div(i, 2)

                @pl.when(lax.rem(i, 2) == 0)
                def _():
                    big.s2(4 + n)
                    big.s3(2 + n)

                @pl.when(lax.rem(i, 2) == 1)
                def _():
                    big.s4(1 + n)
            attend_blocks(g, (2 * b, 2 * b + 1), qkv, pkv, ctx, lse)
            return inner

        return lax.fori_loop(0, 4, block, carry)

    lax.fori_loop(0, 3, group, 0)
    keep(qkv.at[pl.ds(0, 3)], qkv_o)
    keep(pkv, pkv_o)
    keep(ctx, ctx_o)
    keep(lse, lse_o)
    if comm:
        big.s5(3)
        keep(w.at[pl.ds(0, 4)], w_o.at[pl.ds(0, 4)])
    b_out, gain1, shift1, b_down, gain2, shift2 = [vec[pl.ds(i, 1), :] for i in range(6)]
    tiles = [pl.ds(512 * r, 512) for r in range(2)]
    for rows in tiles:
        pre_one = tok[rows, :].astype(F32) + mm_nt(ctx[rows, :], weight(w, 3)) + b_out
        pre[rows, :] = pre_one
        xhat, rate = norm_stats(pre_one)
        low = (xhat * gain1 + shift1).astype(BF)
        first[rows, :] = low
        acc[rows, :] = low.astype(F32) + b_down
        progress()
    keep(pre, pre_o)
    keep(first, first_o)
    for j in range(4):
        if comm:
            big.s5(4 + 2 * j)
            big.s5(5 + 2 * j)
            keep(w.at[pl.ds(4 + 2 * j, 2)], w_o.at[pl.ds(4 + 2 * j, 2)])
        for rows in tiles:
            value, slope = gelu_both(mm(first[rows, :], weight(w, 4 + 2 * j)) + bup[j])
            low = value.astype(BF)
            act[j, rows, :] = low
            gp[j, rows, :] = slope.astype(BF)
            acc[rows, :] += mm_nt(low, weight(w, 5 + 2 * j))
            progress()
        keep(gp.at[j], gp_o.at[j])
    sums = [jnp.zeros((1, 768), F32) for _ in range(3)]
    for r, rows in enumerate(tiles):
        xhat, rate = norm_stats(acc[rows, :])
        out[rows, :] = (xhat * gain2 + shift2).astype(BF)
        row = 512 * r + lax.broadcasted_iota(jnp.int32, (512, 160), 0)
        dy = mm((row == pos[...]).astype(BF), cot[...])
        sums[1] = sums[1] + colsum(dy * xhat)
        sums[2] = sums[2] + colsum(dy)
        dacc = norm_back(xhat, rate, gain2, dy)
        low = dacc.astype(BF)
        dbr[rows, :] = low
        acc[rows, :] = dacc
        sums[0] = sums[0] + colsum(low.astype(F32))
    gsm[...] = jnp.zeros_like(gsm)
    for i in range(3):
        gsm[2 + i:3 + i, :] = sums[i]
    keep(out, out_o)
    keep(dbr, dbr_o)
    keep(acc, acc_o)
    tr[...] = dbr[...].T
    sent = []
    for j in range(4):
        if j >= 2:
            sent[j - 2].wait()
        stage[j % 2] = mm(tr[...], act[j]).astype(BF).reshape(2, 2, 2, 96, 768)
        sent.append(pltpu.make_async_copy(stage.at[j % 2], gwd_o.at[j], sems.at[j % 2]))
        sent[j].start()
    sent[2].wait()
    sent[3].wait()
    for copy in kept:
        copy.wait()
    if comm:
        big.sent(12)
        tiny.sent()


def forward_call(comm, *args):
    outs = [
        (struct((1024, 768), BF), ANY), (struct((1024, 768), F32), ANY), (struct((1024, 768), BF), ANY),
        (struct((1024, 768), F32), ANY), (struct((1024, 768), BF), ANY), (struct((4, 1024, 768), BF), ANY),
        (struct((4, 2, 2, 2, 96, 768), BF), ANY), (struct((3, 1024, 768), BF), ANY), (struct((3, 256, 512), BF), ANY),
        (struct((1024, 768), BF), ANY), (struct((48, 1, 256), F32), ANY), (struct((8, 768), F32), VM),
    ]
    scratch = [
        pltpu.VMEM((12, 2, 2, 2, 96, 768), BF), pltpu.VMEM((3, 1024, 768), BF), pltpu.VMEM((4, 1024, 768), BF),
        pltpu.VMEM((4, 1024, 768), BF), pltpu.VMEM((1024, 768), F32), pltpu.VMEM((1024, 768), F32),
        pltpu.VMEM((1024, 768), BF), pltpu.VMEM((1024, 768), BF), pltpu.VMEM((768, 1024), BF), pltpu.VMEM((1024, 768), BF),
        pltpu.VMEM((3, 256, 512), BF), pltpu.VMEM((48, 1, 256), F32), pltpu.VMEM((1024, 768), BF),
        pltpu.VMEM((4, 1040, 128), F32), pltpu.VMEM((2, 2, 2, 2, 96, 768), BF), DMA((2,)), DMA((20,)),
    ]
    if comm:
        outs += [(struct((12, 2, 2, 2, 96, 768), BF), ANY), (struct((3, 8, 512), F32), VM), (struct((8, 768), F32), VM)]
        scratch += [
            pltpu.VMEM((12, 4, 16, 1152), BF), pltpu.VMEM((4, 24, 128), F32), pltpu.VMEM((2, 2, 2, 4, 24, 128), F32),
            pltpu.VMEM((32, 24, 128), F32), pltpu.VMEM((3, 1, 768), F32), pltpu.VMEM((4, 1, 768), F32),
            DMA((12, 3)), DMA((12, 3)), DMA((12, 4)), DMA((12, 4)), DMA((12,)), DMA((12,)), DMA((7,)), DMA((7,)),
        ]
        params = pltpu.CompilerParams(vmem_limit_bytes=LIMIT, collective_id=1, has_side_effects=True)
    else:
        params = pltpu.CompilerParams(vmem_limit_bytes=LIMIT)
    ins = [VM] * len(args)
    if not comm:
        ins[1] = ANY
    return pl.pallas_call(
        functools.partial(forward_kernel, comm), in_specs=ins, out_specs=[o[1] for o in outs],
        out_shape=[o[0] for o in outs], scratch_shapes=scratch, compiler_params=params, name="forward")(*args)


def qkv_rows(g, start, size):
    return pl.ds(pl.multiple_of(3072 + 1024 * g + start, 32), size)


def back_blocks(g, blocks, wb, pkv, buf, lse, dk, dv, dpk, dpv):
    parts = []
    for b in blocks:
        ns, ps, near, far = window(b)
        first_row = pl.multiple_of(b * 128, 128)
        rows, prow = pl.ds(first_row, 128), pl.ds(ps, 160)
        qrows, krows = qkv_rows(g, first_row, 128), qkv_rows(g, ns, 256)
        for pr in range(2):
            parts.append(dict(
                near=near, far=far, rows=rows, nr=pl.ds(ns, 256), prow=prow, ln=pl.ds(128 * pr, 128),
                qm=head_split(wb[qrows, 128 * pr:128 * pr + 128], 0.125),
                dm=head_split(buf[3, rows, lane_block(256 * g + 128 * pr)], 1.0),
                kn=wb[krows, 256 + 128 * pr:384 + 128 * pr],
                kp=pkv[g, prow, 128 * pr:128 * pr + 128],
                vn=wb[krows, 512 + 128 * pr:640 + 128 * pr],
                vp=pkv[g, prow, 256 + 128 * pr:384 + 128 * pr],
                ls=lse[(g * 2 + pr) * 8 + b]))
    for t in parts:
        t["pn"] = jnp.exp(jnp.where(t["near"], mm_nt(t["kn"], t["qm"]), -1e30) - t["ls"])
        t["pp"] = jnp.exp(jnp.where(t["far"], mm_nt(t["kp"], t["qm"]), -1e30) - t["ls"])
    for t in parts:
        t["dn"] = mm_nt(t["vn"], t["dm"])
        t["dp"] = mm_nt(t["vp"], t["dm"])
        t["gvn"] = mm(t["pn"].astype(BF), t["dm"])
        t["gvp"] = mm(t["pp"].astype(BF), t["dm"])
    for t in parts:
        rd = jnp.sum(t["pn"] * t["dn"], axis=0, keepdims=True) + jnp.sum(t["pp"] * t["dp"], axis=0, keepdims=True)
        t["sn"] = (t["pn"] * (t["dn"] - rd)).astype(BF)
        t["sp"] = (t["pp"] * (t["dp"] - rd)).astype(BF)
    for t in parts:
        t["gkn"] = mm(t["sn"], t["qm"])
        t["gkp"] = mm(t["sp"], t["qm"])
        t["gq"] = (head_join(mm_tn(t["kn"], t["sn"]) + mm_tn(t["kp"], t["sp"])).T * 0.125).astype(BF)
    for t in parts:
        dk[t["nr"], t["ln"]] += t["gkn"]
        dpk[t["prow"], t["ln"]] += t["gkp"]
        dv[t["nr"], t["ln"]] += t["gvn"]
        dpv[t["prow"], t["ln"]] += t["gvp"]
        buf[g, t["rows"], t["ln"]] = t["gq"]


def pool_back(g, conv, wb, kvf, dk, dv, dpk, dpv, buf, gconv):
    for part in range(4):
        kvf[part, 8:1032, :] = wb[qkv_rows(g, 0, 1024), 256 + 128 * part:384 + 128 * part].astype(F32)
    for part in range(4):
        cols = pl.ds(128 * part, 128)
        src, dst = (dpk, dk) if part < 2 else (dpv, dv)
        half = pl.ds(128 * (part % 2), 128)
        dpool = src[:, half]
        for t in range(5):
            gconv[g, pl.ds(t, 1), cols] = colsum(dpool * kvf[part, pl.ds(6 + t, 256, stride=4), :])
        kvf[part, 8:1032, :] = dst[:, half]
        for t in range(5):
            at = pl.ds(6 + t, 256, stride=4)
            kvf[part, at, :] += conv[g, pl.ds(t, 1), cols] * dpool
        buf[g, :, 256 + 128 * part:384 + 128 * part] = kvf[part, 8:1032, :].astype(BF)
        kvf[part, 0:8, :] = jnp.zeros((8, 128), F32)
        kvf[part, 1032:1040, :] = jnp.zeros((8, 128), F32)


BLOCKS = (2, 2, 2, 96, 768)


STEPS = (
    ((1, 0),), (), ((1, 1),), ((2, 0),), ((1, 2),), ((2, 1),), ((3, 0), (1, 3)), ((2, 2),), ((3, 1), (1, 4)),
    ((2, 3),), ((4, 0), (3, 2), (1, 5)), ((2, 4),), ((3, 3), (4, 1), (1, 6), (2, 5)), ((4, 2), (3, 4)), ((4, 3),),
)
LOOP_STEPS = {
    0: ((1, 7),), 1: ((2, 6),), 2: ((3, 5), (4, 4)), 3: ((1, 8), (2, 7)), 4: ((3, 6),), 5: ((4, 5),), 6: ((1, 9), (2, 8), (3, 7)),
    7: ((4, 6),), 8: ((3, 8),), 9: ((1, 10), (2, 9), (4, 7)), 11: ((2, 10), (3, 9), (4, 8)),
}


def backward_kernel(comm, *refs):
    (tok_i, w_i, conv, vec, pre_i, first_i, acc_i, dbr_i, gp_i, qkv_i, pkv_i, ctx_i, lse_i, gsm_in) = refs[:14]
    if comm:
        (gwd_i, gtok_o, fin, tot,
         wb, buf, xb, db, tr, acc, gtok, pkv, lse, kvf, isem, osem,
         gat, gconv, gbias, gbout, gsm, gbup, r0, r1a, r1b, r2, v, r3, own, pieces, small, t0, t1, t2,
         ks, kr, xs, xr, zs, zr, ls, ss, sr) = refs[14:]
    else:
        (gtok_o, gat, gconv, gbias, gbout, gsm, gbup,
         wb, buf, xb, db, tr, acc, gtok, pkv, lse, kvf, isem, osem) = refs[14:]
    dk, dv = acc.at[:, pl.ds(0, 256)], acc.at[:, pl.ds(256, 256)]
    dpk, dpv = acc.at[pl.ds(0, 256), pl.ds(512, 256)], acc.at[pl.ds(256, 256), pl.ds(512, 256)]
    loads = {}

    def load(name, src, dst):
        loads[name] = pltpu.make_async_copy(src, dst, isem.at[len(loads)])
        loads[name].start()

    def slot(n):
        return wb[pl.ds(768 * n, 768), :]

    def load_weight(c, n):
        for i in range(8):
            load(("w", c, i), w_i.at[c, i // 4, i // 2 % 2, i % 2], wb.at[pl.ds(768 * n + 96 * i, 96), :])

    def have_weight(c):
        for i in range(8):
            loads["w", c, i].wait()

    load("dbr", dbr_i, db)
    load_weight(5, 1)
    load(("gp", 0), gp_i.at[0], buf.at[0])
    load_weight(4, 0)
    load("acc", acc_i, acc)
    load("first", first_i, xb)
    if comm:
        p = Place()
        big = Scatter(p, r0, r1a, r1b, r2, v, r3, fin, (ks, kr, xs, xr, zs, zr))
        tiny = SmallScatter(p, small, t0, t1, t2, ss, sr)
        p.greet()

        def fetch(c):
            return pltpu.make_async_copy(gwd_i.at[c, :, :, p.k], own.at[c % 2], ls.at[c % 2])

        for c in range(4):
            big.across(c, gwd_i.at[c]).start()
        fetch(0).start()
        fetch(1).start()

        def take(steps):
            for stage, c in steps:
                if stage > 1:
                    (big.s2, big.s3, big.s4)[stage - 2](c)
                elif c >= 4:
                    at = c - 4 if c < 9 else c - 9
                    big.s1(c, gat.at[0], lambda a, b: gat[at, a, b, p.k])
                else:
                    fetch(c).wait()
                    big.s1(c, gat.at[0], lambda a, b: own[c % 2, a, b])
                    if c < 2:
                        fetch(c + 2).start()

    def run(n):
        if comm:
            take(STEPS[n])

    for j in range(1, 4):
        load_weight(5 + 2 * j, 1 + 2 * j)
        load(("gp", j), gp_i.at[j], buf.at[j])
        load_weight(4 + 2 * j, 2 * j)
    load("pre", pre_i, gtok)
    load("pkv", pkv_i, pkv)
    load("lse", lse_i, lse)
    clear_edges(kvf)
    gbup[...] = jnp.zeros_like(gbup)
    gsm[...] = gsm_in[...]
    tiles = [pl.ds(512 * r, 512) for r in range(2)]
    loads["first"].wait()
    tr[...] = xb[...].T
    load("tok", tok_i, xb)
    loads["dbr"].wait()
    for j in range(4):
        have_weight(5 + 2 * j)
        loads["gp", j].wait()
        for r, rows in enumerate(tiles):
            low = (mm(db[rows, :], slot(1 + 2 * j)) * buf[j, rows, :].astype(F32)).astype(BF)
            buf[j, rows, :] = low
            gbup[j] += colsum(low.astype(F32))
            if r == 0:
                have_weight(4 + 2 * j)
                if j == 0:
                    loads["acc"].wait()
            acc[rows, :] += mm_nt(low, slot(2 * j))
            run(3 * j + r)
        gat[j] = mm(tr[...], buf[j]).astype(BF).reshape(BLOCKS)
        if comm:
            big.across(4 + j, gat.at[j]).start()
            run(3 * j + 2)
        if j == 1:
            for c in range(4):
                load_weight(c, c)
    for g in range(3):
        load(("qkv", g), qkv_i.at[g], wb.at[pl.ds(3072 + 1024 * g, 1024), :])
    load("ctx", ctx_i, db)
    loads["pre"].wait()
    gain1 = vec[1:2, :]
    sums = [jnp.zeros((1, 768), F32) for _ in range(3)]
    have_weight(3)
    for rows in tiles:
        xhat, rate = norm_stats(gtok[rows, :])
        dacc = acc[rows, :]
        sums[0] = sums[0] + colsum(dacc * xhat)
        sums[1] = sums[1] + colsum(dacc)
        dpre = norm_back(xhat, rate, gain1, dacc)
        gtok[rows, :] = dpre
        da = dpre.astype(BF)
        sums[2] = sums[2] + colsum(da.astype(F32))
        buf[3, rows, :] = mm(da, slot(3)).astype(BF)
        tr[:, rows] = da.T
    gsm[0:1, :] = sums[0]
    gsm[1:2, :] = sums[1]
    gbout[...] = sums[2]
    if comm:
        run(12)
        pieces[...] = jnp.zeros_like(pieces)
        pack_small(pieces, 6, [gbout[...]] + [gsm[i:i + 1, :] for i in range(5)], 24, 768)
        pack_small(pieces, 12, [jnp.concatenate([gbup[j] for j in range(4)], axis=1)], 96, 3072)
    loads["ctx"].wait()
    gat[4] = mm(tr[...], db[...]).astype(BF).reshape(BLOCKS)
    if comm:
        big.across(8, gat.at[4]).start()
        run(13)
    loads["tok"].wait()
    tr[...] = xb[...].T
    loads["pkv"].wait()
    loads["lse"].wait()
    for g in range(3):
        loads["qkv", g].wait()
        have_weight(g)
    run(14)

    def group(g, carry):
        acc[...] = jnp.zeros_like(acc)

        def block(b, inner):
            if comm:
                for i, steps in LOOP_STEPS.items():
                    pl.when(4 * g + b == i)(functools.partial(take, steps))
            back_blocks(g, (2 * b, 2 * b + 1), wb, pkv, buf, lse, dk, dv, dpk, dpv)
            return inner

        lax.fori_loop(0, 4, block, 0)
        pool_back(g, conv, wb, kvf, dk, dv, dpk, dpv, buf, gconv)
        if comm:
            big.across(4 + g, gat.at[0]).wait_send()
        gat[g if comm else 5 + g] = mm(tr[...], buf[g]).astype(BF).reshape(BLOCKS)
        if comm:
            big.across(9 + g, gat.at[g]).start()
        gbias[g] = colsum(buf[g].astype(F32))
        return carry

    lax.fori_loop(0, 3, group, 0)
    parts = []

    def token_part(n):
        rows = pl.ds(256 * n, 256)
        total = gtok[rows, :]
        for g in range(3):
            total = total + mm_nt(buf[g, rows, :], slot(g))
        gtok[rows, :] = total
        parts.append(pltpu.make_async_copy(gtok.at[rows, :], gtok_o.at[rows, :], osem.at[n]))
        parts[n].start()

    if not comm:
        for n in range(4):
            token_part(n)
        for copy in parts:
            copy.wait()
        return

    take(((1, 11),))
    kinds = [jnp.concatenate([gbias[g][:, 256 * i:256 * i + 256] for i in range(3) for g in range(3)], axis=1)]
    pack_small(pieces, 0, kinds, 72, 2304)
    pack_small(pieces, 1, [
        jnp.concatenate([gconv[g, t:t + 1, 256 * i:256 * i + 256] for i in range(2) for g in range(3)], axis=1)
        for t in range(5)], 48, 1536)
    small[...] = pieces[...].reshape(2, 2, 2, 96, 128)
    tiny.s0()
    take(((3, 10),))
    token_part(0)
    tiny.s1()
    take(((2, 11),))
    token_part(1)
    tiny.s2()
    take(((4, 9), (3, 11)))
    token_part(2)
    take(((4, 10),))
    token_part(3)
    tot[...] = tiny.s3()
    take(((4, 11),))
    for c in range(12):
        for copy in big.first(c) + big.second(c) + tuple(big.along_z(c, dz) for dz in (1, 2, 3)):
            copy.wait_send()
        if c not in (4, 5, 6):
            big.across(c, gat.at[0]).wait_send()
    tiny.sent()
    for copy in parts:
        copy.wait()


def backward_call(comm, *args):
    scratch = [
        pltpu.VMEM((6144, 768), BF), pltpu.VMEM((4, 1024, 768), BF), pltpu.VMEM((1024, 768), BF), pltpu.VMEM((1024, 768), BF),
        pltpu.VMEM((768, 1024), BF), pltpu.VMEM((1024, 768), F32), pltpu.VMEM((1024, 768), F32),
        pltpu.VMEM((3, 256, 512), BF), pltpu.VMEM((48, 1, 256), F32),
        pltpu.VMEM((4, 1040, 128), F32), DMA((120,)), DMA((4,)),
    ]
    ins = [ANY] * len(args)
    for i in (2, 3, 13):
        ins[i] = VM
    local = [((5 if comm else 8,) + BLOCKS, BF), ((3, 8, 512), F32), ((3, 1, 768), F32), ((1, 768), F32), ((8, 768), F32), ((4, 1, 768), F32)]
    outs = [(struct((1024, 768), F32), ANY)]
    if comm:
        outs += [(struct((12, 24, 768), F32), VM), (struct((24, 128), F32), VM)]
        scratch += [pltpu.VMEM(*s) for s in local]
        scratch += [
            pltpu.VMEM((12, 2, 2, 96, 768), BF), pltpu.VMEM((12, 2, 96, 384), BF), pltpu.VMEM((12, 2, 96, 384), BF),
            pltpu.VMEM((12, 2, 96, 384), BF), pltpu.VMEM((12, 4, 16, 1152), BF), pltpu.VMEM((12, 3, 16, 1152), BF),
            pltpu.VMEM((2, 2, 2, 96, 768), BF), pltpu.VMEM((32, 24, 128), F32),
            pltpu.VMEM((2, 2, 2, 96, 128), F32), pltpu.VMEM((2, 2, 96, 128), F32), pltpu.VMEM((3, 96, 128), F32),
            pltpu.VMEM((3, 24, 128), F32),
            DMA((12,)), DMA((12,)), DMA((12, 4)), DMA((12, 4)), DMA((12, 3)), DMA((12, 3)), DMA((2,)), DMA((7,)), DMA((7,)),
        ]
        params = pltpu.CompilerParams(vmem_limit_bytes=LIMIT, collective_id=2, has_side_effects=True)
    else:
        outs += [(struct(*s), VM) for s in local]
        params = pltpu.CompilerParams(vmem_limit_bytes=LIMIT)
    return pl.pallas_call(
        functools.partial(backward_kernel, comm), in_specs=ins, out_specs=[o[1] for o in outs], out_shape=[o[0] for o in outs],
        scratch_shapes=scratch, compiler_params=params, name="backward")(*args)


def finish_kernel(out_i, gtok_i, fin, tot, out, gtok, gqkv, gqb, gcv, gwo, gbo, gg1, gs1, gwu, gbu, gwd, gbd, gg2, gs2):
    out[...] = out_i[...]
    gtok[...] = gtok_i[...]

    @pl.when(pl.program_id(0) == 0)
    def _():
        for j in range(4):
            gwd[:, 768 * j:768 * j + 768] = fin[j]
            gwu[:, 768 * j:768 * j + 768] = fin[4 + j]
        gwo[...] = fin[8]
        for g in range(3):
            for i in range(3):
                gqkv[:, 768 * i + 256 * g:768 * i + 256 * g + 256] = fin[9 + g, :, 256 * i:256 * i + 256]
        gqb[...] = tot[0:1, 0:72]
        gcv[...] = tot[1:6, 0:48]
        for i, ref in enumerate((gbo, gg1, gs1, gbd, gg2, gs2)):
            ref[...] = tot[6 + i:7 + i, 0:24]
        gbu[...] = tot[12:13, 0:96]


def finish_call(*args):
    shapes = ((24, 2304), (1, 72), (5, 48), (24, 768), (1, 24), (1, 24), (1, 24), (24, 3072), (1, 96),
              (24, 3072), (1, 24), (1, 24), (1, 24))
    part = pl.BlockSpec((256, 768), lambda n: (n, 0))

    def full(shape):
        return pl.BlockSpec(shape, lambda n: (0,) * len(shape))

    return pl.pallas_call(
        finish_kernel, grid=(4,), in_specs=[part, part, full((12, 24, 768)), full((24, 128))],
        out_specs=[part, part] + [full(s) for s in shapes],
        out_shape=[struct((1024, 768), BF), struct((1024, 768), F32)] + [struct(s, F32) for s in shapes],
        name="finish")(*args)


def shards_direct(tokens, w_qkv, b_qkv, conv_kv, w_out, b_out, gain_one, shift_one, w_up, b_up, w_down, b_down, gain_two,
                  shift_two, positions, cotangent):
    tok = tokens[0]
    out, pre, first, acc, dbr, gp, gwd, qkv, pkv, ctx, lse, gsm, w, conv, vec = forward_call(
        True, tok, w_qkv, b_qkv[None], conv_kv, w_out.T, b_out[None], gain_one[None], shift_one[None], b_down[None],
        gain_two[None], shift_two[None], w_up, b_up[None], w_down.T, positions, cotangent[0])
    gtok, fin, tot = backward_call(True, tok, w, conv, vec, pre, first, acc, dbr, gp, qkv, pkv, ctx, lse, gsm, gwd)
    (out, gtok, gqkv, gqb, gcv, gwo, gbo, gg1, gs1, gwu, gbu, gwd, gbd, gg2, gs2) = finish_call(out, gtok, fin, tot)
    return (out[None], gtok[None], gqkv, gqb[0], gcv, gwo.T, gbo[0], gg1[0], gs1[0], gwu, gbu[0], gwd.T, gbd[0], gg2[0], gs2[0])


def small_sizes(count):
    return [2304 // count] + [1536 // count] * 5 + [768 // count] * 6 + [3072 // count]


def by_group(v, kinds):
    return v.reshape(kinds, 3, 256).transpose(1, 0, 2).reshape(3, 1, kinds * 256)


def shards_general(tokens, w_qkv, b_qkv, conv_kv, w_out, b_out, gain_one, shift_one, w_up, b_up, w_down, b_down, gain_two,
                   shift_two, positions, cotangent):
    rows = w_qkv.shape[0]
    count = 768 // rows
    blocks = (2, 2, 2, 96, 768)
    up = w_up.reshape(rows, 4, 768).transpose(1, 0, 2)
    down = w_down.reshape(4, 768, rows).transpose(0, 2, 1)
    own = jnp.concatenate([
        w_qkv.reshape(rows, 3, 3, 256).transpose(2, 0, 1, 3).reshape(3, rows, 768),
        w_out.T[None],
        jnp.stack([up, down], 1).reshape(8, rows, 768),
    ], 0)
    w = lax.all_gather(own, AXES, axis=1, tiled=True).reshape((12,) + blocks)
    small = jnp.concatenate([b_qkv, conv_kv.reshape(-1), b_out, gain_one, shift_one, b_down, gain_two, shift_two, b_up])
    small = lax.all_gather(small[None], AXES, axis=0, tiled=True).astype(F32)
    at, parts = 0, []
    for size in small_sizes(count):
        parts.append(small[:, at:at + size].reshape(-1))
        at += size
    bqkv = by_group(parts[0], 3)
    conv = jnp.concatenate([by_group(p, 2) for p in parts[1:6]] + [jnp.zeros((3, 3, 512), F32)], 1)
    vec = jnp.stack(parts[6:12] + [jnp.zeros((768,), F32)] * 2)
    bup = parts[12].reshape(4, 1, 768)
    out, pre, first, acc, dbr, gp, gwd, qkv, pkv, ctx, lse, gsm = forward_call(
        False, tokens[0], w, bqkv, conv, vec, bup, positions, cotangent[0])
    gwd = lax.psum_scatter(gwd.reshape(4, 768, 768), AXES, scatter_dimension=1, tiled=True).astype(F32)
    gtok, gat, gconv, gbias, gbout, gsm, gbup = backward_call(
        False, tokens[0], w, conv, vec, pre, first, acc, dbr, gp, qkv, pkv, ctx, lse, gsm)
    gat = lax.psum_scatter(gat.reshape(8, 768, 768), AXES, scatter_dimension=1, tiled=True).astype(F32)
    flat = [gbias.reshape(3, 3, 256).transpose(1, 0, 2).reshape(count, -1)]
    flat += [gconv[:, t].reshape(3, 2, 256).transpose(1, 0, 2).reshape(count, -1) for t in range(5)]
    flat += [gbout[0].reshape(count, -1)] + [gsm[i].reshape(count, -1) for i in range(5)] + [gbup.reshape(count, -1)]
    flat = lax.psum_scatter(jnp.concatenate(flat, 1), AXES, scatter_dimension=0, tiled=True)
    at, s = 0, []
    for size in small_sizes(count):
        s.append(flat[0, at:at + size])
        at += size
    return (
        out[None], gtok[None],
        gat[5:].reshape(3, rows, 3, 256).transpose(1, 2, 0, 3).reshape(rows, 2304),
        s[0], jnp.stack(s[1:6]), gat[4].T, s[6], s[7], s[8],
        gat[:4].transpose(1, 0, 2).reshape(rows, 3072), s[12],
        gwd.transpose(0, 2, 1).reshape(3072, rows), s[9], s[10], s[11],
    )


def solution(mesh):
    rows, cols, flat, item = P(AXES, None), P(None, AXES), P(AXES), P(AXES, None, None)
    direct = mesh.shape["dp"] == 8 and mesh.shape["fsdp"] == 4
    return jax.shard_map(
        shards_direct if direct else shards_general,
        mesh=mesh,
        in_specs=(item, rows, flat, cols, cols, flat, flat, flat, rows, flat, cols, flat, flat, flat, rows, item),
        out_specs=(item, item, rows, flat, cols, cols, flat, flat, flat, rows, flat, cols, flat, flat, flat),
        check_vma=False,
    )
```

```python
import functools
import jax
import jax.numpy as jnp
from jax import lax
from jax.experimental import pallas as pl
from jax.experimental.pallas import tpu as pltpu
from jax.sharding import PartitionSpec as P

F32 = jnp.float32
BF = jnp.bfloat16
EPS = 1e-5
NT = (((1,), (1,)), ((), ()))
TN = (((0,), (0,)), ((), ()))
AXES = ("dp", "fsdp")
VM = pl.BlockSpec(memory_space=pltpu.VMEM)
ANY = pl.BlockSpec(memory_space=pl.ANY)
LIMIT = 64 * 1024 * 1024 - 512 * 1024
DMA = pltpu.SemaphoreType.DMA
struct = jax.ShapeDtypeStruct


def mm(a, b):
    return jnp.dot(a, b, preferred_element_type=F32)


def mm_nt(a, b):
    return lax.dot_general(a, b, NT, preferred_element_type=F32)


def mm_tn(a, b):
    return lax.dot_general(a, b, TN, preferred_element_type=F32)


def norm_stats(values):
    average = jnp.mean(values, axis=-1, keepdims=True)
    centred = values - average
    variance = jnp.mean(centred * centred, axis=-1, keepdims=True)
    rate = lax.rsqrt(variance + EPS)
    return centred * rate, rate


def norm_back(xhat, rate, gain, dy):
    e = dy * gain
    mean_e = jnp.mean(e, axis=-1, keepdims=True)
    mean_ex = jnp.mean(e * xhat, axis=-1, keepdims=True)
    return rate * (e - mean_e - xhat * mean_ex)


def colsum(v):
    return jnp.sum(v, axis=0, keepdims=True)


def gelu_both(u):
    c = 0.7978845608028654
    u2 = u * u
    t = jnp.tanh(u * (c + (c * 0.044715) * u2))
    half = 0.5 + 0.5 * t
    value = u * half
    slope = half + (0.5 * u) * (1.0 - t * t) * (c + (3.0 * c * 0.044715) * u2)
    return value, slope


def head_split(x, scale):
    lane = lax.broadcasted_iota(jnp.int32, x.shape, 1)
    low = jnp.where(lane < 64, scale, 0.0).astype(BF)
    high = jnp.where(lane < 64, 0.0, scale).astype(BF)
    return jnp.concatenate([x * low, x * high], axis=0)


def head_join(r):
    return jnp.concatenate([r[:64, :128], r[64:, 128:]], axis=0)


def window(b):
    ns = pl.multiple_of(jnp.clip(b * 128 - 64, 0, 1024 - 256), 64)
    ps = pl.multiple_of(jnp.clip(b * 32 - 64, 0, 256 - 160), 32)
    col = b * 128 + (lax.broadcasted_iota(jnp.int32, (256, 256), 1) & 127)
    row = ns + lax.broadcasted_iota(jnp.int32, (256, 256), 0)
    near = jnp.abs(row - col) <= 64
    colp = b * 128 + (lax.broadcasted_iota(jnp.int32, (160, 256), 1) & 127)
    rowp = 4 * (ps + lax.broadcasted_iota(jnp.int32, (160, 256), 0))
    far = jnp.abs(rowp - colp) <= 256
    return ns, ps, near, far


class Place:
    def __init__(self):
        d = lax.axis_index("dp")
        self.d, self.z = d, lax.axis_index("fsdp")
        self.k, self.x, self.y = lax.rem(d, 2), lax.rem(lax.div(d, 2), 2), lax.div(d, 4)
        self.sib = d + 1 - 2 * self.k
        self.xn = d + 2 - 4 * self.x
        self.yn = d + 4 - 8 * self.y
        self.diag = self.xn + 4 - 8 * self.y

    def up(self, dz):
        return lax.rem(self.z + dz, 4)

    def copy(self, src, dst, send, recv, dp=None, z=None):
        return pltpu.make_async_remote_copy(
            src_ref=src, dst_ref=dst, send_sem=send, recv_sem=recv,
            device_id={"dp": self.d if dp is None else dp, "fsdp": self.z if z is None else z},
            device_id_type=pl.DeviceIdType.MESH)

    def greet(self):
        barrier = pltpu.get_barrier_semaphore()
        for dp in (self.sib, self.xn, self.yn, self.diag):
            pl.semaphore_signal(barrier, inc=1, device_id={"dp": dp, "fsdp": self.z},
                                device_id_type=pl.DeviceIdType.MESH)
        for dz in (1, 2, 3):
            pl.semaphore_signal(barrier, inc=1, device_id={"dp": self.d, "fsdp": self.up(dz)},
                                device_id_type=pl.DeviceIdType.MESH)
        pl.semaphore_wait(barrier, 7)


def slab_of(rows):
    last = jnp.concatenate([rows[..., 16:, :384], rows[..., 16:, 384:]], axis=-2)
    return jnp.concatenate([rows[..., :16, :], last], axis=-1).astype(BF)


def rows_of(slab):
    v = slab.astype(F32)
    last = jnp.concatenate([v[..., :8, 768:], v[..., 8:, 768:]], axis=-1)
    return jnp.concatenate([v[..., :768], last], axis=-2)


class Gather:
    def __init__(self, p, slab, dense, sems):
        self.p, self.slab, self.dense = p, slab, dense
        self.zs, self.zr, self.xs, self.xr, self.ks, self.kr = sems

    def along_z(self, c, dz, arriving=False):
        p = self.p
        slot = p.up(4 - dz) if arriving else p.z
        return p.copy(self.slab.at[c, p.z], self.slab.at[c, slot], self.zs.at[c, dz - 1], self.zr.at[c, dz - 1],
                      z=p.up(dz))

    def first(self, c, arriving=False):
        p, w = self.p, self.dense
        ya = 1 - p.y if arriving else p.y
        xa = 1 - p.x if arriving else p.x
        a, b = pl.ds(0, 384), pl.ds(384, 384)
        return (
            p.copy(w.at[c, p.y, p.x, p.k, :, a], w.at[c, p.y, xa, p.k, :, a], self.xs.at[c, 0], self.xr.at[c, 0], dp=p.xn),
            p.copy(w.at[c, p.y, p.x, p.k, :, b], w.at[c, ya, p.x, p.k, :, b], self.xs.at[c, 1], self.xr.at[c, 1], dp=p.yn),
        )

    def second(self, c, arriving=False):
        p, w = self.p, self.dense
        ya = 1 - p.y if arriving else p.y
        xa = 1 - p.x if arriving else p.x
        a, b = pl.ds(0, 384), pl.ds(384, 384)
        return (
            p.copy(w.at[c, p.y, :, p.k, :, a], w.at[c, ya, :, p.k, :, a], self.xs.at[c, 2], self.xr.at[c, 2], dp=p.yn),
            p.copy(w.at[c, :, p.x, p.k, :, b], w.at[c, :, xa, p.k, :, b], self.xs.at[c, 3], self.xr.at[c, 3], dp=p.xn),
        )

    def across(self, c, arriving=False):
        p, w = self.p, self.dense
        k = 1 - p.k if arriving else p.k
        return p.copy(w.at[c, :, :, p.k], w.at[c, :, :, k], self.ks.at[c], self.kr.at[c], dp=p.sib)

    def s1(self, c):
        for dz in (1, 2, 3):
            self.along_z(c, dz).start()

    def s2(self, c):
        p = self.p
        for dz in (1, 2, 3):
            self.along_z(c, dz, True).wait_recv()
        self.dense[c, p.y, p.x, p.k] = rows_of(self.slab[c]).reshape(96, 768).astype(BF)
        for copy in self.first(c):
            copy.start()

    def s3(self, c):
        for copy in self.first(c, True):
            copy.wait_recv()
        for copy in self.second(c):
            copy.start()

    def s4(self, c):
        for copy in self.second(c, True):
            copy.wait_recv()
        self.across(c).start()

    def s5(self, c):
        self.across(c, True).wait_recv()

    def sent(self, c):
        for dz in (1, 2, 3):
            self.along_z(c, dz).wait_send()
        for copy in self.first(c) + self.second(c) + (self.across(c),):
            copy.wait_send()


class PlaneFirst:
    def __init__(self, gather, c, group, sems):
        self.g, self.p, self.c, self.group = gather, gather.p, c, group
        self.ps, self.pr, self.zs, self.zr = sems

    def plane(self, arriving=False):
        p, me, out = self.p, 2 * self.p.y + self.p.x, []
        for n, (dp, other) in enumerate(((p.xn, me + 1 - 2 * p.x), (p.yn, me + 2 - 4 * p.y), (p.diag, 3 - me))):
            out.append(p.copy(self.group.at[p.z, me], self.group.at[p.z, other if arriving else me], self.ps.at[n], self.pr.at[n],
                              dp=dp))
        return out

    def along_z(self, arriving=False):
        p = self.p
        return [p.copy(self.group.at[p.z], self.group.at[p.up(4 - dz) if arriving else p.z], self.zs.at[dz - 1],
                       self.zr.at[dz - 1], z=p.up(dz)) for dz in (1, 2, 3)]

    def s1(self, slab):
        self.group[self.p.z, 2 * self.p.y + self.p.x] = slab
        for copy in self.plane():
            copy.start()

    def s2(self):
        for copy in self.plane(True):
            copy.wait_recv()
        for copy in self.along_z():
            copy.start()

    def s3(self):
        for copy in self.along_z(True):
            copy.wait_recv()
        for n in range(4):
            self.g.dense[self.c, n // 2, n % 2, self.p.k] = rows_of(self.group[:, n]).reshape(96, 768).astype(BF)
        self.g.across(self.c).start()

    def sent(self):
        for copy in self.plane() + self.along_z() + [self.g.across(self.c)]:
            copy.wait_send()


class SmallGather:
    def __init__(self, p, slab, dense, send, recv):
        self.p, self.slab, self.dense, self.send, self.recv = p, slab, dense, send, recv

    def along_z(self, dz, arriving=False):
        p = self.p
        slot = p.up(4 - dz) if arriving else p.z
        return p.copy(self.slab.at[p.z], self.slab.at[slot], self.send.at[dz - 1], self.recv.at[dz - 1], z=p.up(dz))

    def plane(self, arriving=False):
        p, w = self.p, self.dense
        out = []
        for n, (dp, y, x) in enumerate(((p.xn, p.y, 1 - p.x), (p.yn, 1 - p.y, p.x), (p.diag, 1 - p.y, 1 - p.x))):
            dst = w.at[y, x, p.k] if arriving else w.at[p.y, p.x, p.k]
            out.append(p.copy(w.at[p.y, p.x, p.k], dst, self.send.at[3 + n], self.recv.at[3 + n], dp=dp))
        return out

    def across(self, arriving=False):
        p, w = self.p, self.dense
        k = 1 - p.k if arriving else p.k
        return p.copy(w.at[:, :, p.k], w.at[:, :, k], self.send.at[6], self.recv.at[6], dp=p.sib)

    def s1(self):
        for dz in (1, 2, 3):
            self.along_z(dz).start()

    def s2(self):
        p = self.p
        for dz in (1, 2, 3):
            self.along_z(dz, True).wait_recv()
        self.dense[p.y, p.x, p.k] = self.slab[...]
        for copy in self.plane():
            copy.start()

    def s3(self):
        for copy in self.plane(True):
            copy.wait_recv()
        self.across().start()

    def s4(self):
        self.across(True).wait_recv()

    def sent(self):
        for dz in (1, 2, 3):
            self.along_z(dz).wait_send()
        for copy in self.plane() + [self.across()]:
            copy.wait_send()


class Scatter:
    def __init__(self, p, r0, r1a, r1b, r2, v, r3, fin, sems):
        self.p, self.r0, self.r1a, self.r1b, self.r2, self.v, self.r3, self.fin = p, r0, r1a, r1b, r2, v, r3, fin
        self.ks, self.kr, self.xs, self.xr, self.zs, self.zr = sems

    def across(self, c, src):
        p = self.p
        return p.copy(src.at[:, :, 1 - p.k], self.r0.at[c], self.ks.at[c], self.kr.at[c], dp=p.sib)

    def first(self, c):
        p, r = self.p, self.r0
        return (
            p.copy(r.at[c, :, 1 - p.x, :, pl.ds(0, 384)], self.r1a.at[c], self.xs.at[c, 0], self.xr.at[c, 0], dp=p.xn),
            p.copy(r.at[c, 1 - p.y, :, :, pl.ds(384, 384)], self.r1b.at[c], self.xs.at[c, 1], self.xr.at[c, 1], dp=p.yn),
        )

    def second(self, c):
        p = self.p
        return (
            p.copy(self.r1a.at[c, 1 - p.y], self.r2.at[c, 0], self.xs.at[c, 2], self.xr.at[c, 2], dp=p.yn),
            p.copy(self.r1b.at[c, 1 - p.x], self.r2.at[c, 1], self.xs.at[c, 3], self.xr.at[c, 3], dp=p.xn),
        )

    def along_z(self, c, dz):
        p = self.p
        return p.copy(self.v.at[c, p.up(dz)], self.r3.at[c, dz - 1], self.zs.at[c, dz - 1], self.zr.at[c, dz - 1],
                      z=p.up(dz))

    def s1(self, c, src, own):
        self.across(c, src).wait_recv()
        for a in range(2):
            for b in range(2):
                self.r0[c, a, b] = (self.r0[c, a, b].astype(F32) + own(a, b).astype(F32)).astype(BF)
        for copy in self.first(c):
            copy.start()

    def s2(self, c):
        p = self.p
        for copy in self.first(c):
            copy.wait_recv()
        for a in range(2):
            self.r1a[c, a] = (self.r1a[c, a].astype(F32) + self.r0[c, a, p.x, :, :384].astype(F32)).astype(BF)
            self.r1b[c, a] = (self.r1b[c, a].astype(F32) + self.r0[c, p.y, a, :, 384:].astype(F32)).astype(BF)
        for copy in self.second(c):
            copy.start()

    def s3(self, c):
        p = self.p
        for copy in self.second(c):
            copy.wait_recv()
        left = self.r1a[c, p.y].astype(F32) + self.r2[c, 0].astype(F32)
        right = self.r1b[c, p.x].astype(F32) + self.r2[c, 1].astype(F32)
        self.v[c] = slab_of(jnp.concatenate([left, right], axis=1).reshape(4, 24, 768))
        for dz in (1, 2, 3):
            self.along_z(c, dz).start()

    def s4(self, c):
        for dz in (1, 2, 3):
            self.along_z(c, dz).wait_recv()
        total = rows_of(self.v[c, self.p.z])
        for dz in range(3):
            total = total + rows_of(self.r3[c, dz])
        self.fin[c] = total

    def sent(self, c, src):
        for copy in (self.across(c, src),) + self.first(c) + self.second(c):
            copy.wait_send()
        for dz in (1, 2, 3):
            self.along_z(c, dz).wait_send()


class SmallScatter:
    def __init__(self, p, src, r0, r1, r2, send, recv):
        self.p, self.src, self.r0, self.r1, self.r2, self.send, self.recv = p, src, r0, r1, r2, send, recv

    def across(self):
        p = self.p
        return p.copy(self.src.at[:, :, 1 - p.k], self.r0, self.send.at[0], self.recv.at[0], dp=p.sib)

    def plane(self):
        p = self.p
        return [p.copy(self.r0.at[y, x], self.r1.at[n], self.send.at[1 + n], self.recv.at[1 + n], dp=dp)
                for n, (dp, y, x) in enumerate(((p.xn, p.y, 1 - p.x), (p.yn, 1 - p.y, p.x), (p.diag, 1 - p.y, 1 - p.x)))]

    def along_z(self, dz):
        p = self.p
        return p.copy(self.r0.at[p.y, p.x, pl.ds(pl.multiple_of(24 * p.up(dz), 8), 24)], self.r2.at[dz - 1],
                      self.send.at[3 + dz], self.recv.at[3 + dz], z=p.up(dz))

    def s0(self):
        self.across().start()

    def s1(self):
        p = self.p
        self.across().wait_recv()
        for a in range(2):
            for b in range(2):
                self.r0[a, b] = self.r0[a, b] + self.src[a, b, p.k]
        for copy in self.plane():
            copy.start()

    def s2(self):
        p = self.p
        for copy in self.plane():
            copy.wait_recv()
        self.r0[p.y, p.x] = self.r0[p.y, p.x] + self.r1[0] + self.r1[1] + self.r1[2]
        for dz in (1, 2, 3):
            self.along_z(dz).start()

    def s3(self):
        p = self.p
        for dz in (1, 2, 3):
            self.along_z(dz).wait_recv()
        own = self.r0[p.y, p.x, pl.ds(pl.multiple_of(24 * p.z, 8), 24), :]
        return own + self.r2[0] + self.r2[1] + self.r2[2]

    def sent(self):
        for copy in [self.across()] + self.plane() + [self.along_z(dz) for dz in (1, 2, 3)]:
            copy.wait_send()


def piece_masks(width, total, count):
    lane = lax.broadcasted_iota(jnp.int32, (1, total), 1)
    inside = lax.rem(lane, width)
    place = lax.broadcasted_iota(jnp.int32, (128, total), 0) == inside
    owner = lax.broadcasted_iota(jnp.int32, (count, total), 0) * width == lane - inside
    return place, owner


def unpack_small(pieces, first, number, width, total):
    place, owner = piece_masks(width, total, 32)
    place = place.astype(BF)
    out = []
    for n in range(number):
        spread = mm(pieces[:, first + n, :].astype(BF), place)
        out.append(jnp.sum(jnp.where(owner, spread, 0.0), axis=0, keepdims=True))
    return out


def pack_small(pieces, first, vectors, width, total):
    place, owner = piece_masks(width, total, 32)
    place = place.astype(BF)
    for n, vector in enumerate(vectors):
        high = vector.astype(BF)
        low = (vector - high.astype(F32)).astype(BF)
        both = jnp.concatenate([jnp.where(owner, high.astype(F32), 0.0), jnp.where(owner, low.astype(F32), 0.0)], axis=0)
        both = mm_nt(both.astype(BF), place)
        pieces[:, first + n, :] = both[:32] + both[32:]


def weight(w, c):
    return w[c].reshape(768, 768)


def lane_block(start):
    return pl.ds(pl.multiple_of(start, 128), 128)


def project_group(g, tok, w, bqkv, conv, qkv, pkv, kvf):
    for r in range(2):
        rows = pl.ds(512 * r, 512)
        low = (mm(tok[rows, :], weight(w, g)) + bqkv[g]).astype(BF)
        qkv[g, rows, :] = low
        for part in range(4):
            kvf[part, pl.ds(8 + 512 * r, 512), :] = low[:, 256 + 128 * part:384 + 128 * part].astype(F32)
    for part in range(4):
        cols = pl.ds(128 * part, 128)
        total = jnp.zeros((256, 128), F32)
        for t in range(5):
            total = total + conv[g, pl.ds(t, 1), cols] * kvf[part, pl.ds(6 + t, 256, stride=4), :]
        pkv[g, :, cols] = total.astype(BF)


def attend_blocks(g, blocks, qkv, pkv, ctx, lse):
    parts = []
    for b in blocks:
        ns, ps, near, far = window(b)
        rows = pl.ds(pl.multiple_of(b * 128, 128), 128)
        for pr in range(2):
            parts.append(dict(
                near=near, far=far, rows=rows, lanes=lane_block(256 * g + 128 * pr), at=(g * 2 + pr) * 8 + b,
                qm=head_split(qkv[g, rows, 128 * pr:128 * pr + 128], 0.125),
                kn=qkv[g, pl.ds(ns, 256), 256 + 128 * pr:384 + 128 * pr],
                kp=pkv[g, pl.ds(ps, 160), 128 * pr:128 * pr + 128],
                vn=qkv[g, pl.ds(ns, 256), 512 + 128 * pr:640 + 128 * pr],
                vp=pkv[g, pl.ds(ps, 160), 256 + 128 * pr:384 + 128 * pr]))
    for t in parts:
        t["sn"] = jnp.where(t["near"], mm_nt(t["kn"], t["qm"]), -1e30)
        t["sp"] = jnp.where(t["far"], mm_nt(t["kp"], t["qm"]), -1e30)
    for t in parts:
        t["peak"] = jnp.maximum(jnp.max(t["sn"], axis=0, keepdims=True), jnp.max(t["sp"], axis=0, keepdims=True))
    for t in parts:
        t["en"] = jnp.exp(t["sn"] - t["peak"])
        t["ep"] = jnp.exp(t["sp"] - t["peak"])
    for t in parts:
        t["total"] = jnp.sum(t["en"], axis=0, keepdims=True) + jnp.sum(t["ep"], axis=0, keepdims=True)
    for t in parts:
        out = mm_tn(t["vn"], t["en"].astype(BF)) + mm_tn(t["vp"], t["ep"].astype(BF))
        t["out"] = head_join(out * pl.reciprocal(t["total"])).T.astype(BF)
    for t in parts:
        ctx[t["rows"], t["lanes"]] = t["out"]
        lse[t["at"]] = t["peak"] + jnp.log(t["total"])


def clear_edges(kvf):
    kvf[:, 0:8, :] = jnp.zeros((4, 8, 128), F32)
    kvf[:, 1032:1040, :] = jnp.zeros((4, 8, 128), F32)


def forward_kernel(comm, *refs):
    if comm:
        (tok, wqkv, bq_own, cv_own, wout, *six, wup, bu_own, wdn, pos, cot,
         out_o, pre_o, tokt_o, firstt_o, acc_o, dbr_o, gp_o, gwd_o, qkv_o, pkv_o, ctx_o, lse_o, gsm, w_o, conv, vec,
         w, buf, act, gp, acc, pre, first, dbr, tr, tokt, ctx, pkv, lse, out, kvf, stage, sems, osem,
         slab, slab_s, dense_s, pieces, bqkv, bup, plane,
         zs, zr, xs, xr, ks, kr, ss, sr, ps0, ps1, ps2, ps3) = refs
    else:
        (tok, w_in, bqkv, conv, vec, bup, pos, cot,
         out_o, pre_o, tokt_o, firstt_o, acc_o, dbr_o, gp_o, gwd_o, qkv_o, pkv_o, ctx_o, lse_o, gsm,
         w, buf, act, gp, acc, pre, first, dbr, tr, tokt, ctx, pkv, lse, out, kvf, stage, sems, osem) = refs
    qkv = buf
    clear_edges(kvf)
    kept, number = [], iter(range(20))

    def keep(src, dst):
        kept.append(pltpu.make_async_copy(src, dst, osem.at[next(number)]))
        kept[-1].start()

    todo = []
    if comm:
        p = Place()
        big = Gather(p, slab, w, (zs, zr, xs, xr, ks, kr))
        tiny = SmallGather(p, slab_s, dense_s, ss, sr)
        turned = PlaneFirst(big, 10, plane, (ps0, ps1, ps2, ps3))
        slab_s[p.z] = jnp.zeros((24, 128), F32)
        slab_s[p.z, 0:1, 0:72] = bq_own[...].astype(F32)
        slab_s[p.z, 1:6, 0:48] = cv_own[...].astype(F32)
        for i in range(6):
            slab_s[p.z, 6 + i:7 + i, 0:24] = six[i][...].astype(F32)
        slab_s[p.z, 12:13, 0:96] = bu_own[...].astype(F32)
        p.greet()
        tiny.s1()
        for c in (0, 10, 1, 2, 3, 4, 5, 6, 7, 8, 9, 11):
            if c < 3:
                rows24 = jnp.concatenate([wqkv[:, 768 * i + 256 * c:768 * i + 256 * c + 256] for i in range(3)], axis=1)
            elif c == 3:
                rows24 = wout[...]
            else:
                rows24 = (wup if c % 2 == 0 else wdn)[:, 768 * ((c - 4) // 2):768 * ((c - 4) // 2) + 768]
            if c == 10:
                turned.s1(slab_of(rows24.astype(F32)))
                continue
            slab[c, p.z] = slab_of(rows24.astype(F32))
            if c < 3:
                big.s1(c)
        tokt[...] = tok[...].T
        tiny.s2()
        big.s1(3)
        big.s2(0)
        big.s1(4)
        big.s2(1)
        tiny.s3()
        big.s3(0)
        big.s1(5)
        big.s2(2)
        big.s3(1)
        big.s1(6)
        big.s2(3)
        big.s4(0)
        tiny.s4()
        pieces[...] = dense_s[...].reshape(32, 24, 128)
        whole = unpack_small(pieces, 0, 1, 72, 2304)[0]
        for g in range(3):
            for i in range(3):
                bqkv[g, :, 256 * i:256 * i + 256] = whole[:, 768 * i + 256 * g:768 * i + 256 * g + 256]
        taps = unpack_small(pieces, 1, 5, 48, 1536)
        for t in range(5):
            for g in range(3):
                for i in range(2):
                    conv[g, t:t + 1, 256 * i:256 * i + 256] = taps[t][:, 768 * i + 256 * g:768 * i + 256 * g + 256]
        rest = unpack_small(pieces, 6, 6, 24, 768)
        for i in range(6):
            vec[i:i + 1, :] = rest[i]
        whole = unpack_small(pieces, 12, 1, 96, 3072)[0]
        for j in range(4):
            bup[j] = whole[:, 768 * j:768 * j + 768]
        big.s5(0)
        todo = [[(big.s2, 8), (big.s3, 6)], [(big.s4, 5), (big.s2, 9)],
                [(big.s3, 7)], [(big.s4, 6), (big.s2, 11)], [(big.s3, 8)], [(big.s4, 7)],
                [(big.s3, 9)], [(big.s4, 8)], [(big.s3, 11)], [(big.s4, 9)],
                [], [(lambda c: turned.s3(), 10)], [(big.s4, 11)]]
    else:
        tokt[...] = tok[...].T
        load = pltpu.make_async_copy(w_in, w, sems.at[0])
        load.start()
        load.wait()

    def progress():
        for step, c in todo.pop(0) if todo else ():
            step(c)

    def group(g, carry):
        if comm:
            @pl.when(g > 0)
            def _():
                big.s5(g)
        project_group(g, tok, w, bqkv, conv, qkv, pkv, kvf)

        def block(b, inner):
            if comm:
                i = 4 * g + b
                n = lax.div(i, 3)

                @pl.when(lax.rem(i, 3) == 0)
                def _():
                    big.s1(7 + n + lax.div(n, 3))
                    big.s2(4 + n)
                    big.s3(2 + n)

                @pl.when(lax.rem(i, 3) == 2)
                def _():
                    big.s4(1 + n)

                @pl.when(i == 10)
                def _():
                    turned.s2()
            attend_blocks(g, (2 * b, 2 * b + 1), qkv, pkv, ctx, lse)
            return inner

        return lax.fori_loop(0, 4, block, carry)

    lax.fori_loop(0, 3, group, 0)
    keep(tokt, tokt_o)
    keep(qkv.at[pl.ds(0, 3)], qkv_o)
    keep(pkv, pkv_o)
    keep(ctx, ctx_o)
    keep(lse, lse_o)
    if comm:
        big.s5(3)
        keep(w.at[pl.ds(0, 4)], w_o.at[pl.ds(0, 4)])
    b_out, gain1, shift1, b_down, gain2, shift2 = [vec[pl.ds(i, 1), :] for i in range(6)]
    tiles = [pl.ds(512 * r, 512) for r in range(2)]
    for rows in tiles:
        pre_one = tok[rows, :].astype(F32) + mm_nt(ctx[rows, :], weight(w, 3)) + b_out
        pre[rows, :] = pre_one
        xhat, rate = norm_stats(pre_one)
        low = (xhat * gain1 + shift1).astype(BF)
        first[rows, :] = low
        acc[rows, :] = low.astype(F32) + b_down
        progress()
    keep(pre, pre_o)
    tr[...] = first[...].T
    keep(tr, firstt_o)
    first_kept = len(kept) - 1
    for j in range(4):
        if comm:
            big.s5(4 + 2 * j)
        for rows in tiles:
            value, slope = gelu_both(mm(first[rows, :], weight(w, 4 + 2 * j)) + bup[j])
            act[j, rows, :] = value.astype(BF)
            gp[j, rows, :] = slope.astype(BF)
            progress()
        if comm:
            big.s5(5 + 2 * j)
            keep(w.at[pl.ds(4 + 2 * j, 2)], w_o.at[pl.ds(4 + 2 * j, 2)])
        for rows in tiles:
            acc[rows, :] += mm_nt(act[j, rows, :], weight(w, 5 + 2 * j))
            progress()
        keep(gp.at[j], gp_o.at[j])
    sums = [jnp.zeros((1, 768), F32) for _ in range(3)]
    for r, rows in enumerate(tiles):
        xhat, rate = norm_stats(acc[rows, :])
        out[rows, :] = (xhat * gain2 + shift2).astype(BF)
        row = 512 * r + lax.broadcasted_iota(jnp.int32, (512, 160), 0)
        dy = mm((row == pos[...]).astype(BF), cot[...])
        sums[1] = sums[1] + colsum(dy * xhat)
        sums[2] = sums[2] + colsum(dy)
        dacc = norm_back(xhat, rate, gain2, dy)
        low = dacc.astype(BF)
        dbr[rows, :] = low
        acc[rows, :] = dacc
        sums[0] = sums[0] + colsum(low.astype(F32))
    gsm[...] = jnp.zeros_like(gsm)
    for i in range(3):
        gsm[2 + i:3 + i, :] = sums[i]
    keep(out, out_o)
    keep(dbr, dbr_o)
    keep(acc, acc_o)
    kept.pop(first_kept).wait()
    tr[...] = dbr[...].T
    sent = []
    for j in range(4):
        if j >= 2:
            sent[j - 2].wait()
        stage[j % 2] = mm(tr[...], act[j]).astype(BF).reshape(2, 2, 2, 96, 768)
        sent.append(pltpu.make_async_copy(stage.at[j % 2], gwd_o.at[j], sems.at[j % 2]))
        sent[j].start()
    sent[2].wait()
    sent[3].wait()
    for copy in kept:
        copy.wait()
    if comm:
        for c in range(12):
            (turned.sent() if c == 10 else big.sent(c))
        tiny.sent()


def forward_call(comm, *args):
    outs = [
        (struct((1024, 768), BF), ANY), (struct((1024, 768), F32), ANY), (struct((768, 1024), BF), ANY),
        (struct((768, 1024), BF), ANY),
        (struct((1024, 768), F32), ANY), (struct((1024, 768), BF), ANY), (struct((4, 1024, 768), BF), ANY),
        (struct((4, 2, 2, 2, 96, 768), BF), ANY), (struct((3, 1024, 768), BF), ANY), (struct((3, 256, 512), BF), ANY),
        (struct((1024, 768), BF), ANY), (struct((48, 1, 256), F32), ANY), (struct((8, 768), F32), VM),
    ]
    scratch = [
        pltpu.VMEM((12, 2, 2, 2, 96, 768), BF), pltpu.VMEM((3, 1024, 768), BF), pltpu.VMEM((4, 1024, 768), BF),
        pltpu.VMEM((4, 1024, 768), BF), pltpu.VMEM((1024, 768), F32), pltpu.VMEM((1024, 768), F32),
        pltpu.VMEM((1024, 768), BF), pltpu.VMEM((1024, 768), BF), pltpu.VMEM((768, 1024), BF), pltpu.VMEM((768, 1024), BF),
        pltpu.VMEM((1024, 768), BF),
        pltpu.VMEM((3, 256, 512), BF), pltpu.VMEM((48, 1, 256), F32), pltpu.VMEM((1024, 768), BF),
        pltpu.VMEM((4, 1040, 128), F32), pltpu.VMEM((2, 2, 2, 2, 96, 768), BF), DMA((2,)), DMA((20,)),
    ]
    if comm:
        outs += [(struct((12, 2, 2, 2, 96, 768), BF), ANY), (struct((3, 8, 512), F32), VM), (struct((8, 768), F32), VM)]
        scratch += [
            pltpu.VMEM((12, 4, 16, 1152), BF), pltpu.VMEM((4, 24, 128), F32), pltpu.VMEM((2, 2, 2, 4, 24, 128), F32),
            pltpu.VMEM((32, 24, 128), F32), pltpu.VMEM((3, 1, 768), F32), pltpu.VMEM((4, 1, 768), F32),
            pltpu.VMEM((4, 4, 16, 1152), BF),
            DMA((12, 3)), DMA((12, 3)), DMA((12, 4)), DMA((12, 4)), DMA((12,)), DMA((12,)), DMA((7,)), DMA((7,)),
            DMA((3,)), DMA((3,)), DMA((3,)), DMA((3,)),
        ]
        params = pltpu.CompilerParams(vmem_limit_bytes=LIMIT, collective_id=1, has_side_effects=True)
    else:
        params = pltpu.CompilerParams(vmem_limit_bytes=LIMIT)
    ins = [VM] * len(args)
    if not comm:
        ins[1] = ANY
    return pl.pallas_call(
        functools.partial(forward_kernel, comm), in_specs=ins, out_specs=[o[1] for o in outs],
        out_shape=[o[0] for o in outs], scratch_shapes=scratch, compiler_params=params, name="forward")(*args)


def qkv_rows(g, start, size):
    return pl.ds(pl.multiple_of(3072 + 1024 * g + start, 32), size)


def back_blocks(g, blocks, wb, pkv, buf, lse, dk, dv, dpk, dpv):
    parts = []
    for b in blocks:
        ns, ps, near, far = window(b)
        first_row = pl.multiple_of(b * 128, 128)
        rows, prow = pl.ds(first_row, 128), pl.ds(ps, 160)
        qrows, krows = qkv_rows(g, first_row, 128), qkv_rows(g, ns, 256)
        for pr in range(2):
            parts.append(dict(
                near=near, far=far, rows=rows, nr=pl.ds(ns, 256), prow=prow, ln=pl.ds(128 * pr, 128),
                qm=head_split(wb[qrows, 128 * pr:128 * pr + 128], 0.125),
                dm=head_split(buf[3, rows, lane_block(256 * g + 128 * pr)], 1.0),
                kn=wb[krows, 256 + 128 * pr:384 + 128 * pr],
                kp=pkv[g, prow, 128 * pr:128 * pr + 128],
                vn=wb[krows, 512 + 128 * pr:640 + 128 * pr],
                vp=pkv[g, prow, 256 + 128 * pr:384 + 128 * pr],
                ls=lse[(g * 2 + pr) * 8 + b]))
    for t in parts:
        t["pn"] = jnp.exp(jnp.where(t["near"], mm_nt(t["kn"], t["qm"]), -1e30) - t["ls"])
        t["pp"] = jnp.exp(jnp.where(t["far"], mm_nt(t["kp"], t["qm"]), -1e30) - t["ls"])
    for t in parts:
        t["dn"] = mm_nt(t["vn"], t["dm"])
        t["dp"] = mm_nt(t["vp"], t["dm"])
        t["gvn"] = mm(t["pn"].astype(BF), t["dm"])
        t["gvp"] = mm(t["pp"].astype(BF), t["dm"])
    for t in parts:
        rd = jnp.sum(t["pn"] * t["dn"], axis=0, keepdims=True) + jnp.sum(t["pp"] * t["dp"], axis=0, keepdims=True)
        t["sn"] = (t["pn"] * (t["dn"] - rd)).astype(BF)
        t["sp"] = (t["pp"] * (t["dp"] - rd)).astype(BF)
    for t in parts:
        t["gkn"] = mm(t["sn"], t["qm"])
        t["gkp"] = mm(t["sp"], t["qm"])
        t["gq"] = (head_join(mm_tn(t["kn"], t["sn"]) + mm_tn(t["kp"], t["sp"])).T * 0.125).astype(BF)
    for t in parts:
        dk[t["nr"], t["ln"]] += t["gkn"]
        dpk[t["prow"], t["ln"]] += t["gkp"]
        dv[t["nr"], t["ln"]] += t["gvn"]
        dpv[t["prow"], t["ln"]] += t["gvp"]
        buf[g, t["rows"], t["ln"]] = t["gq"]


def pool_back(g, conv, wb, kvf, dk, dv, dpk, dpv, buf, gconv):
    for part in range(4):
        kvf[part, 8:1032, :] = wb[qkv_rows(g, 0, 1024), 256 + 128 * part:384 + 128 * part].astype(F32)
    for part in range(4):
        cols = pl.ds(128 * part, 128)
        src, dst = (dpk, dk) if part < 2 else (dpv, dv)
        half = pl.ds(128 * (part % 2), 128)
        dpool = src[:, half]
        for t in range(5):
            gconv[g, pl.ds(t, 1), cols] = colsum(dpool * kvf[part, pl.ds(6 + t, 256, stride=4), :])
        kvf[part, 8:1032, :] = dst[:, half]
        for t in range(5):
            at = pl.ds(6 + t, 256, stride=4)
            kvf[part, at, :] += conv[g, pl.ds(t, 1), cols] * dpool
        buf[g, :, 256 + 128 * part:384 + 128 * part] = kvf[part, 8:1032, :].astype(BF)
        kvf[part, 0:8, :] = jnp.zeros((8, 128), F32)
        kvf[part, 1032:1040, :] = jnp.zeros((8, 128), F32)


BLOCKS = (2, 2, 2, 96, 768)


STEPS = (
    (), ((1, 0),), (), ((1, 1),), (), ((1, 2), (2, 0)), (), ((1, 3), (2, 1)), (), ((1, 4), (2, 2), (3, 0)), (),
    ((1, 5), (2, 3), (3, 1)), (), ((1, 6), (2, 4), (3, 2), (4, 0)), ((4, 1),),
)
LOOP_STEPS = {
    0: ((2, 5), (3, 3)), 1: ((1, 7), (2, 6)), 2: ((3, 4), (4, 2)), 3: ((1, 8), (3, 5), (4, 3)), 4: ((2, 7),), 5: ((3, 6), (4, 4)),
    6: ((1, 9), (2, 8)), 7: ((4, 5),), 8: ((3, 7),), 9: ((1, 10), (2, 9), (4, 6)), 10: ((3, 8), (4, 7)), 11: ((2, 10), (3, 9), (4, 8)),
}


def backward_kernel(comm, *refs):
    (tokt_i, w_i, conv, vec, pre_i, firstt_i, acc_i, dbr_i, gp_i, qkv_i, pkv_i, ctx_i, lse_i, gsm_in) = refs[:14]
    if comm:
        (gwd_i, gtok_o, fin, tot,
         wb, buf, xb, db, tr, acc, gtok, pkv, lse, kvf, isem, osem,
         gat, gconv, gbias, gbout, gsm, gbup, r0, r1a, r1b, r2, v, r3, own, pieces, small, t0, t1, t2,
         ks, kr, xs, xr, zs, zr, ls, ss, sr) = refs[14:]
    else:
        (gtok_o, gat, gconv, gbias, gbout, gsm, gbup,
         wb, buf, xb, db, tr, acc, gtok, pkv, lse, kvf, isem, osem) = refs[14:]
    dk, dv = acc.at[:, pl.ds(0, 256)], acc.at[:, pl.ds(256, 256)]
    dpk, dpv = acc.at[pl.ds(0, 256), pl.ds(512, 256)], acc.at[pl.ds(256, 256), pl.ds(512, 256)]
    loads = {}

    def load(name, src, dst):
        loads[name] = pltpu.make_async_copy(src, dst, isem.at[len(loads)])
        loads[name].start()

    def slot(n):
        return wb[pl.ds(768 * n, 768), :]

    def load_weight(c, n):
        for i in range(8):
            load(("w", c, i), w_i.at[c, i // 4, i // 2 % 2, i % 2], wb.at[pl.ds(768 * n + 96 * i, 96), :])

    def have_weight(c):
        for i in range(8):
            loads["w", c, i].wait()

    load("dbr", dbr_i, db)
    load_weight(5, 1)
    load(("gp", 0), gp_i.at[0], buf.at[0])
    load_weight(4, 0)
    load("acc", acc_i, acc)
    load("first", firstt_i, tr)
    load("tok", tokt_i, xb)
    if comm:
        p = Place()
        big = Scatter(p, r0, r1a, r1b, r2, v, r3, fin, (ks, kr, xs, xr, zs, zr))
        tiny = SmallScatter(p, small, t0, t1, t2, ss, sr)
        p.greet()

        def fetch(c):
            return pltpu.make_async_copy(gwd_i.at[c, :, :, p.k], own.at[c % 2], ls.at[c % 2])

        for c in range(4):
            big.across(c, gwd_i.at[c]).start()
        fetch(0).start()
        fetch(1).start()

        def take(steps):
            for stage, c in steps:
                if stage > 1:
                    (big.s2, big.s3, big.s4)[stage - 2](c)
                elif c >= 4:
                    at = c - 4 if c < 9 else c - 9
                    big.s1(c, gat.at[0], lambda a, b: gat[at, a, b, p.k])
                else:
                    fetch(c).wait()
                    big.s1(c, gat.at[0], lambda a, b: own[c % 2, a, b])
                    if c < 2:
                        fetch(c + 2).start()

    def run(n):
        if comm:
            take(STEPS[n])

    for j in range(1, 4):
        load_weight(5 + 2 * j, 1 + 2 * j)
        load(("gp", j), gp_i.at[j], buf.at[j])
        load_weight(4 + 2 * j, 2 * j)
    load("pre", pre_i, gtok)
    load("pkv", pkv_i, pkv)
    load("lse", lse_i, lse)
    clear_edges(kvf)
    gbup[...] = jnp.zeros_like(gbup)
    gsm[...] = gsm_in[...]
    tiles = [pl.ds(512 * r, 512) for r in range(2)]
    loads["dbr"].wait()
    for j in range(4):
        have_weight(5 + 2 * j)
        loads["gp", j].wait()
        for r, rows in enumerate(tiles):
            low = (mm(db[rows, :], slot(1 + 2 * j)) * buf[j, rows, :].astype(F32)).astype(BF)
            buf[j, rows, :] = low
            gbup[j] += colsum(low.astype(F32))
            if r == 0:
                have_weight(4 + 2 * j)
                if j == 0:
                    loads["acc"].wait()
            acc[rows, :] += mm_nt(low, slot(2 * j))
            run(3 * j + r)
        if j == 0:
            loads["first"].wait()
        gat[j] = mm(tr[...], buf[j]).astype(BF).reshape(BLOCKS)
        if comm:
            big.across(4 + j, gat.at[j]).start()
            run(3 * j + 2)
        if j == 1:
            for c in range(4):
                load_weight(c, c)
    for g in range(3):
        load(("qkv", g), qkv_i.at[g], wb.at[pl.ds(3072 + 1024 * g, 1024), :])
    load("ctx", ctx_i, db)
    loads["pre"].wait()
    gain1 = vec[1:2, :]
    sums = [jnp.zeros((1, 768), F32) for _ in range(3)]
    have_weight(3)
    for rows in tiles:
        xhat, rate = norm_stats(gtok[rows, :])
        dacc = acc[rows, :]
        sums[0] = sums[0] + colsum(dacc * xhat)
        sums[1] = sums[1] + colsum(dacc)
        dpre = norm_back(xhat, rate, gain1, dacc)
        gtok[rows, :] = dpre
        da = dpre.astype(BF)
        sums[2] = sums[2] + colsum(da.astype(F32))
        buf[3, rows, :] = mm(da, slot(3)).astype(BF)
        tr[:, rows] = da.T
    gsm[0:1, :] = sums[0]
    gsm[1:2, :] = sums[1]
    gbout[...] = sums[2]
    if comm:
        run(12)
        pieces[...] = jnp.zeros_like(pieces)
        pack_small(pieces, 6, [gbout[...]] + [gsm[i:i + 1, :] for i in range(5)], 24, 768)
        pack_small(pieces, 12, [jnp.concatenate([gbup[j] for j in range(4)], axis=1)], 96, 3072)
    loads["ctx"].wait()
    gat[4] = mm(tr[...], db[...]).astype(BF).reshape(BLOCKS)
    if comm:
        big.across(8, gat.at[4]).start()
        run(13)
    loads["tok"].wait()
    loads["pkv"].wait()
    loads["lse"].wait()
    for g in range(3):
        loads["qkv", g].wait()
        have_weight(g)
    run(14)

    def group(g, carry):
        acc[...] = jnp.zeros_like(acc)

        def block(b, inner):
            if comm:
                for i, steps in LOOP_STEPS.items():
                    pl.when(4 * g + b == i)(functools.partial(take, steps))
            back_blocks(g, (2 * b, 2 * b + 1), wb, pkv, buf, lse, dk, dv, dpk, dpv)
            return inner

        lax.fori_loop(0, 4, block, 0)
        pool_back(g, conv, wb, kvf, dk, dv, dpk, dpv, buf, gconv)
        if comm:
            big.across(4 + g, gat.at[0]).wait_send()
        gat[g if comm else 5 + g] = mm(xb[...], buf[g]).astype(BF).reshape(BLOCKS)
        if comm:
            big.across(9 + g, gat.at[g]).start()
        gbias[g] = colsum(buf[g].astype(F32))
        return carry

    lax.fori_loop(0, 3, group, 0)
    parts = []

    def token_part(n):
        rows = pl.ds(256 * n, 256)
        total = gtok[rows, :]
        for g in range(3):
            total = total + mm_nt(buf[g, rows, :], slot(g))
        gtok[rows, :] = total
        parts.append(pltpu.make_async_copy(gtok.at[rows, :], gtok_o.at[rows, :], osem.at[n]))
        parts[n].start()

    if not comm:
        for n in range(4):
            token_part(n)
        for copy in parts:
            copy.wait()
        return

    take(((1, 11),))
    kinds = [jnp.concatenate([gbias[g][:, 256 * i:256 * i + 256] for i in range(3) for g in range(3)], axis=1)]
    pack_small(pieces, 0, kinds, 72, 2304)
    pack_small(pieces, 1, [
        jnp.concatenate([gconv[g, t:t + 1, 256 * i:256 * i + 256] for i in range(2) for g in range(3)], axis=1)
        for t in range(5)], 48, 1536)
    small[...] = pieces[...].reshape(2, 2, 2, 96, 128)
    tiny.s0()
    take(((3, 10),))
    token_part(0)
    tiny.s1()
    take(((2, 11),))
    token_part(1)
    tiny.s2()
    take(((4, 9), (3, 11)))
    token_part(2)
    take(((4, 10),))
    token_part(3)
    tot[...] = tiny.s3()
    take(((4, 11),))
    for c in range(12):
        for copy in big.first(c) + big.second(c) + tuple(big.along_z(c, dz) for dz in (1, 2, 3)):
            copy.wait_send()
        if c not in (4, 5, 6):
            big.across(c, gat.at[0]).wait_send()
    tiny.sent()
    for copy in parts:
        copy.wait()


def backward_call(comm, *args):
    scratch = [
        pltpu.VMEM((6144, 768), BF), pltpu.VMEM((4, 1024, 768), BF), pltpu.VMEM((768, 1024), BF), pltpu.VMEM((1024, 768), BF),
        pltpu.VMEM((768, 1024), BF), pltpu.VMEM((1024, 768), F32), pltpu.VMEM((1024, 768), F32),
        pltpu.VMEM((3, 256, 512), BF), pltpu.VMEM((48, 1, 256), F32),
        pltpu.VMEM((4, 1040, 128), F32), DMA((120,)), DMA((4,)),
    ]
    ins = [ANY] * len(args)
    for i in (2, 3, 13):
        ins[i] = VM
    local = [((5 if comm else 8,) + BLOCKS, BF), ((3, 8, 512), F32), ((3, 1, 768), F32), ((1, 768), F32), ((8, 768), F32), ((4, 1, 768), F32)]
    outs = [(struct((1024, 768), F32), ANY)]
    if comm:
        outs += [(struct((12, 24, 768), F32), VM), (struct((24, 128), F32), VM)]
        scratch += [pltpu.VMEM(*s) for s in local]
        scratch += [
            pltpu.VMEM((12, 2, 2, 96, 768), BF), pltpu.VMEM((12, 2, 96, 384), BF), pltpu.VMEM((12, 2, 96, 384), BF),
            pltpu.VMEM((12, 2, 96, 384), BF), pltpu.VMEM((12, 4, 16, 1152), BF), pltpu.VMEM((12, 3, 16, 1152), BF),
            pltpu.VMEM((2, 2, 2, 96, 768), BF), pltpu.VMEM((32, 24, 128), F32),
            pltpu.VMEM((2, 2, 2, 96, 128), F32), pltpu.VMEM((2, 2, 96, 128), F32), pltpu.VMEM((3, 96, 128), F32),
            pltpu.VMEM((3, 24, 128), F32),
            DMA((12,)), DMA((12,)), DMA((12, 4)), DMA((12, 4)), DMA((12, 3)), DMA((12, 3)), DMA((2,)), DMA((7,)), DMA((7,)),
        ]
        params = pltpu.CompilerParams(vmem_limit_bytes=LIMIT, collective_id=2, has_side_effects=True)
    else:
        outs += [(struct(*s), VM) for s in local]
        params = pltpu.CompilerParams(vmem_limit_bytes=LIMIT)
    return pl.pallas_call(
        functools.partial(backward_kernel, comm), in_specs=ins, out_specs=[o[1] for o in outs], out_shape=[o[0] for o in outs],
        scratch_shapes=scratch, compiler_params=params, name="backward")(*args)


def finish_kernel(out_i, gtok_i, fin, tot, out, gtok, gqkv, gqb, gcv, gwo, gbo, gg1, gs1, gwu, gbu, gwd, gbd, gg2, gs2):
    out[...] = out_i[...]
    gtok[...] = gtok_i[...]

    @pl.when(pl.program_id(0) == 0)
    def _():
        for j in range(4):
            gwd[:, 768 * j:768 * j + 768] = fin[j]
            gwu[:, 768 * j:768 * j + 768] = fin[4 + j]
        gwo[...] = fin[8]
        for g in range(3):
            for i in range(3):
                gqkv[:, 768 * i + 256 * g:768 * i + 256 * g + 256] = fin[9 + g, :, 256 * i:256 * i + 256]
        gqb[...] = tot[0:1, 0:72]
        gcv[...] = tot[1:6, 0:48]
        for i, ref in enumerate((gbo, gg1, gs1, gbd, gg2, gs2)):
            ref[...] = tot[6 + i:7 + i, 0:24]
        gbu[...] = tot[12:13, 0:96]


def finish_call(*args):
    shapes = ((24, 2304), (1, 72), (5, 48), (24, 768), (1, 24), (1, 24), (1, 24), (24, 3072), (1, 96),
              (24, 3072), (1, 24), (1, 24), (1, 24))
    part = pl.BlockSpec((512, 768), lambda n: (n, 0))

    def full(shape):
        return pl.BlockSpec(shape, lambda n: (0,) * len(shape))

    return pl.pallas_call(
        finish_kernel, grid=(2,), in_specs=[part, part, full((12, 24, 768)), full((24, 128))],
        out_specs=[part, part] + [full(s) for s in shapes],
        out_shape=[struct((1024, 768), BF), struct((1024, 768), F32)] + [struct(s, F32) for s in shapes],
        name="finish")(*args)


def shards_direct(tokens, w_qkv, b_qkv, conv_kv, w_out, b_out, gain_one, shift_one, w_up, b_up, w_down, b_down, gain_two,
                  shift_two, positions, cotangent):
    tok = tokens[0]
    out, pre, tokt, firstt, acc, dbr, gp, gwd, qkv, pkv, ctx, lse, gsm, w, conv, vec = forward_call(
        True, tok, w_qkv, b_qkv[None], conv_kv, w_out.T, b_out[None], gain_one[None], shift_one[None], b_down[None],
        gain_two[None], shift_two[None], w_up, b_up[None], w_down.T, positions, cotangent[0])
    gtok, fin, tot = backward_call(True, tokt, w, conv, vec, pre, firstt, acc, dbr, gp, qkv, pkv, ctx, lse, gsm, gwd)
    (out, gtok, gqkv, gqb, gcv, gwo, gbo, gg1, gs1, gwu, gbu, gwd, gbd, gg2, gs2) = finish_call(out, gtok, fin, tot)
    return (out[None], gtok[None], gqkv, gqb[0], gcv, gwo.T, gbo[0], gg1[0], gs1[0], gwu, gbu[0], gwd.T, gbd[0], gg2[0], gs2[0])


def small_sizes(count):
    return [2304 // count] + [1536 // count] * 5 + [768 // count] * 6 + [3072 // count]


def by_group(v, kinds):
    return v.reshape(kinds, 3, 256).transpose(1, 0, 2).reshape(3, 1, kinds * 256)


def shards_general(tokens, w_qkv, b_qkv, conv_kv, w_out, b_out, gain_one, shift_one, w_up, b_up, w_down, b_down, gain_two,
                   shift_two, positions, cotangent):
    rows = w_qkv.shape[0]
    count = 768 // rows
    blocks = (2, 2, 2, 96, 768)
    up = w_up.reshape(rows, 4, 768).transpose(1, 0, 2)
    down = w_down.reshape(4, 768, rows).transpose(0, 2, 1)
    own = jnp.concatenate([
        w_qkv.reshape(rows, 3, 3, 256).transpose(2, 0, 1, 3).reshape(3, rows, 768),
        w_out.T[None],
        jnp.stack([up, down], 1).reshape(8, rows, 768),
    ], 0)
    w = lax.all_gather(own, AXES, axis=1, tiled=True).reshape((12,) + blocks)
    small = jnp.concatenate([b_qkv, conv_kv.reshape(-1), b_out, gain_one, shift_one, b_down, gain_two, shift_two, b_up])
    small = lax.all_gather(small[None], AXES, axis=0, tiled=True).astype(F32)
    at, parts = 0, []
    for size in small_sizes(count):
        parts.append(small[:, at:at + size].reshape(-1))
        at += size
    bqkv = by_group(parts[0], 3)
    conv = jnp.concatenate([by_group(p, 2) for p in parts[1:6]] + [jnp.zeros((3, 3, 512), F32)], 1)
    vec = jnp.stack(parts[6:12] + [jnp.zeros((768,), F32)] * 2)
    bup = parts[12].reshape(4, 1, 768)
    out, pre, tokt, firstt, acc, dbr, gp, gwd, qkv, pkv, ctx, lse, gsm = forward_call(
        False, tokens[0], w, bqkv, conv, vec, bup, positions, cotangent[0])
    gwd = lax.psum_scatter(gwd.reshape(4, 768, 768), AXES, scatter_dimension=1, tiled=True).astype(F32)
    gtok, gat, gconv, gbias, gbout, gsm, gbup = backward_call(
        False, tokt, w, conv, vec, pre, firstt, acc, dbr, gp, qkv, pkv, ctx, lse, gsm)
    gat = lax.psum_scatter(gat.reshape(8, 768, 768), AXES, scatter_dimension=1, tiled=True).astype(F32)
    flat = [gbias.reshape(3, 3, 256).transpose(1, 0, 2).reshape(count, -1)]
    flat += [gconv[:, t].reshape(3, 2, 256).transpose(1, 0, 2).reshape(count, -1) for t in range(5)]
    flat += [gbout[0].reshape(count, -1)] + [gsm[i].reshape(count, -1) for i in range(5)] + [gbup.reshape(count, -1)]
    flat = lax.psum_scatter(jnp.concatenate(flat, 1), AXES, scatter_dimension=0, tiled=True)
    at, s = 0, []
    for size in small_sizes(count):
        s.append(flat[0, at:at + size])
        at += size
    return (
        out[None], gtok[None],
        gat[5:].reshape(3, rows, 3, 256).transpose(1, 2, 0, 3).reshape(rows, 2304),
        s[0], jnp.stack(s[1:6]), gat[4].T, s[6], s[7], s[8],
        gat[:4].transpose(1, 0, 2).reshape(rows, 3072), s[12],
        gwd.transpose(0, 2, 1).reshape(3072, rows), s[9], s[10], s[11],
    )


def solution(mesh):
    rows, cols, flat, item = P(AXES, None), P(None, AXES), P(AXES), P(AXES, None, None)
    direct = mesh.shape["dp"] == 8 and mesh.shape["fsdp"] == 4
    return jax.shard_map(
        shards_direct if direct else shards_general,
        mesh=mesh,
        in_specs=(item, rows, flat, cols, cols, flat, flat, flat, rows, flat, cols, flat, flat, flat, rows, item),
        out_specs=(item, item, rows, flat, cols, cols, flat, flat, flat, rows, flat, cols, flat, flat, flat),
        check_vma=False,
    )
```

```python
import functools
import jax
import jax.numpy as jnp
from jax import lax
from jax.experimental import pallas as pl
from jax.experimental.pallas import tpu as pltpu
from jax.sharding import PartitionSpec as P

F32 = jnp.float32
BF = jnp.bfloat16
EPS = 1e-5
NT = (((1,), (1,)), ((), ()))
TN = (((0,), (0,)), ((), ()))
AXES = ("dp", "fsdp")
VM = pl.BlockSpec(memory_space=pltpu.VMEM)
ANY = pl.BlockSpec(memory_space=pl.ANY)
LIMIT = 64 * 1024 * 1024 - 512 * 1024
DMA = pltpu.SemaphoreType.DMA
struct = jax.ShapeDtypeStruct


def mm(a, b):
    return jnp.dot(a, b, preferred_element_type=F32)


def mm_nt(a, b):
    return lax.dot_general(a, b, NT, preferred_element_type=F32)


def mm_tn(a, b):
    return lax.dot_general(a, b, TN, preferred_element_type=F32)


def norm_stats(values):
    average = jnp.mean(values, axis=-1, keepdims=True)
    centred = values - average
    variance = jnp.mean(centred * centred, axis=-1, keepdims=True)
    rate = lax.rsqrt(variance + EPS)
    return centred * rate, rate


def norm_back(xhat, rate, gain, dy):
    e = dy * gain
    mean_e = jnp.mean(e, axis=-1, keepdims=True)
    mean_ex = jnp.mean(e * xhat, axis=-1, keepdims=True)
    return rate * (e - mean_e - xhat * mean_ex)


def colsum(v):
    return jnp.sum(v, axis=0, keepdims=True)


def gelu_both(u):
    c = 0.7978845608028654
    u2 = u * u
    t = jnp.tanh(u * (c + (c * 0.044715) * u2))
    half = 0.5 + 0.5 * t
    value = u * half
    slope = half + (0.5 * u) * (1.0 - t * t) * (c + (3.0 * c * 0.044715) * u2)
    return value, slope


def head_split(x, scale):
    lane = lax.broadcasted_iota(jnp.int32, x.shape, 1)
    low = jnp.where(lane < 64, scale, 0.0).astype(BF)
    high = jnp.where(lane < 64, 0.0, scale).astype(BF)
    return jnp.concatenate([x * low, x * high], axis=0)


def head_join(r):
    return jnp.concatenate([r[:64, :128], r[64:, 128:]], axis=0)


def window(b):
    ns = pl.multiple_of(jnp.clip(b * 128 - 64, 0, 1024 - 256), 64)
    ps = pl.multiple_of(jnp.clip(b * 32 - 64, 0, 256 - 160), 32)
    col = b * 128 + (lax.broadcasted_iota(jnp.int32, (256, 256), 1) & 127)
    row = ns + lax.broadcasted_iota(jnp.int32, (256, 256), 0)
    near = jnp.abs(row - col) <= 64
    colp = b * 128 + (lax.broadcasted_iota(jnp.int32, (160, 256), 1) & 127)
    rowp = 4 * (ps + lax.broadcasted_iota(jnp.int32, (160, 256), 0))
    far = jnp.abs(rowp - colp) <= 256
    return ns, ps, near, far


class Place:
    def __init__(self):
        d = lax.axis_index("dp")
        self.d, self.z = d, lax.axis_index("fsdp")
        self.k, self.x, self.y = lax.rem(d, 2), lax.rem(lax.div(d, 2), 2), lax.div(d, 4)
        self.sib = d + 1 - 2 * self.k
        self.xn = d + 2 - 4 * self.x
        self.yn = d + 4 - 8 * self.y
        self.diag = self.xn + 4 - 8 * self.y

    def up(self, dz):
        return lax.rem(self.z + dz, 4)

    def copy(self, src, dst, send, recv, dp=None, z=None):
        return pltpu.make_async_remote_copy(
            src_ref=src, dst_ref=dst, send_sem=send, recv_sem=recv,
            device_id={"dp": self.d if dp is None else dp, "fsdp": self.z if z is None else z},
            device_id_type=pl.DeviceIdType.MESH)

    def greet(self):
        barrier = pltpu.get_barrier_semaphore()
        for dp in (self.sib, self.xn, self.yn, self.diag):
            pl.semaphore_signal(barrier, inc=1, device_id={"dp": dp, "fsdp": self.z},
                                device_id_type=pl.DeviceIdType.MESH)
        for dz in (1, 2, 3):
            pl.semaphore_signal(barrier, inc=1, device_id={"dp": self.d, "fsdp": self.up(dz)},
                                device_id_type=pl.DeviceIdType.MESH)
        pl.semaphore_wait(barrier, 7)


def slab_of(rows):
    last = jnp.concatenate([rows[..., 16:, :384], rows[..., 16:, 384:]], axis=-2)
    return jnp.concatenate([rows[..., :16, :], last], axis=-1).astype(BF)


def rows_of(slab):
    v = slab.astype(F32)
    last = jnp.concatenate([v[..., :8, 768:], v[..., 8:, 768:]], axis=-1)
    return jnp.concatenate([v[..., :768], last], axis=-2)


class Gather:
    def __init__(self, p, slab, dense, sems):
        self.p, self.slab, self.dense = p, slab, dense
        self.zs, self.zr, self.xs, self.xr, self.ks, self.kr = sems

    def along_z(self, c, dz, arriving=False):
        p = self.p
        slot = p.up(4 - dz) if arriving else p.z
        return p.copy(self.slab.at[c, p.z], self.slab.at[c, slot], self.zs.at[c, dz - 1], self.zr.at[c, dz - 1],
                      z=p.up(dz))

    def first(self, c, arriving=False):
        p, w = self.p, self.dense
        ya = 1 - p.y if arriving else p.y
        xa = 1 - p.x if arriving else p.x
        a, b = pl.ds(0, 384), pl.ds(384, 384)
        return (
            p.copy(w.at[c, p.y, p.x, p.k, :, a], w.at[c, p.y, xa, p.k, :, a], self.xs.at[c, 0], self.xr.at[c, 0], dp=p.xn),
            p.copy(w.at[c, p.y, p.x, p.k, :, b], w.at[c, ya, p.x, p.k, :, b], self.xs.at[c, 1], self.xr.at[c, 1], dp=p.yn),
        )

    def second(self, c, arriving=False):
        p, w = self.p, self.dense
        ya = 1 - p.y if arriving else p.y
        xa = 1 - p.x if arriving else p.x
        a, b = pl.ds(0, 384), pl.ds(384, 384)
        return (
            p.copy(w.at[c, p.y, :, p.k, :, a], w.at[c, ya, :, p.k, :, a], self.xs.at[c, 2], self.xr.at[c, 2], dp=p.yn),
            p.copy(w.at[c, :, p.x, p.k, :, b], w.at[c, :, xa, p.k, :, b], self.xs.at[c, 3], self.xr.at[c, 3], dp=p.xn),
        )

    def across(self, c, arriving=False):
        p, w = self.p, self.dense
        k = 1 - p.k if arriving else p.k
        return p.copy(w.at[c, :, :, p.k], w.at[c, :, :, k], self.ks.at[c], self.kr.at[c], dp=p.sib)

    def s1(self, c):
        for dz in (1, 2, 3):
            self.along_z(c, dz).start()

    def s2(self, c):
        p = self.p
        for dz in (1, 2, 3):
            self.along_z(c, dz, True).wait_recv()
        self.dense[c, p.y, p.x, p.k] = rows_of(self.slab[c]).reshape(96, 768).astype(BF)
        for copy in self.first(c):
            copy.start()

    def s3(self, c):
        for copy in self.first(c, True):
            copy.wait_recv()
        for copy in self.second(c):
            copy.start()

    def s4(self, c):
        for copy in self.second(c, True):
            copy.wait_recv()
        self.across(c).start()

    def s5(self, c):
        self.across(c, True).wait_recv()

    def sent(self, c):
        for dz in (1, 2, 3):
            self.along_z(c, dz).wait_send()
        for copy in self.first(c) + self.second(c) + (self.across(c),):
            copy.wait_send()


class PlaneFirst:
    def __init__(self, gather, c, group, sems):
        self.g, self.p, self.c, self.group = gather, gather.p, c, group
        self.ps, self.pr, self.zs, self.zr = sems

    def plane(self, arriving=False):
        p, me, out = self.p, 2 * self.p.y + self.p.x, []
        for n, (dp, other) in enumerate(((p.xn, me + 1 - 2 * p.x), (p.yn, me + 2 - 4 * p.y), (p.diag, 3 - me))):
            out.append(p.copy(self.group.at[p.z, me], self.group.at[p.z, other if arriving else me], self.ps.at[n], self.pr.at[n],
                              dp=dp))
        return out

    def along_z(self, arriving=False):
        p = self.p
        return [p.copy(self.group.at[p.z], self.group.at[p.up(4 - dz) if arriving else p.z], self.zs.at[dz - 1],
                       self.zr.at[dz - 1], z=p.up(dz)) for dz in (1, 2, 3)]

    def s1(self, slab):
        self.group[self.p.z, 2 * self.p.y + self.p.x] = slab
        for copy in self.plane():
            copy.start()

    def s2(self):
        for copy in self.plane(True):
            copy.wait_recv()
        for copy in self.along_z():
            copy.start()

    def s3(self):
        for copy in self.along_z(True):
            copy.wait_recv()
        for n in range(4):
            self.g.dense[self.c, n // 2, n % 2, self.p.k] = rows_of(self.group[:, n]).reshape(96, 768).astype(BF)
        self.g.across(self.c).start()

    def sent(self):
        for copy in self.plane() + self.along_z() + [self.g.across(self.c)]:
            copy.wait_send()


class SmallGather:
    def __init__(self, p, slab, dense, send, recv):
        self.p, self.slab, self.dense, self.send, self.recv = p, slab, dense, send, recv

    def along_z(self, dz, arriving=False):
        p = self.p
        slot = p.up(4 - dz) if arriving else p.z
        return p.copy(self.slab.at[p.z], self.slab.at[slot], self.send.at[dz - 1], self.recv.at[dz - 1], z=p.up(dz))

    def plane(self, arriving=False):
        p, w = self.p, self.dense
        out = []
        for n, (dp, y, x) in enumerate(((p.xn, p.y, 1 - p.x), (p.yn, 1 - p.y, p.x), (p.diag, 1 - p.y, 1 - p.x))):
            dst = w.at[y, x, p.k] if arriving else w.at[p.y, p.x, p.k]
            out.append(p.copy(w.at[p.y, p.x, p.k], dst, self.send.at[3 + n], self.recv.at[3 + n], dp=dp))
        return out

    def across(self, arriving=False):
        p, w = self.p, self.dense
        k = 1 - p.k if arriving else p.k
        return p.copy(w.at[:, :, p.k], w.at[:, :, k], self.send.at[6], self.recv.at[6], dp=p.sib)

    def s1(self):
        for dz in (1, 2, 3):
            self.along_z(dz).start()

    def s2(self):
        p = self.p
        for dz in (1, 2, 3):
            self.along_z(dz, True).wait_recv()
        self.dense[p.y, p.x, p.k] = self.slab[...]
        for copy in self.plane():
            copy.start()

    def s3(self):
        for copy in self.plane(True):
            copy.wait_recv()
        self.across().start()

    def s4(self):
        self.across(True).wait_recv()

    def sent(self):
        for dz in (1, 2, 3):
            self.along_z(dz).wait_send()
        for copy in self.plane() + [self.across()]:
            copy.wait_send()


class Scatter:
    def __init__(self, p, r0, r1a, r1b, r2, v, r3, fin, sems):
        self.p, self.r0, self.r1a, self.r1b, self.r2, self.v, self.r3, self.fin = p, r0, r1a, r1b, r2, v, r3, fin
        self.ks, self.kr, self.xs, self.xr, self.zs, self.zr = sems

    def across(self, c, src):
        p = self.p
        return p.copy(src.at[:, :, 1 - p.k], self.r0.at[c], self.ks.at[c], self.kr.at[c], dp=p.sib)

    def first(self, c):
        p, r = self.p, self.r0
        return (
            p.copy(r.at[c, :, 1 - p.x, :, pl.ds(0, 384)], self.r1a.at[c], self.xs.at[c, 0], self.xr.at[c, 0], dp=p.xn),
            p.copy(r.at[c, 1 - p.y, :, :, pl.ds(384, 384)], self.r1b.at[c], self.xs.at[c, 1], self.xr.at[c, 1], dp=p.yn),
        )

    def second(self, c):
        p = self.p
        return (
            p.copy(self.r1a.at[c, 1 - p.y], self.r2.at[c, 0], self.xs.at[c, 2], self.xr.at[c, 2], dp=p.yn),
            p.copy(self.r1b.at[c, 1 - p.x], self.r2.at[c, 1], self.xs.at[c, 3], self.xr.at[c, 3], dp=p.xn),
        )

    def along_z(self, c, dz):
        p = self.p
        return p.copy(self.v.at[c, p.up(dz)], self.r3.at[c, dz - 1], self.zs.at[c, dz - 1], self.zr.at[c, dz - 1],
                      z=p.up(dz))

    def s1(self, c, src, own):
        self.across(c, src).wait_recv()
        for a in range(2):
            for b in range(2):
                self.r0[c, a, b] = (self.r0[c, a, b].astype(F32) + own(a, b).astype(F32)).astype(BF)
        for copy in self.first(c):
            copy.start()

    def s2(self, c):
        p = self.p
        for copy in self.first(c):
            copy.wait_recv()
        for a in range(2):
            self.r1a[c, a] = (self.r1a[c, a].astype(F32) + self.r0[c, a, p.x, :, :384].astype(F32)).astype(BF)
            self.r1b[c, a] = (self.r1b[c, a].astype(F32) + self.r0[c, p.y, a, :, 384:].astype(F32)).astype(BF)
        for copy in self.second(c):
            copy.start()

    def s3(self, c):
        p = self.p
        for copy in self.second(c):
            copy.wait_recv()
        left = self.r1a[c, p.y].astype(F32) + self.r2[c, 0].astype(F32)
        right = self.r1b[c, p.x].astype(F32) + self.r2[c, 1].astype(F32)
        self.v[c] = slab_of(jnp.concatenate([left, right], axis=1).reshape(4, 24, 768))
        for dz in (1, 2, 3):
            self.along_z(c, dz).start()

    def s4(self, c):
        for dz in (1, 2, 3):
            self.along_z(c, dz).wait_recv()
        total = rows_of(self.v[c, self.p.z])
        for dz in range(3):
            total = total + rows_of(self.r3[c, dz])
        self.fin[c] = total

    def sent(self, c, src):
        for copy in (self.across(c, src),) + self.first(c) + self.second(c):
            copy.wait_send()
        for dz in (1, 2, 3):
            self.along_z(c, dz).wait_send()


class SmallScatter:
    def __init__(self, p, src, r0, r1, r2, send, recv):
        self.p, self.src, self.r0, self.r1, self.r2, self.send, self.recv = p, src, r0, r1, r2, send, recv

    def across(self):
        p = self.p
        return p.copy(self.src.at[:, :, 1 - p.k], self.r0, self.send.at[0], self.recv.at[0], dp=p.sib)

    def plane(self):
        p = self.p
        return [p.copy(self.r0.at[y, x], self.r1.at[n], self.send.at[1 + n], self.recv.at[1 + n], dp=dp)
                for n, (dp, y, x) in enumerate(((p.xn, p.y, 1 - p.x), (p.yn, 1 - p.y, p.x), (p.diag, 1 - p.y, 1 - p.x)))]

    def along_z(self, dz):
        p = self.p
        return p.copy(self.r0.at[p.y, p.x, pl.ds(pl.multiple_of(24 * p.up(dz), 8), 24)], self.r2.at[dz - 1],
                      self.send.at[3 + dz], self.recv.at[3 + dz], z=p.up(dz))

    def s0(self):
        self.across().start()

    def s1(self):
        p = self.p
        self.across().wait_recv()
        for a in range(2):
            for b in range(2):
                self.r0[a, b] = self.r0[a, b] + self.src[a, b, p.k]
        for copy in self.plane():
            copy.start()

    def s2(self):
        p = self.p
        for copy in self.plane():
            copy.wait_recv()
        self.r0[p.y, p.x] = self.r0[p.y, p.x] + self.r1[0] + self.r1[1] + self.r1[2]
        for dz in (1, 2, 3):
            self.along_z(dz).start()

    def s3(self):
        p = self.p
        for dz in (1, 2, 3):
            self.along_z(dz).wait_recv()
        own = self.r0[p.y, p.x, pl.ds(pl.multiple_of(24 * p.z, 8), 24), :]
        return own + self.r2[0] + self.r2[1] + self.r2[2]

    def sent(self):
        for copy in [self.across()] + self.plane() + [self.along_z(dz) for dz in (1, 2, 3)]:
            copy.wait_send()


def piece_masks(width, total, count):
    lane = lax.broadcasted_iota(jnp.int32, (1, total), 1)
    inside = lax.rem(lane, width)
    place = lax.broadcasted_iota(jnp.int32, (128, total), 0) == inside
    owner = lax.broadcasted_iota(jnp.int32, (count, total), 0) * width == lane - inside
    return place, owner


def unpack_small(pieces, first, number, width, total):
    place, owner = piece_masks(width, total, 32)
    place = place.astype(BF)
    out = []
    for n in range(number):
        spread = mm(pieces[:, first + n, :].astype(BF), place)
        out.append(jnp.sum(jnp.where(owner, spread, 0.0), axis=0, keepdims=True))
    return out


def pack_small(pieces, first, vectors, width, total):
    place, owner = piece_masks(width, total, 32)
    place = place.astype(BF)
    for n, vector in enumerate(vectors):
        high = vector.astype(BF)
        low = (vector - high.astype(F32)).astype(BF)
        both = jnp.concatenate([jnp.where(owner, high.astype(F32), 0.0), jnp.where(owner, low.astype(F32), 0.0)], axis=0)
        both = mm_nt(both.astype(BF), place)
        pieces[:, first + n, :] = both[:32] + both[32:]


def weight(w, c):
    return w[c].reshape(768, 768)


def lane_block(start):
    return pl.ds(pl.multiple_of(start, 128), 128)


def project_group(g, tok, w, bqkv, conv, qkv, pkv, kvf):
    for r in range(2):
        rows = pl.ds(512 * r, 512)
        low = (mm(tok[rows, :], weight(w, g)) + bqkv[g]).astype(BF)
        qkv[g, rows, :] = low
        for part in range(4):
            kvf[part, pl.ds(8 + 512 * r, 512), :] = low[:, 256 + 128 * part:384 + 128 * part].astype(F32)
    for part in range(4):
        cols = pl.ds(128 * part, 128)
        total = jnp.zeros((256, 128), F32)
        for t in range(5):
            total = total + conv[g, pl.ds(t, 1), cols] * kvf[part, pl.ds(6 + t, 256, stride=4), :]
        pkv[g, :, cols] = total.astype(BF)


def attend_blocks(g, blocks, qkv, pkv, ctx, lse):
    parts = []
    for b in blocks:
        ns, ps, near, far = window(b)
        rows = pl.ds(pl.multiple_of(b * 128, 128), 128)
        for pr in range(2):
            parts.append(dict(
                near=near, far=far, rows=rows, lanes=lane_block(256 * g + 128 * pr), at=(g * 2 + pr) * 8 + b,
                qm=head_split(qkv[g, rows, 128 * pr:128 * pr + 128], 0.125),
                kn=qkv[g, pl.ds(ns, 256), 256 + 128 * pr:384 + 128 * pr],
                kp=pkv[g, pl.ds(ps, 160), 128 * pr:128 * pr + 128],
                vn=qkv[g, pl.ds(ns, 256), 512 + 128 * pr:640 + 128 * pr],
                vp=pkv[g, pl.ds(ps, 160), 256 + 128 * pr:384 + 128 * pr]))
    for t in parts:
        t["sn"] = jnp.where(t["near"], mm_nt(t["kn"], t["qm"]), -1e30)
        t["sp"] = jnp.where(t["far"], mm_nt(t["kp"], t["qm"]), -1e30)
    for t in parts:
        t["peak"] = jnp.maximum(jnp.max(t["sn"], axis=0, keepdims=True), jnp.max(t["sp"], axis=0, keepdims=True))
    for t in parts:
        t["en"] = jnp.exp(t["sn"] - t["peak"])
        t["ep"] = jnp.exp(t["sp"] - t["peak"])
    for t in parts:
        t["total"] = jnp.sum(t["en"], axis=0, keepdims=True) + jnp.sum(t["ep"], axis=0, keepdims=True)
    for t in parts:
        out = mm_tn(t["vn"], t["en"].astype(BF)) + mm_tn(t["vp"], t["ep"].astype(BF))
        t["out"] = head_join(out * pl.reciprocal(t["total"])).T.astype(BF)
    for t in parts:
        ctx[t["rows"], t["lanes"]] = t["out"]
        lse[t["at"]] = t["peak"] + jnp.log(t["total"])


def clear_edges(kvf):
    kvf[:, 0:8, :] = jnp.zeros((4, 8, 128), F32)
    kvf[:, 1032:1040, :] = jnp.zeros((4, 8, 128), F32)


def forward_kernel(comm, *refs):
    if comm:
        (tok, wqkv, bq_own, cv_own, wout, *six, wup, bu_own, wdn, pos, cot,
         out_o, pre_o, tokt_o, firstt_o, acc_o, dbr_o, gp_o, gwd_o, qkv_o, pkv_o, ctx_o, lse_o, gsm, w_o, conv, vec,
         w, buf, act, gp, acc, pre, first, dbr, tr, tokt, ctx, pkv, lse, out, kvf, stage, sems, osem,
         slab, slab_s, dense_s, pieces, bqkv, bup, plane,
         zs, zr, xs, xr, ks, kr, ss, sr, ps0, ps1, ps2, ps3) = refs
    else:
        (tok, w_in, bqkv, conv, vec, bup, pos, cot,
         out_o, pre_o, tokt_o, firstt_o, acc_o, dbr_o, gp_o, gwd_o, qkv_o, pkv_o, ctx_o, lse_o, gsm,
         w, buf, act, gp, acc, pre, first, dbr, tr, tokt, ctx, pkv, lse, out, kvf, stage, sems, osem) = refs
    qkv = buf
    clear_edges(kvf)
    kept, number = [], iter(range(20))

    def keep(src, dst):
        kept.append(pltpu.make_async_copy(src, dst, osem.at[next(number)]))
        kept[-1].start()

    todo = []
    if comm:
        p = Place()
        big = Gather(p, slab, w, (zs, zr, xs, xr, ks, kr))
        tiny = SmallGather(p, slab_s, dense_s, ss, sr)
        turned = PlaneFirst(big, 10, plane, (ps0, ps1, ps2, ps3))
        slab_s[p.z] = jnp.zeros((24, 128), F32)
        slab_s[p.z, 0:1, 0:72] = bq_own[...].astype(F32)
        slab_s[p.z, 1:6, 0:48] = cv_own[...].astype(F32)
        for i in range(6):
            slab_s[p.z, 6 + i:7 + i, 0:24] = six[i][...].astype(F32)
        slab_s[p.z, 12:13, 0:96] = bu_own[...].astype(F32)
        p.greet()
        tiny.s1()
        for c in (0, 10, 1, 2, 3, 4, 5, 6, 7, 8, 9, 11):
            if c < 3:
                rows24 = jnp.concatenate([wqkv[:, 768 * i + 256 * c:768 * i + 256 * c + 256] for i in range(3)], axis=1)
            elif c == 3:
                rows24 = wout[...]
            else:
                rows24 = (wup if c % 2 == 0 else wdn)[:, 768 * ((c - 4) // 2):768 * ((c - 4) // 2) + 768]
            if c == 10:
                turned.s1(slab_of(rows24.astype(F32)))
                continue
            slab[c, p.z] = slab_of(rows24.astype(F32))
            if c < 3:
                big.s1(c)
        tokt[...] = tok[...].T
        tiny.s2()
        big.s1(3)
        big.s2(0)
        big.s1(4)
        big.s2(1)
        tiny.s3()
        big.s3(0)
        big.s1(5)
        big.s2(2)
        big.s3(1)
        big.s1(6)
        big.s2(3)
        big.s4(0)
        tiny.s4()
        pieces[...] = dense_s[...].reshape(32, 24, 128)
        whole = unpack_small(pieces, 0, 1, 72, 2304)[0]
        for g in range(3):
            for i in range(3):
                bqkv[g, :, 256 * i:256 * i + 256] = whole[:, 768 * i + 256 * g:768 * i + 256 * g + 256]
        taps = unpack_small(pieces, 1, 5, 48, 1536)
        for t in range(5):
            for g in range(3):
                for i in range(2):
                    conv[g, t:t + 1, 256 * i:256 * i + 256] = taps[t][:, 768 * i + 256 * g:768 * i + 256 * g + 256]
        rest = unpack_small(pieces, 6, 6, 24, 768)
        for i in range(6):
            vec[i:i + 1, :] = rest[i]
        whole = unpack_small(pieces, 12, 1, 96, 3072)[0]
        for j in range(4):
            bup[j] = whole[:, 768 * j:768 * j + 768]
        big.s5(0)
        todo = [[(big.s2, 8), (big.s3, 6)], [(big.s4, 5), (big.s2, 9)],
                [(big.s3, 7)], [(big.s4, 6), (big.s2, 11)], [(big.s3, 8)], [(big.s4, 7)],
                [(big.s3, 9)], [(big.s4, 8)], [(big.s3, 11)], [(big.s4, 9)],
                [], [(lambda c: turned.s3(), 10)], [(big.s4, 11)]]
    else:
        tokt[...] = tok[...].T
        load = pltpu.make_async_copy(w_in, w, sems.at[0])
        load.start()
        load.wait()

    def progress():
        for step, c in todo.pop(0) if todo else ():
            step(c)

    def group(g, carry):
        if comm:
            @pl.when(g > 0)
            def _():
                big.s5(g)
        project_group(g, tok, w, bqkv, conv, qkv, pkv, kvf)

        def block(b, inner):
            if comm:
                i = 4 * g + b
                n = lax.div(i, 3)

                @pl.when(lax.rem(i, 3) == 0)
                def _():
                    big.s1(7 + n + lax.div(n, 3))
                    big.s2(4 + n)
                    big.s3(2 + n)

                @pl.when(lax.rem(i, 3) == 2)
                def _():
                    big.s4(1 + n)

                @pl.when(i == 10)
                def _():
                    turned.s2()
            attend_blocks(g, (2 * b, 2 * b + 1), qkv, pkv, ctx, lse)
            return inner

        return lax.fori_loop(0, 4, block, carry)

    lax.fori_loop(0, 3, group, 0)
    keep(tokt, tokt_o)
    keep(qkv.at[pl.ds(0, 3)], qkv_o)
    keep(pkv, pkv_o)
    keep(ctx, ctx_o)
    keep(lse, lse_o)
    if comm:
        big.s5(3)
        keep(w.at[pl.ds(0, 4)], w_o.at[pl.ds(0, 4)])
    b_out, gain1, shift1, b_down, gain2, shift2 = [vec[pl.ds(i, 1), :] for i in range(6)]
    tiles = [pl.ds(512 * r, 512) for r in range(2)]
    for rows in tiles:
        pre_one = tok[rows, :].astype(F32) + mm_nt(ctx[rows, :], weight(w, 3)) + b_out
        pre[rows, :] = pre_one
        xhat, rate = norm_stats(pre_one)
        low = (xhat * gain1 + shift1).astype(BF)
        first[rows, :] = low
        acc[rows, :] = low.astype(F32) + b_down
        progress()
    keep(pre, pre_o)
    tr[...] = first[...].T
    keep(tr, firstt_o)
    first_kept = len(kept) - 1
    for j in range(4):
        if comm:
            big.s5(4 + 2 * j)
        for rows in tiles:
            value, slope = gelu_both(mm(first[rows, :], weight(w, 4 + 2 * j)) + bup[j])
            act[j, rows, :] = value.astype(BF)
            gp[j, rows, :] = slope.astype(BF)
            progress()
        if comm:
            big.s5(5 + 2 * j)
            keep(w.at[pl.ds(4 + 2 * j, 2)], w_o.at[pl.ds(4 + 2 * j, 2)])
        for rows in tiles:
            acc[rows, :] += mm_nt(act[j, rows, :], weight(w, 5 + 2 * j))
            progress()
        keep(gp.at[j], gp_o.at[j])
    sums = [jnp.zeros((1, 768), F32) for _ in range(3)]
    for r, rows in enumerate(tiles):
        xhat, rate = norm_stats(acc[rows, :])
        out[rows, :] = (xhat * gain2 + shift2).astype(BF)
        row = 512 * r + lax.broadcasted_iota(jnp.int32, (512, 160), 0)
        dy = mm((row == pos[...]).astype(BF), cot[...])
        sums[1] = sums[1] + colsum(dy * xhat)
        sums[2] = sums[2] + colsum(dy)
        dacc = norm_back(xhat, rate, gain2, dy)
        low = dacc.astype(BF)
        dbr[rows, :] = low
        acc[rows, :] = dacc
        sums[0] = sums[0] + colsum(low.astype(F32))
    gsm[...] = jnp.zeros_like(gsm)
    for i in range(3):
        gsm[2 + i:3 + i, :] = sums[i]
    keep(out, out_o)
    keep(dbr, dbr_o)
    keep(acc, acc_o)
    kept.pop(first_kept).wait()
    tr[...] = dbr[...].T
    sent = []
    for j in range(4):
        if j >= 2:
            sent[j - 2].wait()
        stage[j % 2] = mm(tr[...], act[j]).astype(BF).reshape(2, 2, 2, 96, 768)
        sent.append(pltpu.make_async_copy(stage.at[j % 2], gwd_o.at[j], sems.at[j % 2]))
        sent[j].start()
    sent[2].wait()
    sent[3].wait()
    for copy in kept:
        copy.wait()
    if comm:
        for c in range(12):
            (turned.sent() if c == 10 else big.sent(c))
        tiny.sent()


def forward_call(comm, *args):
    outs = [
        (struct((1024, 768), BF), ANY), (struct((1024, 768), F32), ANY), (struct((768, 1024), BF), ANY),
        (struct((768, 1024), BF), ANY),
        (struct((1024, 768), F32), ANY), (struct((1024, 768), BF), ANY), (struct((4, 1024, 768), BF), ANY),
        (struct((4, 2, 2, 2, 96, 768), BF), ANY), (struct((3, 1024, 768), BF), ANY), (struct((3, 256, 512), BF), ANY),
        (struct((1024, 768), BF), ANY), (struct((48, 1, 256), F32), ANY), (struct((8, 768), F32), VM),
    ]
    scratch = [
        pltpu.VMEM((12, 2, 2, 2, 96, 768), BF), pltpu.VMEM((3, 1024, 768), BF), pltpu.VMEM((4, 1024, 768), BF),
        pltpu.VMEM((4, 1024, 768), BF), pltpu.VMEM((1024, 768), F32), pltpu.VMEM((1024, 768), F32),
        pltpu.VMEM((1024, 768), BF), pltpu.VMEM((1024, 768), BF), pltpu.VMEM((768, 1024), BF), pltpu.VMEM((768, 1024), BF),
        pltpu.VMEM((1024, 768), BF),
        pltpu.VMEM((3, 256, 512), BF), pltpu.VMEM((48, 1, 256), F32), pltpu.VMEM((1024, 768), BF),
        pltpu.VMEM((4, 1040, 128), F32), pltpu.VMEM((2, 2, 2, 2, 96, 768), BF), DMA((2,)), DMA((20,)),
    ]
    if comm:
        outs += [(struct((12, 2, 2, 2, 96, 768), BF), ANY), (struct((3, 8, 512), F32), VM), (struct((8, 768), F32), VM)]
        scratch += [
            pltpu.VMEM((12, 4, 16, 1152), BF), pltpu.VMEM((4, 24, 128), F32), pltpu.VMEM((2, 2, 2, 4, 24, 128), F32),
            pltpu.VMEM((32, 24, 128), F32), pltpu.VMEM((3, 1, 768), F32), pltpu.VMEM((4, 1, 768), F32),
            pltpu.VMEM((4, 4, 16, 1152), BF),
            DMA((12, 3)), DMA((12, 3)), DMA((12, 4)), DMA((12, 4)), DMA((12,)), DMA((12,)), DMA((7,)), DMA((7,)),
            DMA((3,)), DMA((3,)), DMA((3,)), DMA((3,)),
        ]
        params = pltpu.CompilerParams(vmem_limit_bytes=LIMIT, collective_id=1, has_side_effects=True)
    else:
        params = pltpu.CompilerParams(vmem_limit_bytes=LIMIT)
    ins = [VM] * len(args)
    if not comm:
        ins[1] = ANY
    return pl.pallas_call(
        functools.partial(forward_kernel, comm), in_specs=ins, out_specs=[o[1] for o in outs],
        out_shape=[o[0] for o in outs], scratch_shapes=scratch, compiler_params=params, name="forward")(*args)


def qkv_rows(g, start, size):
    return pl.ds(pl.multiple_of(3072 + 1024 * g + start, 32), size)


def back_blocks(g, blocks, wb, pkv, buf, lse, dk, dv, dpk, dpv):
    parts = []
    for b in blocks:
        ns, ps, near, far = window(b)
        first_row = pl.multiple_of(b * 128, 128)
        rows, prow = pl.ds(first_row, 128), pl.ds(ps, 160)
        qrows, krows = qkv_rows(g, first_row, 128), qkv_rows(g, ns, 256)
        for pr in range(2):
            parts.append(dict(
                near=near, far=far, rows=rows, nr=pl.ds(ns, 256), prow=prow, ln=pl.ds(128 * pr, 128),
                qm=head_split(wb[qrows, 128 * pr:128 * pr + 128], 0.125),
                dm=head_split(buf[3, rows, lane_block(256 * g + 128 * pr)], 1.0),
                kn=wb[krows, 256 + 128 * pr:384 + 128 * pr],
                kp=pkv[g, prow, 128 * pr:128 * pr + 128],
                vn=wb[krows, 512 + 128 * pr:640 + 128 * pr],
                vp=pkv[g, prow, 256 + 128 * pr:384 + 128 * pr],
                ls=lse[(g * 2 + pr) * 8 + b]))
    for t in parts:
        t["pn"] = jnp.exp(jnp.where(t["near"], mm_nt(t["kn"], t["qm"]), -1e30) - t["ls"])
        t["pp"] = jnp.exp(jnp.where(t["far"], mm_nt(t["kp"], t["qm"]), -1e30) - t["ls"])
    for t in parts:
        t["dn"] = mm_nt(t["vn"], t["dm"])
        t["dp"] = mm_nt(t["vp"], t["dm"])
        t["gvn"] = mm(t["pn"].astype(BF), t["dm"])
        t["gvp"] = mm(t["pp"].astype(BF), t["dm"])
    for t in parts:
        rd = jnp.sum(t["pn"] * t["dn"], axis=0, keepdims=True) + jnp.sum(t["pp"] * t["dp"], axis=0, keepdims=True)
        t["sn"] = (t["pn"] * (t["dn"] - rd)).astype(BF)
        t["sp"] = (t["pp"] * (t["dp"] - rd)).astype(BF)
    for t in parts:
        t["gkn"] = mm(t["sn"], t["qm"])
        t["gkp"] = mm(t["sp"], t["qm"])
        t["gq"] = (head_join(mm_tn(t["kn"], t["sn"]) + mm_tn(t["kp"], t["sp"])).T * 0.125).astype(BF)
    for t in parts:
        dk[t["nr"], t["ln"]] += t["gkn"]
        dpk[t["prow"], t["ln"]] += t["gkp"]
        dv[t["nr"], t["ln"]] += t["gvn"]
        dpv[t["prow"], t["ln"]] += t["gvp"]
        buf[g, t["rows"], t["ln"]] = t["gq"]


def pool_back(g, conv, wb, kvf, dk, dv, dpk, dpv, buf, gconv):
    for part in range(4):
        kvf[part, 8:1032, :] = wb[qkv_rows(g, 0, 1024), 256 + 128 * part:384 + 128 * part].astype(F32)
    for part in range(4):
        cols = pl.ds(128 * part, 128)
        src, dst = (dpk, dk) if part < 2 else (dpv, dv)
        half = pl.ds(128 * (part % 2), 128)
        dpool = src[:, half]
        for t in range(5):
            gconv[g, pl.ds(t, 1), cols] = colsum(dpool * kvf[part, pl.ds(6 + t, 256, stride=4), :])
        kvf[part, 8:1032, :] = dst[:, half]
        for t in range(5):
            at = pl.ds(6 + t, 256, stride=4)
            kvf[part, at, :] += conv[g, pl.ds(t, 1), cols] * dpool
        buf[g, :, 256 + 128 * part:384 + 128 * part] = kvf[part, 8:1032, :].astype(BF)
        kvf[part, 0:8, :] = jnp.zeros((8, 128), F32)
        kvf[part, 1032:1040, :] = jnp.zeros((8, 128), F32)


BLOCKS = (2, 2, 2, 96, 768)


STEPS = (
    (), ((1, 0),), (), ((1, 1),), (), ((1, 2), (2, 0)), (), ((1, 3), (2, 1)), (), ((1, 4), (2, 2), (3, 0)), (),
    ((1, 5), (2, 3), (3, 1)), (), ((1, 6), (2, 4), (3, 2), (4, 0)), ((4, 1),),
)
LOOP_STEPS = {
    0: ((2, 5), (3, 3)), 1: ((1, 7), (2, 6)), 2: ((3, 4), (4, 2)), 3: ((1, 8), (3, 5), (4, 3)), 4: ((2, 7),), 5: ((3, 6), (4, 4)),
    6: ((1, 9), (2, 8)), 7: ((4, 5),), 8: ((3, 7),), 9: ((1, 10), (2, 9), (4, 6)), 10: ((3, 8), (4, 7)), 11: ((2, 10), (3, 9), (4, 8)),
}


def backward_kernel(comm, *refs):
    (tokt_i, w_i, conv, vec, pre_i, firstt_i, acc_i, dbr_i, gp_i, qkv_i, pkv_i, ctx_i, lse_i, gsm_in) = refs[:14]
    if comm:
        (gwd_i, gtok_o, fin, tot,
         wb, buf, xb, db, tr, acc, gtok, pkv, lse, kvf, isem, osem,
         gat, gconv, gbias, gbout, gsm, gbup, r0, r1a, r1b, r2, v, r3, own, pieces, small, t0, t1, t2,
         ks, kr, xs, xr, zs, zr, ls, ss, sr) = refs[14:]
    else:
        (gtok_o, gat, gconv, gbias, gbout, gsm, gbup,
         wb, buf, xb, db, tr, acc, gtok, pkv, lse, kvf, isem, osem) = refs[14:]
    dk, dv = acc.at[:, pl.ds(0, 256)], acc.at[:, pl.ds(256, 256)]
    dpk, dpv = acc.at[pl.ds(0, 256), pl.ds(512, 256)], acc.at[pl.ds(256, 256), pl.ds(512, 256)]
    loads = {}

    def load(name, src, dst):
        loads[name] = pltpu.make_async_copy(src, dst, isem.at[len(loads)])
        loads[name].start()

    def slot(n):
        return wb[pl.ds(768 * n, 768), :]

    def load_weight(c, n):
        for i in range(8):
            load(("w", c, i), w_i.at[c, i // 4, i // 2 % 2, i % 2], wb.at[pl.ds(768 * n + 96 * i, 96), :])

    def have_weight(c):
        for i in range(8):
            loads["w", c, i].wait()

    load("dbr", dbr_i, db)
    load_weight(5, 1)
    load(("gp", 0), gp_i.at[0], buf.at[0])
    if comm:
        p = Place()
        big = Scatter(p, r0, r1a, r1b, r2, v, r3, fin, (ks, kr, xs, xr, zs, zr))
        tiny = SmallScatter(p, small, t0, t1, t2, ss, sr)
        p.greet()

        def fetch(c):
            return pltpu.make_async_copy(gwd_i.at[c, :, :, p.k], own.at[c % 2], ls.at[c % 2])

        big.across(0, gwd_i.at[0]).start()
        fetch(0).start()
        big.across(1, gwd_i.at[1]).start()

        def take(steps):
            for stage, c in steps:
                if stage > 1:
                    (big.s2, big.s3, big.s4)[stage - 2](c)
                elif c >= 4:
                    at = c - 4 if c < 9 else c - 9
                    big.s1(c, gat.at[0], lambda a, b: gat[at, a, b, p.k])
                else:
                    fetch(c).wait()
                    big.s1(c, gat.at[0], lambda a, b: own[c % 2, a, b])
                    if c < 2:
                        fetch(c + 2).start()

    def run(n):
        if comm:
            take(STEPS[n])

    load_weight(4, 0)
    load("acc", acc_i, acc)

    def load_next(j):
        if j == 0:
            load("first", firstt_i, tr)
            if comm:
                fetch(1).start()
                big.across(2, gwd_i.at[2]).start()
                big.across(3, gwd_i.at[3]).start()
        if j < 3:
            load_weight(7 + 2 * j, 3 + 2 * j)
            load(("gp", j + 1), gp_i.at[j + 1], buf.at[j + 1])
            load_weight(6 + 2 * j, 2 + 2 * j)
        if j == 2:
            load("tok", tokt_i, xb)
        if j == 3:
            load("pre", pre_i, gtok)
            load("pkv", pkv_i, pkv)
            load("lse", lse_i, lse)

    clear_edges(kvf)
    gbup[...] = jnp.zeros_like(gbup)
    gsm[...] = gsm_in[...]
    tiles = [pl.ds(512 * r, 512) for r in range(2)]
    loads["dbr"].wait()
    for j in range(4):
        have_weight(5 + 2 * j)
        loads["gp", j].wait()
        load_next(j)
        for r, rows in enumerate(tiles):
            low = (mm(db[rows, :], slot(1 + 2 * j)) * buf[j, rows, :].astype(F32)).astype(BF)
            buf[j, rows, :] = low
            gbup[j] += colsum(low.astype(F32))
            if r == 0:
                have_weight(4 + 2 * j)
                if j == 0:
                    loads["acc"].wait()
            acc[rows, :] += mm_nt(low, slot(2 * j))
            run(3 * j + r)
        if j == 0:
            loads["first"].wait()
        gat[j] = mm(tr[...], buf[j]).astype(BF).reshape(BLOCKS)
        if comm:
            big.across(4 + j, gat.at[j]).start()
            run(3 * j + 2)
        if j == 1:
            for c in range(4):
                load_weight(c, c)
    for g in range(3):
        load(("qkv", g), qkv_i.at[g], wb.at[pl.ds(3072 + 1024 * g, 1024), :])
    load("ctx", ctx_i, db)
    loads["pre"].wait()
    gain1 = vec[1:2, :]
    sums = [jnp.zeros((1, 768), F32) for _ in range(3)]
    have_weight(3)
    for rows in tiles:
        xhat, rate = norm_stats(gtok[rows, :])
        dacc = acc[rows, :]
        sums[0] = sums[0] + colsum(dacc * xhat)
        sums[1] = sums[1] + colsum(dacc)
        dpre = norm_back(xhat, rate, gain1, dacc)
        gtok[rows, :] = dpre
        da = dpre.astype(BF)
        sums[2] = sums[2] + colsum(da.astype(F32))
        buf[3, rows, :] = mm(da, slot(3)).astype(BF)
        tr[:, rows] = da.T
    gsm[0:1, :] = sums[0]
    gsm[1:2, :] = sums[1]
    gbout[...] = sums[2]
    if comm:
        run(12)
        pieces[...] = jnp.zeros_like(pieces)
        pack_small(pieces, 6, [gbout[...]] + [gsm[i:i + 1, :] for i in range(5)], 24, 768)
        pack_small(pieces, 12, [jnp.concatenate([gbup[j] for j in range(4)], axis=1)], 96, 3072)
    loads["ctx"].wait()
    gat[4] = mm(tr[...], db[...]).astype(BF).reshape(BLOCKS)
    if comm:
        big.across(8, gat.at[4]).start()
        run(13)
    loads["tok"].wait()
    loads["pkv"].wait()
    loads["lse"].wait()
    for g in range(3):
        loads["qkv", g].wait()
        have_weight(g)
    run(14)

    def group(g, carry):
        acc[...] = jnp.zeros_like(acc)

        def block(b, inner):
            if comm:
                for i, steps in LOOP_STEPS.items():
                    pl.when(4 * g + b == i)(functools.partial(take, steps))
            back_blocks(g, (2 * b, 2 * b + 1), wb, pkv, buf, lse, dk, dv, dpk, dpv)
            return inner

        lax.fori_loop(0, 4, block, 0)
        pool_back(g, conv, wb, kvf, dk, dv, dpk, dpv, buf, gconv)
        if comm:
            big.across(4 + g, gat.at[0]).wait_send()
        gat[g if comm else 5 + g] = mm(xb[...], buf[g]).astype(BF).reshape(BLOCKS)
        if comm:
            big.across(9 + g, gat.at[g]).start()
        gbias[g] = colsum(buf[g].astype(F32))
        return carry

    lax.fori_loop(0, 3, group, 0)
    parts = []

    def token_part(n):
        rows = pl.ds(256 * n, 256)
        total = gtok[rows, :]
        for g in range(3):
            total = total + mm_nt(buf[g, rows, :], slot(g))
        gtok[rows, :] = total
        parts.append(pltpu.make_async_copy(gtok.at[rows, :], gtok_o.at[rows, :], osem.at[n]))
        parts[n].start()

    if not comm:
        for n in range(4):
            token_part(n)
        for copy in parts:
            copy.wait()
        return

    token_part(0)
    take(((1, 11),))
    kinds = [jnp.concatenate([gbias[g][:, 256 * i:256 * i + 256] for i in range(3) for g in range(3)], axis=1)]
    pack_small(pieces, 0, kinds, 72, 2304)
    pack_small(pieces, 1, [
        jnp.concatenate([gconv[g, t:t + 1, 256 * i:256 * i + 256] for i in range(2) for g in range(3)], axis=1)
        for t in range(5)], 48, 1536)
    small[...] = pieces[...].reshape(2, 2, 2, 96, 128)
    tiny.s0()
    take(((3, 10),))
    token_part(1)
    tiny.s1()
    take(((2, 11), (4, 9)))
    token_part(2)
    tiny.s2()
    take(((3, 11), (4, 10)))
    token_part(3)
    tot[...] = tiny.s3()
    take(((4, 11),))
    for c in range(12):
        for copy in big.first(c) + big.second(c) + tuple(big.along_z(c, dz) for dz in (1, 2, 3)):
            copy.wait_send()
        if c not in (4, 5, 6):
            big.across(c, gat.at[0]).wait_send()
    tiny.sent()
    for copy in parts:
        copy.wait()


def backward_call(comm, *args):
    scratch = [
        pltpu.VMEM((6144, 768), BF), pltpu.VMEM((4, 1024, 768), BF), pltpu.VMEM((768, 1024), BF), pltpu.VMEM((1024, 768), BF),
        pltpu.VMEM((768, 1024), BF), pltpu.VMEM((1024, 768), F32), pltpu.VMEM((1024, 768), F32),
        pltpu.VMEM((3, 256, 512), BF), pltpu.VMEM((48, 1, 256), F32),
        pltpu.VMEM((4, 1040, 128), F32), DMA((120,)), DMA((4,)),
    ]
    ins = [ANY] * len(args)
    for i in (2, 3, 13):
        ins[i] = VM
    local = [((5 if comm else 8,) + BLOCKS, BF), ((3, 8, 512), F32), ((3, 1, 768), F32), ((1, 768), F32), ((8, 768), F32), ((4, 1, 768), F32)]
    outs = [(struct((1024, 768), F32), ANY)]
    if comm:
        outs += [(struct((12, 24, 768), F32), VM), (struct((24, 128), F32), VM)]
        scratch += [pltpu.VMEM(*s) for s in local]
        scratch += [
            pltpu.VMEM((12, 2, 2, 96, 768), BF), pltpu.VMEM((12, 2, 96, 384), BF), pltpu.VMEM((12, 2, 96, 384), BF),
            pltpu.VMEM((12, 2, 96, 384), BF), pltpu.VMEM((12, 4, 16, 1152), BF), pltpu.VMEM((12, 3, 16, 1152), BF),
            pltpu.VMEM((2, 2, 2, 96, 768), BF), pltpu.VMEM((32, 24, 128), F32),
            pltpu.VMEM((2, 2, 2, 96, 128), F32), pltpu.VMEM((2, 2, 96, 128), F32), pltpu.VMEM((3, 96, 128), F32),
            pltpu.VMEM((3, 24, 128), F32),
            DMA((12,)), DMA((12,)), DMA((12, 4)), DMA((12, 4)), DMA((12, 3)), DMA((12, 3)), DMA((2,)), DMA((7,)), DMA((7,)),
        ]
        params = pltpu.CompilerParams(vmem_limit_bytes=LIMIT, collective_id=2, has_side_effects=True)
    else:
        outs += [(struct(*s), VM) for s in local]
        params = pltpu.CompilerParams(vmem_limit_bytes=LIMIT)
    return pl.pallas_call(
        functools.partial(backward_kernel, comm), in_specs=ins, out_specs=[o[1] for o in outs], out_shape=[o[0] for o in outs],
        scratch_shapes=scratch, compiler_params=params, name="backward")(*args)


def finish_kernel(out_i, gtok_i, fin, tot, out, gtok, gqkv, gqb, gcv, gwo, gbo, gg1, gs1, gwu, gbu, gwd, gbd, gg2, gs2):
    out[...] = out_i[...]
    gtok[...] = gtok_i[...]

    @pl.when(pl.program_id(0) == 0)
    def _():
        for j in range(4):
            gwd[:, 768 * j:768 * j + 768] = fin[j]
            gwu[:, 768 * j:768 * j + 768] = fin[4 + j]
        gwo[...] = fin[8]
        for g in range(3):
            for i in range(3):
                gqkv[:, 768 * i + 256 * g:768 * i + 256 * g + 256] = fin[9 + g, :, 256 * i:256 * i + 256]
        gqb[...] = tot[0:1, 0:72]
        gcv[...] = tot[1:6, 0:48]
        for i, ref in enumerate((gbo, gg1, gs1, gbd, gg2, gs2)):
            ref[...] = tot[6 + i:7 + i, 0:24]
        gbu[...] = tot[12:13, 0:96]


def finish_call(*args):
    shapes = ((24, 2304), (1, 72), (5, 48), (24, 768), (1, 24), (1, 24), (1, 24), (24, 3072), (1, 96),
              (24, 3072), (1, 24), (1, 24), (1, 24))
    part = pl.BlockSpec((512, 768), lambda n: (n, 0))

    def full(shape):
        return pl.BlockSpec(shape, lambda n: (0,) * len(shape))

    return pl.pallas_call(
        finish_kernel, grid=(2,), in_specs=[part, part, full((12, 24, 768)), full((24, 128))],
        out_specs=[part, part] + [full(s) for s in shapes],
        out_shape=[struct((1024, 768), BF), struct((1024, 768), F32)] + [struct(s, F32) for s in shapes],
        name="finish")(*args)


def shards_direct(tokens, w_qkv, b_qkv, conv_kv, w_out, b_out, gain_one, shift_one, w_up, b_up, w_down, b_down, gain_two,
                  shift_two, positions, cotangent):
    tok = tokens[0]
    out, pre, tokt, firstt, acc, dbr, gp, gwd, qkv, pkv, ctx, lse, gsm, w, conv, vec = forward_call(
        True, tok, w_qkv, b_qkv[None], conv_kv, w_out.T, b_out[None], gain_one[None], shift_one[None], b_down[None],
        gain_two[None], shift_two[None], w_up, b_up[None], w_down.T, positions, cotangent[0])
    gtok, fin, tot = backward_call(True, tokt, w, conv, vec, pre, firstt, acc, dbr, gp, qkv, pkv, ctx, lse, gsm, gwd)
    (out, gtok, gqkv, gqb, gcv, gwo, gbo, gg1, gs1, gwu, gbu, gwd, gbd, gg2, gs2) = finish_call(out, gtok, fin, tot)
    return (out[None], gtok[None], gqkv, gqb[0], gcv, gwo.T, gbo[0], gg1[0], gs1[0], gwu, gbu[0], gwd.T, gbd[0], gg2[0], gs2[0])


def small_sizes(count):
    return [2304 // count] + [1536 // count] * 5 + [768 // count] * 6 + [3072 // count]


def by_group(v, kinds):
    return v.reshape(kinds, 3, 256).transpose(1, 0, 2).reshape(3, 1, kinds * 256)


def shards_general(tokens, w_qkv, b_qkv, conv_kv, w_out, b_out, gain_one, shift_one, w_up, b_up, w_down, b_down, gain_two,
                   shift_two, positions, cotangent):
    rows = w_qkv.shape[0]
    count = 768 // rows
    blocks = (2, 2, 2, 96, 768)
    up = w_up.reshape(rows, 4, 768).transpose(1, 0, 2)
    down = w_down.reshape(4, 768, rows).transpose(0, 2, 1)
    own = jnp.concatenate([
        w_qkv.reshape(rows, 3, 3, 256).transpose(2, 0, 1, 3).reshape(3, rows, 768),
        w_out.T[None],
        jnp.stack([up, down], 1).reshape(8, rows, 768),
    ], 0)
    w = lax.all_gather(own, AXES, axis=1, tiled=True).reshape((12,) + blocks)
    small = jnp.concatenate([b_qkv, conv_kv.reshape(-1), b_out, gain_one, shift_one, b_down, gain_two, shift_two, b_up])
    small = lax.all_gather(small[None], AXES, axis=0, tiled=True).astype(F32)
    at, parts = 0, []
    for size in small_sizes(count):
        parts.append(small[:, at:at + size].reshape(-1))
        at += size
    bqkv = by_group(parts[0], 3)
    conv = jnp.concatenate([by_group(p, 2) for p in parts[1:6]] + [jnp.zeros((3, 3, 512), F32)], 1)
    vec = jnp.stack(parts[6:12] + [jnp.zeros((768,), F32)] * 2)
    bup = parts[12].reshape(4, 1, 768)
    out, pre, tokt, firstt, acc, dbr, gp, gwd, qkv, pkv, ctx, lse, gsm = forward_call(
        False, tokens[0], w, bqkv, conv, vec, bup, positions, cotangent[0])
    gwd = lax.psum_scatter(gwd.reshape(4, 768, 768), AXES, scatter_dimension=1, tiled=True).astype(F32)
    gtok, gat, gconv, gbias, gbout, gsm, gbup = backward_call(
        False, tokt, w, conv, vec, pre, firstt, acc, dbr, gp, qkv, pkv, ctx, lse, gsm)
    gat = lax.psum_scatter(gat.reshape(8, 768, 768), AXES, scatter_dimension=1, tiled=True).astype(F32)
    flat = [gbias.reshape(3, 3, 256).transpose(1, 0, 2).reshape(count, -1)]
    flat += [gconv[:, t].reshape(3, 2, 256).transpose(1, 0, 2).reshape(count, -1) for t in range(5)]
    flat += [gbout[0].reshape(count, -1)] + [gsm[i].reshape(count, -1) for i in range(5)] + [gbup.reshape(count, -1)]
    flat = lax.psum_scatter(jnp.concatenate(flat, 1), AXES, scatter_dimension=0, tiled=True)
    at, s = 0, []
    for size in small_sizes(count):
        s.append(flat[0, at:at + size])
        at += size
    return (
        out[None], gtok[None],
        gat[5:].reshape(3, rows, 3, 256).transpose(1, 2, 0, 3).reshape(rows, 2304),
        s[0], jnp.stack(s[1:6]), gat[4].T, s[6], s[7], s[8],
        gat[:4].transpose(1, 0, 2).reshape(rows, 3072), s[12],
        gwd.transpose(0, 2, 1).reshape(3072, rows), s[9], s[10], s[11],
    )


def solution(mesh):
    rows, cols, flat, item = P(AXES, None), P(None, AXES), P(AXES), P(AXES, None, None)
    direct = mesh.shape["dp"] == 8 and mesh.shape["fsdp"] == 4
    return jax.shard_map(
        shards_direct if direct else shards_general,
        mesh=mesh,
        in_specs=(item, rows, flat, cols, cols, flat, flat, flat, rows, flat, cols, flat, flat, flat, rows, item),
        out_specs=(item, item, rows, flat, cols, cols, flat, flat, flat, rows, flat, cols, flat, flat, flat),
        check_vma=False,
    )
```

```python
import functools
import jax
import jax.numpy as jnp
from jax import lax
from jax.experimental import pallas as pl
from jax.experimental.pallas import tpu as pltpu
from jax.sharding import PartitionSpec as P

F32 = jnp.float32
BF = jnp.bfloat16
EPS = 1e-5
NT = (((1,), (1,)), ((), ()))
TN = (((0,), (0,)), ((), ()))
AXES = ("dp", "fsdp")
VM = pl.BlockSpec(memory_space=pltpu.VMEM)
ANY = pl.BlockSpec(memory_space=pl.ANY)
LIMIT = 64 * 1024 * 1024 - 512 * 1024
DMA = pltpu.SemaphoreType.DMA
struct = jax.ShapeDtypeStruct


def mm(a, b):
    return jnp.dot(a, b, preferred_element_type=F32)


def mm_nt(a, b):
    return lax.dot_general(a, b, NT, preferred_element_type=F32)


def mm_tn(a, b):
    return lax.dot_general(a, b, TN, preferred_element_type=F32)


def norm_stats(values):
    average = jnp.mean(values, axis=-1, keepdims=True)
    centred = values - average
    variance = jnp.mean(centred * centred, axis=-1, keepdims=True)
    rate = lax.rsqrt(variance + EPS)
    return centred * rate, rate


def norm_back(xhat, rate, gain, dy):
    e = dy * gain
    mean_e = jnp.mean(e, axis=-1, keepdims=True)
    mean_ex = jnp.mean(e * xhat, axis=-1, keepdims=True)
    return rate * (e - mean_e - xhat * mean_ex)


def colsum(v):
    return jnp.sum(v, axis=0, keepdims=True)


def gelu_both(u):
    c = 0.7978845608028654
    u2 = u * u
    t = jnp.tanh(u * (c + (c * 0.044715) * u2))
    half = 0.5 + 0.5 * t
    value = u * half
    slope = half + (0.5 * u) * (1.0 - t * t) * (c + (3.0 * c * 0.044715) * u2)
    return value, slope


def head_split(x, scale):
    lane = lax.broadcasted_iota(jnp.int32, x.shape, 1)
    low = jnp.where(lane < 64, scale, 0.0).astype(BF)
    high = jnp.where(lane < 64, 0.0, scale).astype(BF)
    return jnp.concatenate([x * low, x * high], axis=0)


def head_join(r):
    return jnp.concatenate([r[:64, :128], r[64:, 128:]], axis=0)


def window(b):
    ns = pl.multiple_of(jnp.clip(b * 128 - 64, 0, 1024 - 256), 64)
    ps = pl.multiple_of(jnp.clip(b * 32 - 64, 0, 256 - 160), 32)
    col = b * 128 + (lax.broadcasted_iota(jnp.int32, (256, 256), 1) & 127)
    row = ns + lax.broadcasted_iota(jnp.int32, (256, 256), 0)
    near = jnp.abs(row - col) <= 64
    colp = b * 128 + (lax.broadcasted_iota(jnp.int32, (160, 256), 1) & 127)
    rowp = 4 * (ps + lax.broadcasted_iota(jnp.int32, (160, 256), 0))
    far = jnp.abs(rowp - colp) <= 256
    return ns, ps, near, far


class Place:
    def __init__(self):
        d = lax.axis_index("dp")
        self.d, self.z = d, lax.axis_index("fsdp")
        self.k, self.x, self.y = lax.rem(d, 2), lax.rem(lax.div(d, 2), 2), lax.div(d, 4)
        self.sib = d + 1 - 2 * self.k
        self.xn = d + 2 - 4 * self.x
        self.yn = d + 4 - 8 * self.y
        self.diag = self.xn + 4 - 8 * self.y

    def up(self, dz):
        return lax.rem(self.z + dz, 4)

    def copy(self, src, dst, send, recv, dp=None, z=None):
        return pltpu.make_async_remote_copy(
            src_ref=src, dst_ref=dst, send_sem=send, recv_sem=recv,
            device_id={"dp": self.d if dp is None else dp, "fsdp": self.z if z is None else z},
            device_id_type=pl.DeviceIdType.MESH)

    def greet(self):
        barrier = pltpu.get_barrier_semaphore()
        for dp in (self.sib, self.xn, self.yn, self.diag):
            pl.semaphore_signal(barrier, inc=1, device_id={"dp": dp, "fsdp": self.z},
                                device_id_type=pl.DeviceIdType.MESH)
        for dz in (1, 2, 3):
            pl.semaphore_signal(barrier, inc=1, device_id={"dp": self.d, "fsdp": self.up(dz)},
                                device_id_type=pl.DeviceIdType.MESH)
        pl.semaphore_wait(barrier, 7)


def slab_of(rows):
    last = jnp.concatenate([rows[..., 16:, :384], rows[..., 16:, 384:]], axis=-2)
    return jnp.concatenate([rows[..., :16, :], last], axis=-1).astype(BF)


def rows_of(slab):
    v = slab.astype(F32)
    last = jnp.concatenate([v[..., :8, 768:], v[..., 8:, 768:]], axis=-1)
    return jnp.concatenate([v[..., :768], last], axis=-2)


class Gather:
    def __init__(self, p, slab, dense, sems):
        self.p, self.slab, self.dense = p, slab, dense
        self.zs, self.zr, self.xs, self.xr, self.ks, self.kr = sems

    def along_z(self, c, dz, arriving=False):
        p = self.p
        slot = p.up(4 - dz) if arriving else p.z
        return p.copy(self.slab.at[c, p.z], self.slab.at[c, slot], self.zs.at[c, dz - 1], self.zr.at[c, dz - 1],
                      z=p.up(dz))

    def first(self, c, arriving=False):
        p, w = self.p, self.dense
        ya = 1 - p.y if arriving else p.y
        xa = 1 - p.x if arriving else p.x
        a, b = pl.ds(0, 384), pl.ds(384, 384)
        return (
            p.copy(w.at[c, p.y, p.x, p.k, :, a], w.at[c, p.y, xa, p.k, :, a], self.xs.at[c, 0], self.xr.at[c, 0], dp=p.xn),
            p.copy(w.at[c, p.y, p.x, p.k, :, b], w.at[c, ya, p.x, p.k, :, b], self.xs.at[c, 1], self.xr.at[c, 1], dp=p.yn),
        )

    def second(self, c, arriving=False):
        p, w = self.p, self.dense
        ya = 1 - p.y if arriving else p.y
        xa = 1 - p.x if arriving else p.x
        a, b = pl.ds(0, 384), pl.ds(384, 384)
        return (
            p.copy(w.at[c, p.y, :, p.k, :, a], w.at[c, ya, :, p.k, :, a], self.xs.at[c, 2], self.xr.at[c, 2], dp=p.yn),
            p.copy(w.at[c, :, p.x, p.k, :, b], w.at[c, :, xa, p.k, :, b], self.xs.at[c, 3], self.xr.at[c, 3], dp=p.xn),
        )

    def across(self, c, arriving=False):
        p, w = self.p, self.dense
        k = 1 - p.k if arriving else p.k
        return p.copy(w.at[c, :, :, p.k], w.at[c, :, :, k], self.ks.at[c], self.kr.at[c], dp=p.sib)

    def s1(self, c):
        for dz in (1, 2, 3):
            self.along_z(c, dz).start()

    def s2(self, c):
        p = self.p
        for dz in (1, 2, 3):
            self.along_z(c, dz, True).wait_recv()
        self.dense[c, p.y, p.x, p.k] = rows_of(self.slab[c]).reshape(96, 768).astype(BF)
        for copy in self.first(c):
            copy.start()

    def s3(self, c):
        for copy in self.first(c, True):
            copy.wait_recv()
        for copy in self.second(c):
            copy.start()

    def s4(self, c):
        for copy in self.second(c, True):
            copy.wait_recv()
        self.across(c).start()

    def s5(self, c):
        self.across(c, True).wait_recv()

    def sent(self, c):
        for dz in (1, 2, 3):
            self.along_z(c, dz).wait_send()
        for copy in self.first(c) + self.second(c) + (self.across(c),):
            copy.wait_send()


class PlaneFirst:
    def __init__(self, gather, c, group, sems):
        self.g, self.p, self.c, self.group = gather, gather.p, c, group
        self.ps, self.pr, self.zs, self.zr = sems

    def plane(self, arriving=False):
        p, me, out = self.p, 2 * self.p.y + self.p.x, []
        for n, (dp, other) in enumerate(((p.xn, me + 1 - 2 * p.x), (p.yn, me + 2 - 4 * p.y), (p.diag, 3 - me))):
            out.append(p.copy(self.group.at[p.z, me], self.group.at[p.z, other if arriving else me], self.ps.at[n], self.pr.at[n],
                              dp=dp))
        return out

    def along_z(self, arriving=False):
        p = self.p
        return [p.copy(self.group.at[p.z], self.group.at[p.up(4 - dz) if arriving else p.z], self.zs.at[dz - 1],
                       self.zr.at[dz - 1], z=p.up(dz)) for dz in (1, 2, 3)]

    def s1(self, slab):
        self.group[self.p.z, 2 * self.p.y + self.p.x] = slab
        for copy in self.plane():
            copy.start()

    def s2(self):
        for copy in self.plane(True):
            copy.wait_recv()
        for copy in self.along_z():
            copy.start()

    def s3(self):
        for copy in self.along_z(True):
            copy.wait_recv()
        for n in range(4):
            self.g.dense[self.c, n // 2, n % 2, self.p.k] = rows_of(self.group[:, n]).reshape(96, 768).astype(BF)
        self.g.across(self.c).start()

    def sent(self):
        for copy in self.plane() + self.along_z() + [self.g.across(self.c)]:
            copy.wait_send()


class SmallGather:
    def __init__(self, p, slab, dense, send, recv):
        self.p, self.slab, self.dense, self.send, self.recv = p, slab, dense, send, recv

    def along_z(self, dz, arriving=False):
        p = self.p
        slot = p.up(4 - dz) if arriving else p.z
        return p.copy(self.slab.at[p.z], self.slab.at[slot], self.send.at[dz - 1], self.recv.at[dz - 1], z=p.up(dz))

    def plane(self, arriving=False):
        p, w = self.p, self.dense
        out = []
        for n, (dp, y, x) in enumerate(((p.xn, p.y, 1 - p.x), (p.yn, 1 - p.y, p.x), (p.diag, 1 - p.y, 1 - p.x))):
            dst = w.at[y, x, p.k] if arriving else w.at[p.y, p.x, p.k]
            out.append(p.copy(w.at[p.y, p.x, p.k], dst, self.send.at[3 + n], self.recv.at[3 + n], dp=dp))
        return out

    def across(self, arriving=False):
        p, w = self.p, self.dense
        k = 1 - p.k if arriving else p.k
        return p.copy(w.at[:, :, p.k], w.at[:, :, k], self.send.at[6], self.recv.at[6], dp=p.sib)

    def s1(self):
        for dz in (1, 2, 3):
            self.along_z(dz).start()

    def s2(self):
        p = self.p
        for dz in (1, 2, 3):
            self.along_z(dz, True).wait_recv()
        self.dense[p.y, p.x, p.k] = self.slab[...]
        for copy in self.plane():
            copy.start()

    def s3(self):
        for copy in self.plane(True):
            copy.wait_recv()
        self.across().start()

    def s4(self):
        self.across(True).wait_recv()

    def sent(self):
        for dz in (1, 2, 3):
            self.along_z(dz).wait_send()
        for copy in self.plane() + [self.across()]:
            copy.wait_send()


class Scatter:
    def __init__(self, p, r0, r1a, r1b, r2, v, r3, fin, sems):
        self.p, self.r0, self.r1a, self.r1b, self.r2, self.v, self.r3, self.fin = p, r0, r1a, r1b, r2, v, r3, fin
        self.ks, self.kr, self.xs, self.xr, self.zs, self.zr = sems

    def across(self, c, src):
        p = self.p
        return p.copy(src.at[:, :, 1 - p.k], self.r0.at[c], self.ks.at[c], self.kr.at[c], dp=p.sib)

    def first(self, c):
        p, r = self.p, self.r0
        return (
            p.copy(r.at[c, :, 1 - p.x, :, pl.ds(0, 384)], self.r1a.at[c], self.xs.at[c, 0], self.xr.at[c, 0], dp=p.xn),
            p.copy(r.at[c, 1 - p.y, :, :, pl.ds(384, 384)], self.r1b.at[c], self.xs.at[c, 1], self.xr.at[c, 1], dp=p.yn),
        )

    def second(self, c):
        p = self.p
        return (
            p.copy(self.r1a.at[c, 1 - p.y], self.r2.at[c, 0], self.xs.at[c, 2], self.xr.at[c, 2], dp=p.yn),
            p.copy(self.r1b.at[c, 1 - p.x], self.r2.at[c, 1], self.xs.at[c, 3], self.xr.at[c, 3], dp=p.xn),
        )

    def along_z(self, c, dz):
        p = self.p
        return p.copy(self.v.at[c, p.up(dz)], self.r3.at[c, dz - 1], self.zs.at[c, dz - 1], self.zr.at[c, dz - 1],
                      z=p.up(dz))

    def s1(self, c, src, own):
        self.across(c, src).wait_recv()
        for a in range(2):
            for b in range(2):
                self.r0[c, a, b] = (self.r0[c, a, b].astype(F32) + own(a, b).astype(F32)).astype(BF)
        for copy in self.first(c):
            copy.start()

    def s2(self, c):
        p = self.p
        for copy in self.first(c):
            copy.wait_recv()
        for a in range(2):
            self.r1a[c, a] = (self.r1a[c, a].astype(F32) + self.r0[c, a, p.x, :, :384].astype(F32)).astype(BF)
            self.r1b[c, a] = (self.r1b[c, a].astype(F32) + self.r0[c, p.y, a, :, 384:].astype(F32)).astype(BF)
        for copy in self.second(c):
            copy.start()

    def s3(self, c):
        p = self.p
        for copy in self.second(c):
            copy.wait_recv()
        left = self.r1a[c, p.y].astype(F32) + self.r2[c, 0].astype(F32)
        right = self.r1b[c, p.x].astype(F32) + self.r2[c, 1].astype(F32)
        self.v[c] = slab_of(jnp.concatenate([left, right], axis=1).reshape(4, 24, 768))
        for dz in (1, 2, 3):
            self.along_z(c, dz).start()

    def s4(self, c):
        for dz in (1, 2, 3):
            self.along_z(c, dz).wait_recv()
        total = rows_of(self.v[c, self.p.z])
        for dz in range(3):
            total = total + rows_of(self.r3[c, dz])
        self.fin[c] = total

    def sent(self, c, src):
        for copy in (self.across(c, src),) + self.first(c) + self.second(c):
            copy.wait_send()
        for dz in (1, 2, 3):
            self.along_z(c, dz).wait_send()


class SmallScatter:
    def __init__(self, p, src, r0, r1, r2, send, recv):
        self.p, self.src, self.r0, self.r1, self.r2, self.send, self.recv = p, src, r0, r1, r2, send, recv

    def across(self):
        p = self.p
        return p.copy(self.src.at[:, :, 1 - p.k], self.r0, self.send.at[0], self.recv.at[0], dp=p.sib)

    def plane(self):
        p = self.p
        return [p.copy(self.r0.at[y, x], self.r1.at[n], self.send.at[1 + n], self.recv.at[1 + n], dp=dp)
                for n, (dp, y, x) in enumerate(((p.xn, p.y, 1 - p.x), (p.yn, 1 - p.y, p.x), (p.diag, 1 - p.y, 1 - p.x)))]

    def along_z(self, dz):
        p = self.p
        return p.copy(self.r0.at[p.y, p.x, pl.ds(pl.multiple_of(24 * p.up(dz), 8), 24)], self.r2.at[dz - 1],
                      self.send.at[3 + dz], self.recv.at[3 + dz], z=p.up(dz))

    def s0(self):
        self.across().start()

    def s1(self):
        p = self.p
        self.across().wait_recv()
        for a in range(2):
            for b in range(2):
                self.r0[a, b] = self.r0[a, b] + self.src[a, b, p.k]
        for copy in self.plane():
            copy.start()

    def s2(self):
        p = self.p
        for copy in self.plane():
            copy.wait_recv()
        self.r0[p.y, p.x] = self.r0[p.y, p.x] + self.r1[0] + self.r1[1] + self.r1[2]
        for dz in (1, 2, 3):
            self.along_z(dz).start()

    def s3(self):
        p = self.p
        for dz in (1, 2, 3):
            self.along_z(dz).wait_recv()
        own = self.r0[p.y, p.x, pl.ds(pl.multiple_of(24 * p.z, 8), 24), :]
        return own + self.r2[0] + self.r2[1] + self.r2[2]

    def sent(self):
        for copy in [self.across()] + self.plane() + [self.along_z(dz) for dz in (1, 2, 3)]:
            copy.wait_send()


def piece_masks(width, total, count):
    lane = lax.broadcasted_iota(jnp.int32, (1, total), 1)
    inside = lax.rem(lane, width)
    place = lax.broadcasted_iota(jnp.int32, (128, total), 0) == inside
    owner = lax.broadcasted_iota(jnp.int32, (count, total), 0) * width == lane - inside
    return place, owner


def unpack_small(pieces, first, number, width, total):
    place, owner = piece_masks(width, total, 32)
    place = place.astype(BF)
    out = []
    for n in range(number):
        spread = mm(pieces[:, first + n, :].astype(BF), place)
        out.append(jnp.sum(jnp.where(owner, spread, 0.0), axis=0, keepdims=True))
    return out


def pack_small(pieces, first, vectors, width, total):
    place, owner = piece_masks(width, total, 32)
    place = place.astype(BF)
    for n, vector in enumerate(vectors):
        high = vector.astype(BF)
        low = (vector - high.astype(F32)).astype(BF)
        both = jnp.concatenate([jnp.where(owner, high.astype(F32), 0.0), jnp.where(owner, low.astype(F32), 0.0)], axis=0)
        both = mm_nt(both.astype(BF), place)
        pieces[:, first + n, :] = both[:32] + both[32:]


def weight(w, c):
    return w[c].reshape(768, 768)


def lane_block(start):
    return pl.ds(pl.multiple_of(start, 128), 128)


def project_group(g, tok, w, bqkv, conv, qkv, pkv, kvf):
    for r in range(2):
        rows = pl.ds(512 * r, 512)
        low = (mm(tok[rows, :], weight(w, g)) + bqkv[g]).astype(BF)
        qkv[g, rows, :] = low
        for part in range(4):
            kvf[part, pl.ds(8 + 512 * r, 512), :] = low[:, 256 + 128 * part:384 + 128 * part].astype(F32)
    for part in range(4):
        cols = pl.ds(128 * part, 128)
        total = jnp.zeros((256, 128), F32)
        for t in range(5):
            total = total + conv[g, pl.ds(t, 1), cols] * kvf[part, pl.ds(6 + t, 256, stride=4), :]
        pkv[g, :, cols] = total.astype(BF)


def attend_blocks(g, blocks, qkv, pkv, ctx, lse):
    parts = []
    for b in blocks:
        ns, ps, near, far = window(b)
        rows = pl.ds(pl.multiple_of(b * 128, 128), 128)
        for pr in range(2):
            parts.append(dict(
                near=near, far=far, rows=rows, lanes=lane_block(256 * g + 128 * pr), at=(g * 2 + pr) * 8 + b,
                qm=head_split(qkv[g, rows, 128 * pr:128 * pr + 128], 0.125),
                kn=qkv[g, pl.ds(ns, 256), 256 + 128 * pr:384 + 128 * pr],
                kp=pkv[g, pl.ds(ps, 160), 128 * pr:128 * pr + 128],
                vn=qkv[g, pl.ds(ns, 256), 512 + 128 * pr:640 + 128 * pr],
                vp=pkv[g, pl.ds(ps, 160), 256 + 128 * pr:384 + 128 * pr]))
    for t in parts:
        t["sn"] = jnp.where(t["near"], mm_nt(t["kn"], t["qm"]), -1e30)
        t["sp"] = jnp.where(t["far"], mm_nt(t["kp"], t["qm"]), -1e30)
    for t in parts:
        t["peak"] = jnp.maximum(jnp.max(t["sn"], axis=0, keepdims=True), jnp.max(t["sp"], axis=0, keepdims=True))
    for t in parts:
        t["en"] = jnp.exp(t["sn"] - t["peak"])
        t["ep"] = jnp.exp(t["sp"] - t["peak"])
    for t in parts:
        t["total"] = jnp.sum(t["en"], axis=0, keepdims=True) + jnp.sum(t["ep"], axis=0, keepdims=True)
    for t in parts:
        out = mm_tn(t["vn"], t["en"].astype(BF)) + mm_tn(t["vp"], t["ep"].astype(BF))
        t["out"] = head_join(out * pl.reciprocal(t["total"])).T.astype(BF)
    for t in parts:
        ctx[t["rows"], t["lanes"]] = t["out"]
        lse[t["at"]] = t["peak"] + jnp.log(t["total"])


def clear_edges(kvf):
    kvf[:, 0:8, :] = jnp.zeros((4, 8, 128), F32)
    kvf[:, 1032:1040, :] = jnp.zeros((4, 8, 128), F32)


def forward_kernel(comm, *refs):
    if comm:
        (tok, wqkv, bq_own, cv_own, wout, *six, wup, bu_own, wdn, pos, cot,
         out_o, pre_o, tokt_o, firstt_o, acc_o, dbr_o, gp_o, gwd_o, qkv_o, pkv_o, ctx_o, lse_o, gsm, w_o, conv, vec,
         w, buf, act, gp, acc, pre, first, dbr, tr, tokt, ctx, pkv, lse, out, kvf, stage, sems, osem,
         slab, slab_s, dense_s, pieces, bqkv, bup, plane,
         zs, zr, xs, xr, ks, kr, ss, sr, ps0, ps1, ps2, ps3) = refs
    else:
        (tok, w_in, bqkv, conv, vec, bup, pos, cot,
         out_o, pre_o, tokt_o, firstt_o, acc_o, dbr_o, gp_o, gwd_o, qkv_o, pkv_o, ctx_o, lse_o, gsm,
         w, buf, act, gp, acc, pre, first, dbr, tr, tokt, ctx, pkv, lse, out, kvf, stage, sems, osem) = refs
    qkv = buf
    clear_edges(kvf)
    kept, number = [], iter(range(20))

    def keep(src, dst):
        kept.append(pltpu.make_async_copy(src, dst, osem.at[next(number)]))
        kept[-1].start()

    def early():
        tokt[...] = tok[...].T
        gsm[...] = jnp.zeros_like(gsm)

        def part(r, carry):
            row = 128 * r + lax.broadcasted_iota(jnp.int32, (128, 160), 0)
            dy = mm((row == pos[...]).astype(BF), cot[...])
            dbr[pl.ds(pl.multiple_of(128 * r, 128), 128), :] = dy.astype(BF)
            gsm[4:5, :] += colsum(dy)
            return carry

        lax.fori_loop(0, 8, part, 0)

    todo = []
    if comm:
        p = Place()
        big = Gather(p, slab, w, (zs, zr, xs, xr, ks, kr))
        tiny = SmallGather(p, slab_s, dense_s, ss, sr)
        turned = PlaneFirst(big, 10, plane, (ps0, ps1, ps2, ps3))
        slab_s[p.z] = jnp.zeros((24, 128), F32)
        slab_s[p.z, 0:1, 0:72] = bq_own[...].astype(F32)
        slab_s[p.z, 1:6, 0:48] = cv_own[...].astype(F32)
        for i in range(6):
            slab_s[p.z, 6 + i:7 + i, 0:24] = six[i][...].astype(F32)
        slab_s[p.z, 12:13, 0:96] = bu_own[...].astype(F32)
        p.greet()
        tiny.s1()
        for c in (0, 10, 1, 2, 3, 4, 5, 6, 7, 8, 9, 11):
            if c < 3:
                rows24 = jnp.concatenate([wqkv[:, 768 * i + 256 * c:768 * i + 256 * c + 256] for i in range(3)], axis=1)
            elif c == 3:
                rows24 = wout[...]
            else:
                rows24 = (wup if c % 2 == 0 else wdn)[:, 768 * ((c - 4) // 2):768 * ((c - 4) // 2) + 768]
            if c == 10:
                turned.s1(slab_of(rows24.astype(F32)))
                continue
            slab[c, p.z] = slab_of(rows24.astype(F32))
            if c < 3:
                big.s1(c)
        early()
        tiny.s2()
        big.s1(3)
        big.s2(0)
        big.s1(4)
        big.s2(1)
        tiny.s3()
        big.s3(0)
        big.s1(5)
        big.s2(2)
        big.s3(1)
        big.s1(6)
        big.s2(3)
        big.s4(0)
        tiny.s4()
        pieces[...] = dense_s[...].reshape(32, 24, 128)
        whole = unpack_small(pieces, 0, 1, 72, 2304)[0]
        for g in range(3):
            for i in range(3):
                bqkv[g, :, 256 * i:256 * i + 256] = whole[:, 768 * i + 256 * g:768 * i + 256 * g + 256]
        taps = unpack_small(pieces, 1, 5, 48, 1536)
        for t in range(5):
            for g in range(3):
                for i in range(2):
                    conv[g, t:t + 1, 256 * i:256 * i + 256] = taps[t][:, 768 * i + 256 * g:768 * i + 256 * g + 256]
        rest = unpack_small(pieces, 6, 6, 24, 768)
        for i in range(6):
            vec[i:i + 1, :] = rest[i]
        whole = unpack_small(pieces, 12, 1, 96, 3072)[0]
        for j in range(4):
            bup[j] = whole[:, 768 * j:768 * j + 768]
        big.s5(0)
        todo = [[(big.s2, 8), (big.s3, 6)], [(big.s4, 5), (big.s2, 9)],
                [(big.s3, 7)], [(big.s4, 6), (big.s2, 11)], [(big.s3, 8)], [(big.s4, 7)],
                [(big.s3, 9)], [(big.s4, 8)], [(big.s3, 11)], [(big.s4, 9)],
                [], [(lambda c: turned.s3(), 10)], [(big.s4, 11)]]
    else:
        early()
        load = pltpu.make_async_copy(w_in, w, sems.at[0])
        load.start()
        load.wait()

    def progress():
        for step, c in todo.pop(0) if todo else ():
            step(c)

    def group(g, carry):
        if comm:
            @pl.when(g > 0)
            def _():
                big.s5(g)
        project_group(g, tok, w, bqkv, conv, qkv, pkv, kvf)

        def block(b, inner):
            if comm:
                i = 4 * g + b
                n = lax.div(i, 3)

                @pl.when(lax.rem(i, 3) == 0)
                def _():
                    big.s1(7 + n + lax.div(n, 3))
                    big.s2(4 + n)
                    big.s3(2 + n)

                @pl.when(lax.rem(i, 3) == 2)
                def _():
                    big.s4(1 + n)

                @pl.when(i == 10)
                def _():
                    turned.s2()
            attend_blocks(g, (2 * b, 2 * b + 1), qkv, pkv, ctx, lse)
            return inner

        return lax.fori_loop(0, 4, block, carry)

    lax.fori_loop(0, 3, group, 0)
    keep(tokt, tokt_o)
    keep(qkv.at[pl.ds(0, 3)], qkv_o)
    keep(pkv, pkv_o)
    keep(ctx, ctx_o)
    keep(lse, lse_o)
    if comm:
        big.s5(3)
        keep(w.at[pl.ds(0, 4)], w_o.at[pl.ds(0, 4)])
    b_out, gain1, shift1, b_down, gain2, shift2 = [vec[pl.ds(i, 1), :] for i in range(6)]
    tiles = [pl.ds(512 * r, 512) for r in range(2)]
    for rows in tiles:
        pre_one = tok[rows, :].astype(F32) + mm_nt(ctx[rows, :], weight(w, 3)) + b_out
        pre[rows, :] = pre_one
        xhat, rate = norm_stats(pre_one)
        low = (xhat * gain1 + shift1).astype(BF)
        first[rows, :] = low
        acc[rows, :] = low.astype(F32) + b_down
        progress()
    keep(pre, pre_o)
    tr[...] = first[...].T
    keep(tr, firstt_o)
    first_kept = len(kept) - 1
    for j in range(4):
        if comm:
            big.s5(4 + 2 * j)
        for rows in tiles:
            value, slope = gelu_both(mm(first[rows, :], weight(w, 4 + 2 * j)) + bup[j])
            act[j, rows, :] = value.astype(BF)
            gp[j, rows, :] = slope.astype(BF)
            progress()
        if comm:
            big.s5(5 + 2 * j)
            keep(w.at[pl.ds(4 + 2 * j, 2)], w_o.at[pl.ds(4 + 2 * j, 2)])
        for rows in tiles:
            acc[rows, :] += mm_nt(act[j, rows, :], weight(w, 5 + 2 * j))
            progress()
        keep(gp.at[j], gp_o.at[j])

    def last_norm(r, carry):
        rows = pl.ds(pl.multiple_of(256 * r, 256), 256)
        xhat, rate = norm_stats(acc[rows, :])
        out[rows, :] = (xhat * gain2 + shift2).astype(BF)
        dy = dbr[rows, :].astype(F32)
        gsm[3:4, :] += colsum(dy * xhat)
        dacc = norm_back(xhat, rate, gain2, dy)
        low = dacc.astype(BF)
        dbr[rows, :] = low
        acc[rows, :] = dacc
        gsm[2:3, :] += colsum(low.astype(F32))
        return carry

    lax.fori_loop(0, 4, last_norm, 0)
    keep(out, out_o)
    keep(dbr, dbr_o)
    keep(acc, acc_o)
    kept.pop(first_kept).wait()
    tr[...] = dbr[...].T
    sent = []
    for j in range(4):
        if j >= 2:
            sent[j - 2].wait()
        stage[j % 2] = mm(tr[...], act[j]).astype(BF).reshape(2, 2, 2, 96, 768)
        sent.append(pltpu.make_async_copy(stage.at[j % 2], gwd_o.at[j], sems.at[j % 2]))
        sent[j].start()
    sent[2].wait()
    sent[3].wait()
    for copy in kept:
        copy.wait()
    if comm:
        for c in range(12):
            (turned.sent() if c == 10 else big.sent(c))
        tiny.sent()


def forward_call(comm, *args):
    outs = [
        (struct((1024, 768), BF), ANY), (struct((1024, 768), F32), ANY), (struct((768, 1024), BF), ANY),
        (struct((768, 1024), BF), ANY),
        (struct((1024, 768), F32), ANY), (struct((1024, 768), BF), ANY), (struct((4, 1024, 768), BF), ANY),
        (struct((4, 2, 2, 2, 96, 768), BF), ANY), (struct((3, 1024, 768), BF), ANY), (struct((3, 256, 512), BF), ANY),
        (struct((1024, 768), BF), ANY), (struct((48, 1, 256), F32), ANY), (struct((8, 768), F32), VM),
    ]
    scratch = [
        pltpu.VMEM((12, 2, 2, 2, 96, 768), BF), pltpu.VMEM((3, 1024, 768), BF), pltpu.VMEM((4, 1024, 768), BF),
        pltpu.VMEM((4, 1024, 768), BF), pltpu.VMEM((1024, 768), F32), pltpu.VMEM((1024, 768), F32),
        pltpu.VMEM((1024, 768), BF), pltpu.VMEM((1024, 768), BF), pltpu.VMEM((768, 1024), BF), pltpu.VMEM((768, 1024), BF),
        pltpu.VMEM((1024, 768), BF),
        pltpu.VMEM((3, 256, 512), BF), pltpu.VMEM((48, 1, 256), F32), pltpu.VMEM((1024, 768), BF),
        pltpu.VMEM((4, 1040, 128), F32), pltpu.VMEM((2, 2, 2, 2, 96, 768), BF), DMA((2,)), DMA((20,)),
    ]
    if comm:
        outs += [(struct((12, 2, 2, 2, 96, 768), BF), ANY), (struct((3, 8, 512), F32), VM), (struct((8, 768), F32), VM)]
        scratch += [
            pltpu.VMEM((12, 4, 16, 1152), BF), pltpu.VMEM((4, 24, 128), F32), pltpu.VMEM((2, 2, 2, 4, 24, 128), F32),
            pltpu.VMEM((32, 24, 128), F32), pltpu.VMEM((3, 1, 768), F32), pltpu.VMEM((4, 1, 768), F32),
            pltpu.VMEM((4, 4, 16, 1152), BF),
            DMA((12, 3)), DMA((12, 3)), DMA((12, 4)), DMA((12, 4)), DMA((12,)), DMA((12,)), DMA((7,)), DMA((7,)),
            DMA((3,)), DMA((3,)), DMA((3,)), DMA((3,)),
        ]
        params = pltpu.CompilerParams(vmem_limit_bytes=LIMIT, collective_id=1, has_side_effects=True)
    else:
        params = pltpu.CompilerParams(vmem_limit_bytes=LIMIT)
    ins = [VM] * len(args)
    if not comm:
        ins[1] = ANY
    return pl.pallas_call(
        functools.partial(forward_kernel, comm), in_specs=ins, out_specs=[o[1] for o in outs],
        out_shape=[o[0] for o in outs], scratch_shapes=scratch, compiler_params=params, name="forward")(*args)


def qkv_rows(g, start, size):
    return pl.ds(pl.multiple_of(3072 + 1024 * g + start, 32), size)


def back_blocks(g, blocks, wb, pkv, buf, lse, dk, dv, dpk, dpv):
    parts = []
    for b in blocks:
        ns, ps, near, far = window(b)
        first_row = pl.multiple_of(b * 128, 128)
        rows, prow = pl.ds(first_row, 128), pl.ds(ps, 160)
        qrows, krows = qkv_rows(g, first_row, 128), qkv_rows(g, ns, 256)
        for pr in range(2):
            parts.append(dict(
                near=near, far=far, rows=rows, nr=pl.ds(ns, 256), prow=prow, ln=pl.ds(128 * pr, 128),
                qm=head_split(wb[qrows, 128 * pr:128 * pr + 128], 0.125),
                dm=head_split(buf[3, rows, lane_block(256 * g + 128 * pr)], 1.0),
                kn=wb[krows, 256 + 128 * pr:384 + 128 * pr],
                kp=pkv[g, prow, 128 * pr:128 * pr + 128],
                vn=wb[krows, 512 + 128 * pr:640 + 128 * pr],
                vp=pkv[g, prow, 256 + 128 * pr:384 + 128 * pr],
                ls=lse[(g * 2 + pr) * 8 + b]))
    for t in parts:
        t["pn"] = jnp.exp(jnp.where(t["near"], mm_nt(t["kn"], t["qm"]), -1e30) - t["ls"])
        t["pp"] = jnp.exp(jnp.where(t["far"], mm_nt(t["kp"], t["qm"]), -1e30) - t["ls"])
    for t in parts:
        t["dn"] = mm_nt(t["vn"], t["dm"])
        t["dp"] = mm_nt(t["vp"], t["dm"])
        t["gvn"] = mm(t["pn"].astype(BF), t["dm"])
        t["gvp"] = mm(t["pp"].astype(BF), t["dm"])
    for t in parts:
        rd = jnp.sum(t["pn"] * t["dn"], axis=0, keepdims=True) + jnp.sum(t["pp"] * t["dp"], axis=0, keepdims=True)
        t["sn"] = (t["pn"] * (t["dn"] - rd)).astype(BF)
        t["sp"] = (t["pp"] * (t["dp"] - rd)).astype(BF)
    for t in parts:
        t["gkn"] = mm(t["sn"], t["qm"])
        t["gkp"] = mm(t["sp"], t["qm"])
        t["gq"] = (head_join(mm_tn(t["kn"], t["sn"]) + mm_tn(t["kp"], t["sp"])).T * 0.125).astype(BF)
    for t in parts:
        dk[t["nr"], t["ln"]] += t["gkn"]
        dpk[t["prow"], t["ln"]] += t["gkp"]
        dv[t["nr"], t["ln"]] += t["gvn"]
        dpv[t["prow"], t["ln"]] += t["gvp"]
        buf[g, t["rows"], t["ln"]] = t["gq"]


def pool_back(g, conv, wb, kvf, dk, dv, dpk, dpv, buf, gconv):
    for part in range(4):
        kvf[part, 8:1032, :] = wb[qkv_rows(g, 0, 1024), 256 + 128 * part:384 + 128 * part].astype(F32)
    for part in range(4):
        cols = pl.ds(128 * part, 128)
        src, dst = (dpk, dk) if part < 2 else (dpv, dv)
        half = pl.ds(128 * (part % 2), 128)
        dpool = src[:, half]
        for t in range(5):
            gconv[g, pl.ds(t, 1), cols] = colsum(dpool * kvf[part, pl.ds(6 + t, 256, stride=4), :])
        kvf[part, 8:1032, :] = dst[:, half]
        for t in range(5):
            at = pl.ds(6 + t, 256, stride=4)
            kvf[part, at, :] += conv[g, pl.ds(t, 1), cols] * dpool
        buf[g, :, 256 + 128 * part:384 + 128 * part] = kvf[part, 8:1032, :].astype(BF)
        kvf[part, 0:8, :] = jnp.zeros((8, 128), F32)
        kvf[part, 1032:1040, :] = jnp.zeros((8, 128), F32)


BLOCKS = (2, 2, 2, 96, 768)


STEPS = (
    (), ((1, 0),), (), ((1, 1),), (), ((1, 2), (2, 0)), (), ((1, 3), (2, 1)), (), ((1, 4), (2, 2), (3, 0)), (),
    ((1, 5), (2, 3), (3, 1)), (), ((1, 6), (2, 4), (3, 2), (4, 0)), ((4, 1),),
)
LOOP_STEPS = {
    0: ((2, 5), (3, 3)), 1: ((1, 7), (2, 6)), 2: ((3, 4), (4, 2)), 3: ((1, 8), (3, 5), (4, 3)), 4: ((2, 7),), 5: ((3, 6), (4, 4)),
    6: ((1, 9), (2, 8)), 7: ((4, 5),), 8: ((3, 7),), 9: ((1, 10), (2, 9), (4, 6)), 10: ((3, 8), (4, 7)), 11: ((2, 10), (3, 9), (4, 8)),
}


def backward_kernel(comm, *refs):
    (tokt_i, w_i, conv, vec, pre_i, firstt_i, acc_i, dbr_i, gp_i, qkv_i, pkv_i, ctx_i, lse_i, gsm_in) = refs[:14]
    if comm:
        (gwd_i, gtok_o, fin, tot,
         wb, buf, xb, db, tr, acc, gtok, pkv, lse, kvf, isem, osem,
         gat, gconv, gbias, gbout, gsm, gbup, r0, r1a, r1b, r2, v, r3, own, pieces, small, t0, t1, t2,
         ks, kr, xs, xr, zs, zr, ls, ss, sr) = refs[14:]
    else:
        (gtok_o, gat, gconv, gbias, gbout, gsm, gbup,
         wb, buf, xb, db, tr, acc, gtok, pkv, lse, kvf, isem, osem) = refs[14:]
    dk, dv = acc.at[:, pl.ds(0, 256)], acc.at[:, pl.ds(256, 256)]
    dpk, dpv = acc.at[pl.ds(0, 256), pl.ds(512, 256)], acc.at[pl.ds(256, 256), pl.ds(512, 256)]
    loads = {}

    def load(name, src, dst):
        loads[name] = pltpu.make_async_copy(src, dst, isem.at[len(loads)])
        loads[name].start()

    def slot(n):
        return wb[pl.ds(768 * n, 768), :]

    def load_weight(c, n):
        for i in range(8):
            load(("w", c, i), w_i.at[c, i // 4, i // 2 % 2, i % 2], wb.at[pl.ds(768 * n + 96 * i, 96), :])

    def have_weight(c):
        for i in range(8):
            loads["w", c, i].wait()

    load("dbr", dbr_i, db)
    load_weight(5, 1)
    load(("gp", 0), gp_i.at[0], buf.at[0])
    if comm:
        p = Place()
        big = Scatter(p, r0, r1a, r1b, r2, v, r3, fin, (ks, kr, xs, xr, zs, zr))
        tiny = SmallScatter(p, small, t0, t1, t2, ss, sr)
        p.greet()

        def fetch(c):
            return pltpu.make_async_copy(gwd_i.at[c, :, :, p.k], own.at[c % 2], ls.at[c % 2])

        big.across(0, gwd_i.at[0]).start()
        fetch(0).start()
        big.across(1, gwd_i.at[1]).start()

        def take(steps):
            for stage, c in steps:
                if stage > 1:
                    (big.s2, big.s3, big.s4)[stage - 2](c)
                elif c >= 4:
                    at = c - 4 if c < 9 else c - 9
                    big.s1(c, gat.at[0], lambda a, b: gat[at, a, b, p.k])
                else:
                    fetch(c).wait()
                    big.s1(c, gat.at[0], lambda a, b: own[c % 2, a, b])
                    if c < 2:
                        fetch(c + 2).start()

    def run(n):
        if comm:
            take(STEPS[n])

    load_weight(4, 0)
    load("acc", acc_i, acc)

    def load_next(j):
        if j == 0:
            load("first", firstt_i, tr)
            if comm:
                fetch(1).start()
                big.across(2, gwd_i.at[2]).start()
                big.across(3, gwd_i.at[3]).start()
        if j < 3:
            load_weight(7 + 2 * j, 3 + 2 * j)
            load(("gp", j + 1), gp_i.at[j + 1], buf.at[j + 1])
            load_weight(6 + 2 * j, 2 + 2 * j)
        if j == 2:
            load("tok", tokt_i, xb)
        if j == 3:
            load("pre", pre_i, gtok)
            load("pkv", pkv_i, pkv)
            load("lse", lse_i, lse)

    clear_edges(kvf)
    gbup[...] = jnp.zeros_like(gbup)
    gsm[...] = gsm_in[...]
    tiles = [pl.ds(512 * r, 512) for r in range(2)]
    loads["dbr"].wait()
    for j in range(4):
        have_weight(5 + 2 * j)
        loads["gp", j].wait()
        load_next(j)
        for r, rows in enumerate(tiles):
            low = (mm(db[rows, :], slot(1 + 2 * j)) * buf[j, rows, :].astype(F32)).astype(BF)
            buf[j, rows, :] = low
            gbup[j] += colsum(low.astype(F32))
            if r == 0:
                have_weight(4 + 2 * j)
                if j == 0:
                    loads["acc"].wait()
            acc[rows, :] += mm_nt(low, slot(2 * j))
            run(3 * j + r)
        if j == 0:
            loads["first"].wait()
        gat[j] = mm(tr[...], buf[j]).astype(BF).reshape(BLOCKS)
        if comm:
            big.across(4 + j, gat.at[j]).start()
            run(3 * j + 2)
        if j == 1:
            for c in range(4):
                load_weight(c, c)
    for g in range(3):
        load(("qkv", g), qkv_i.at[g], wb.at[pl.ds(3072 + 1024 * g, 1024), :])
    load("ctx", ctx_i, db)
    loads["pre"].wait()
    gain1 = vec[1:2, :]
    sums = [jnp.zeros((1, 768), F32) for _ in range(3)]
    have_weight(3)
    for rows in tiles:
        xhat, rate = norm_stats(gtok[rows, :])
        dacc = acc[rows, :]
        sums[0] = sums[0] + colsum(dacc * xhat)
        sums[1] = sums[1] + colsum(dacc)
        dpre = norm_back(xhat, rate, gain1, dacc)
        gtok[rows, :] = dpre
        da = dpre.astype(BF)
        sums[2] = sums[2] + colsum(da.astype(F32))
        buf[3, rows, :] = mm(da, slot(3)).astype(BF)
        tr[:, rows] = da.T
    gsm[0:1, :] = sums[0]
    gsm[1:2, :] = sums[1]
    gbout[...] = sums[2]
    if comm:
        run(12)
        pieces[...] = jnp.zeros_like(pieces)
        pack_small(pieces, 6, [gbout[...]] + [gsm[i:i + 1, :] for i in range(5)], 24, 768)
        pack_small(pieces, 12, [jnp.concatenate([gbup[j] for j in range(4)], axis=1)], 96, 3072)
    loads["ctx"].wait()
    gat[4] = mm(tr[...], db[...]).astype(BF).reshape(BLOCKS)
    if comm:
        big.across(8, gat.at[4]).start()
        run(13)
    loads["tok"].wait()
    loads["pkv"].wait()
    loads["lse"].wait()
    for g in range(3):
        loads["qkv", g].wait()
        have_weight(g)
    run(14)

    def group(g, carry):
        acc[...] = jnp.zeros_like(acc)

        def block(b, inner):
            if comm:
                for i, steps in LOOP_STEPS.items():
                    pl.when(4 * g + b == i)(functools.partial(take, steps))
            back_blocks(g, (2 * b, 2 * b + 1), wb, pkv, buf, lse, dk, dv, dpk, dpv)
            return inner

        lax.fori_loop(0, 4, block, 0)
        pool_back(g, conv, wb, kvf, dk, dv, dpk, dpv, buf, gconv)
        if comm:
            big.across(4 + g, gat.at[0]).wait_send()
        gat[g if comm else 5 + g] = mm(xb[...], buf[g]).astype(BF).reshape(BLOCKS)
        if comm:
            big.across(9 + g, gat.at[g]).start()
        gbias[g] = colsum(buf[g].astype(F32))
        return carry

    lax.fori_loop(0, 3, group, 0)
    parts = []

    def token_part(n):
        rows = pl.ds(256 * n, 256)
        total = gtok[rows, :]
        for g in range(3):
            total = total + mm_nt(buf[g, rows, :], slot(g))
        gtok[rows, :] = total
        parts.append(pltpu.make_async_copy(gtok.at[rows, :], gtok_o.at[rows, :], osem.at[n]))
        parts[n].start()

    if not comm:
        for n in range(4):
            token_part(n)
        for copy in parts:
            copy.wait()
        return

    token_part(0)
    take(((1, 11),))
    kinds = [jnp.concatenate([gbias[g][:, 256 * i:256 * i + 256] for i in range(3) for g in range(3)], axis=1)]
    pack_small(pieces, 0, kinds, 72, 2304)
    pack_small(pieces, 1, [
        jnp.concatenate([gconv[g, t:t + 1, 256 * i:256 * i + 256] for i in range(2) for g in range(3)], axis=1)
        for t in range(5)], 48, 1536)
    small[...] = pieces[...].reshape(2, 2, 2, 96, 128)
    tiny.s0()
    take(((3, 10),))
    token_part(1)
    tiny.s1()
    take(((2, 11), (4, 9)))
    token_part(2)
    tiny.s2()
    take(((3, 11), (4, 10)))
    token_part(3)
    tot[...] = tiny.s3()
    take(((4, 11),))
    for c in range(12):
        for copy in big.first(c) + big.second(c) + tuple(big.along_z(c, dz) for dz in (1, 2, 3)):
            copy.wait_send()
        if c not in (4, 5, 6):
            big.across(c, gat.at[0]).wait_send()
    tiny.sent()
    for copy in parts:
        copy.wait()


def backward_call(comm, *args):
    scratch = [
        pltpu.VMEM((6144, 768), BF), pltpu.VMEM((4, 1024, 768), BF), pltpu.VMEM((768, 1024), BF), pltpu.VMEM((1024, 768), BF),
        pltpu.VMEM((768, 1024), BF), pltpu.VMEM((1024, 768), F32), pltpu.VMEM((1024, 768), F32),
        pltpu.VMEM((3, 256, 512), BF), pltpu.VMEM((48, 1, 256), F32),
        pltpu.VMEM((4, 1040, 128), F32), DMA((120,)), DMA((4,)),
    ]
    ins = [ANY] * len(args)
    for i in (2, 3, 13):
        ins[i] = VM
    local = [((5 if comm else 8,) + BLOCKS, BF), ((3, 8, 512), F32), ((3, 1, 768), F32), ((1, 768), F32), ((8, 768), F32), ((4, 1, 768), F32)]
    outs = [(struct((1024, 768), F32), ANY)]
    if comm:
        outs += [(struct((12, 24, 768), F32), VM), (struct((24, 128), F32), VM)]
        scratch += [pltpu.VMEM(*s) for s in local]
        scratch += [
            pltpu.VMEM((12, 2, 2, 96, 768), BF), pltpu.VMEM((12, 2, 96, 384), BF), pltpu.VMEM((12, 2, 96, 384), BF),
            pltpu.VMEM((12, 2, 96, 384), BF), pltpu.VMEM((12, 4, 16, 1152), BF), pltpu.VMEM((12, 3, 16, 1152), BF),
            pltpu.VMEM((2, 2, 2, 96, 768), BF), pltpu.VMEM((32, 24, 128), F32),
            pltpu.VMEM((2, 2, 2, 96, 128), F32), pltpu.VMEM((2, 2, 96, 128), F32), pltpu.VMEM((3, 96, 128), F32),
            pltpu.VMEM((3, 24, 128), F32),
            DMA((12,)), DMA((12,)), DMA((12, 4)), DMA((12, 4)), DMA((12, 3)), DMA((12, 3)), DMA((2,)), DMA((7,)), DMA((7,)),
        ]
        params = pltpu.CompilerParams(vmem_limit_bytes=LIMIT, collective_id=2, has_side_effects=True)
    else:
        outs += [(struct(*s), VM) for s in local]
        params = pltpu.CompilerParams(vmem_limit_bytes=LIMIT)
    return pl.pallas_call(
        functools.partial(backward_kernel, comm), in_specs=ins, out_specs=[o[1] for o in outs], out_shape=[o[0] for o in outs],
        scratch_shapes=scratch, compiler_params=params, name="backward")(*args)


def finish_kernel(out_i, gtok_i, fin, tot, out, gtok, gqkv, gqb, gcv, gwo, gbo, gg1, gs1, gwu, gbu, gwd, gbd, gg2, gs2):
    out[...] = out_i[...]
    gtok[...] = gtok_i[...]

    @pl.when(pl.program_id(0) == 0)
    def _():
        for j in range(4):
            gwd[:, 768 * j:768 * j + 768] = fin[j]
            gwu[:, 768 * j:768 * j + 768] = fin[4 + j]
        gwo[...] = fin[8]
        for g in range(3):
            for i in range(3):
                gqkv[:, 768 * i + 256 * g:768 * i + 256 * g + 256] = fin[9 + g, :, 256 * i:256 * i + 256]
        gqb[...] = tot[0:1, 0:72]
        gcv[...] = tot[1:6, 0:48]
        for i, ref in enumerate((gbo, gg1, gs1, gbd, gg2, gs2)):
            ref[...] = tot[6 + i:7 + i, 0:24]
        gbu[...] = tot[12:13, 0:96]


def finish_call(*args):
    shapes = ((24, 2304), (1, 72), (5, 48), (24, 768), (1, 24), (1, 24), (1, 24), (24, 3072), (1, 96),
              (24, 3072), (1, 24), (1, 24), (1, 24))
    part = pl.BlockSpec((512, 768), lambda n: (n, 0))

    def full(shape):
        return pl.BlockSpec(shape, lambda n: (0,) * len(shape))

    return pl.pallas_call(
        finish_kernel, grid=(2,), in_specs=[part, part, full((12, 24, 768)), full((24, 128))],
        out_specs=[part, part] + [full(s) for s in shapes],
        out_shape=[struct((1024, 768), BF), struct((1024, 768), F32)] + [struct(s, F32) for s in shapes],
        name="finish")(*args)


def shards_direct(tokens, w_qkv, b_qkv, conv_kv, w_out, b_out, gain_one, shift_one, w_up, b_up, w_down, b_down, gain_two,
                  shift_two, positions, cotangent):
    tok = tokens[0]
    out, pre, tokt, firstt, acc, dbr, gp, gwd, qkv, pkv, ctx, lse, gsm, w, conv, vec = forward_call(
        True, tok, w_qkv, b_qkv[None], conv_kv, w_out.T, b_out[None], gain_one[None], shift_one[None], b_down[None],
        gain_two[None], shift_two[None], w_up, b_up[None], w_down.T, positions, cotangent[0])
    gtok, fin, tot = backward_call(True, tokt, w, conv, vec, pre, firstt, acc, dbr, gp, qkv, pkv, ctx, lse, gsm, gwd)
    (out, gtok, gqkv, gqb, gcv, gwo, gbo, gg1, gs1, gwu, gbu, gwd, gbd, gg2, gs2) = finish_call(out, gtok, fin, tot)
    return (out[None], gtok[None], gqkv, gqb[0], gcv, gwo.T, gbo[0], gg1[0], gs1[0], gwu, gbu[0], gwd.T, gbd[0], gg2[0], gs2[0])


def small_sizes(count):
    return [2304 // count] + [1536 // count] * 5 + [768 // count] * 6 + [3072 // count]


def by_group(v, kinds):
    return v.reshape(kinds, 3, 256).transpose(1, 0, 2).reshape(3, 1, kinds * 256)


def shards_general(tokens, w_qkv, b_qkv, conv_kv, w_out, b_out, gain_one, shift_one, w_up, b_up, w_down, b_down, gain_two,
                   shift_two, positions, cotangent):
    rows = w_qkv.shape[0]
    count = 768 // rows
    blocks = (2, 2, 2, 96, 768)
    up = w_up.reshape(rows, 4, 768).transpose(1, 0, 2)
    down = w_down.reshape(4, 768, rows).transpose(0, 2, 1)
    own = jnp.concatenate([
        w_qkv.reshape(rows, 3, 3, 256).transpose(2, 0, 1, 3).reshape(3, rows, 768),
        w_out.T[None],
        jnp.stack([up, down], 1).reshape(8, rows, 768),
    ], 0)
    w = lax.all_gather(own, AXES, axis=1, tiled=True).reshape((12,) + blocks)
    small = jnp.concatenate([b_qkv, conv_kv.reshape(-1), b_out, gain_one, shift_one, b_down, gain_two, shift_two, b_up])
    small = lax.all_gather(small[None], AXES, axis=0, tiled=True).astype(F32)
    at, parts = 0, []
    for size in small_sizes(count):
        parts.append(small[:, at:at + size].reshape(-1))
        at += size
    bqkv = by_group(parts[0], 3)
    conv = jnp.concatenate([by_group(p, 2) for p in parts[1:6]] + [jnp.zeros((3, 3, 512), F32)], 1)
    vec = jnp.stack(parts[6:12] + [jnp.zeros((768,), F32)] * 2)
    bup = parts[12].reshape(4, 1, 768)
    out, pre, tokt, firstt, acc, dbr, gp, gwd, qkv, pkv, ctx, lse, gsm = forward_call(
        False, tokens[0], w, bqkv, conv, vec, bup, positions, cotangent[0])
    gwd = lax.psum_scatter(gwd.reshape(4, 768, 768), AXES, scatter_dimension=1, tiled=True).astype(F32)
    gtok, gat, gconv, gbias, gbout, gsm, gbup = backward_call(
        False, tokt, w, conv, vec, pre, firstt, acc, dbr, gp, qkv, pkv, ctx, lse, gsm)
    gat = lax.psum_scatter(gat.reshape(8, 768, 768), AXES, scatter_dimension=1, tiled=True).astype(F32)
    flat = [gbias.reshape(3, 3, 256).transpose(1, 0, 2).reshape(count, -1)]
    flat += [gconv[:, t].reshape(3, 2, 256).transpose(1, 0, 2).reshape(count, -1) for t in range(5)]
    flat += [gbout[0].reshape(count, -1)] + [gsm[i].reshape(count, -1) for i in range(5)] + [gbup.reshape(count, -1)]
    flat = lax.psum_scatter(jnp.concatenate(flat, 1), AXES, scatter_dimension=0, tiled=True)
    at, s = 0, []
    for size in small_sizes(count):
        s.append(flat[0, at:at + size])
        at += size
    return (
        out[None], gtok[None],
        gat[5:].reshape(3, rows, 3, 256).transpose(1, 2, 0, 3).reshape(rows, 2304),
        s[0], jnp.stack(s[1:6]), gat[4].T, s[6], s[7], s[8],
        gat[:4].transpose(1, 0, 2).reshape(rows, 3072), s[12],
        gwd.transpose(0, 2, 1).reshape(3072, rows), s[9], s[10], s[11],
    )


def solution(mesh):
    rows, cols, flat, item = P(AXES, None), P(None, AXES), P(AXES), P(AXES, None, None)
    direct = mesh.shape["dp"] == 8 and mesh.shape["fsdp"] == 4
    return jax.shard_map(
        shards_direct if direct else shards_general,
        mesh=mesh,
        in_specs=(item, rows, flat, cols, cols, flat, flat, flat, rows, flat, cols, flat, flat, flat, rows, item),
        out_specs=(item, item, rows, flat, cols, cols, flat, flat, flat, rows, flat, cols, flat, flat, flat),
        check_vma=False,
    )
```
